32 devices in a mesh: dp: 8 (over z, core), tensor: 4 (over y, x).
Axes of the slice: x: 2, y: 2, z: 4, core: 2. Of those that a mesh axis runs over, the one named last changes fastest.
Arguments:
- tokens: bfloat16 [8192, 2048], P('dp', 'tensor'), may hold values from -6 to 6
- cotangent: bfloat16 [8192, 2048], P('dp', 'tensor'), may hold values from -6 to 6
- attn_gain: float32 [2048], replicated, may hold values from 0.25 to 1.75
- w_query: bfloat16 [2048, 2048], P(None, 'tensor'), may hold values from -0.125 to 0.125
- w_key: bfloat16 [2048, 2048], P(None, 'tensor'), may hold values from -0.125 to 0.125
- w_value: bfloat16 [2048, 2048], P(None, 'tensor'), may hold values from -0.125 to 0.125
- query_gain: float32 [16, 128], P('tensor'), may hold values from 0.25 to 1.75
- key_gain: float32 [16, 128], P('tensor'), may hold values from 0.25 to 1.75
- w_output: bfloat16 [2048, 2048], P('tensor'), may hold values from -1 to 1
- ffn_gain: float32 [2048], replicated, may hold values from 0.25 to 1.75
- w_router: bfloat16 [2048, 16], replicated, may hold values from -0.0625 to 0.0625
- w_gate: bfloat16 [16, 2048, 1024], P(None, None, 'tensor'), may hold values from -0.125 to 0.125
- w_up: bfloat16 [16, 2048, 1024], P(None, None, 'tensor'), may hold values from -0.125 to 0.125
- w_down: bfloat16 [16, 1024, 2048], P(None, 'tensor'), may hold values from -2 to 2
- expert_ids: int32 [8192, 8], P('dp'), may hold values from 0 to 15, all different within a row
Outputs:
- output: bfloat16 [8192, 2048], P('dp', 'tensor')
- input_grad: bfloat16 [8192, 2048], P('dp', 'tensor')
- grad_attn_gain: float32 [2048], P('dp')
- grad_query: float32 [2048, 2048], P('dp', 'tensor')
- grad_key: float32 [2048, 2048], P('dp', 'tensor')
- grad_value: float32 [2048, 2048], P('dp', 'tensor')
- grad_query_gain: float32 [16, 128], P('tensor', 'dp')
- grad_key_gain: float32 [16, 128], P('tensor', 'dp')
- grad_output: float32 [2048, 2048], P('tensor', 'dp')
- grad_ffn_gain: float32 [2048], P('dp')
- grad_router: float32 [2048, 16], P('dp')
- grad_gate: float32 [16, 2048, 1024], P(None, 'dp', 'tensor')
- grad_up: float32 [16, 2048, 1024], P(None, 'dp', 'tensor')
- grad_down: float32 [16, 1024, 2048], P(None, 'tensor', 'dp')
The draws below stay inside these ranges and needn't reach their ends.
Inputs may be any that keep to these rules, and one draw needn't show every extreme that they name: `expert_ids`: each row names 8 different experts; every expert is named by some row.
All inputs are finite; a program needn't handle non-finite values.
Results may differ from the reference program's by a relative error of at most 0.022.
Values may be sent and summed in bfloat16 or wider, within the bound.
No kernel may reach another device: no remote copies, remote signals or barrier semaphores. Data moves between devices by JAX's collectives and lax.ppermute only.
A program may use at most 640 MiB of HBM per device.

```python
import math
import jax
import jax.numpy as jnp
from jax import lax

D = 2048
HEADS = 16
HD = 128
FF = 1024
TOPK = 8
EXPERTS = 16
LEN = 1024
TOK_DP = 1024
TOKENS = 8192
CAP = 512
N_DP = 8


def steps_of(rng, shape, pieces, low, largest):
    factor_of, own = 1.0, jax.random.fold_in(rng, 6)
    for dim, parts in pieces:
        steps = jnp.exp(jax.random.uniform(jax.random.fold_in(own, dim), (parts,), jnp.float32, low / len(pieces), largest / len(pieces)))
        factor_of = factor_of * jnp.repeat(steps, shape[dim] // parts).reshape([-1 if axis == dim else 1 for axis in range(len(shape))])
    return factor_of


def choose_distinct(rng, rows, amount, top, lift):
    ranking = jax.random.permutation(jax.random.fold_in(rng, 1), amount)
    boost = ranking
    for power in range(3):
        boost = boost * boost // amount
    boost = boost * lift // amount
    tickets = jax.random.randint(jax.random.fold_in(rng, 2), (rows, amount), 0, 4096) + boost
    fixed_rows = jax.random.permutation(jax.random.fold_in(rng, 3), rows)[jnp.arange(amount) % rows]
    tickets = jnp.where(jnp.arange(rows)[:, None] == fixed_rows[None, :], 1 << 14, tickets)
    merit = tickets * amount + jnp.arange(amount)
    return lax.top_k(merit.astype(jnp.int32), top)[1].astype(jnp.int32)


def normal_values(own_key, extent, spread, limit, pieces=(), kind=jnp.bfloat16):
    values = jax.random.normal(own_key, extent, jnp.float32) * spread
    if len(pieces) > 0:
        values = steps_of(own_key, extent, pieces, -0.22, 0.18) * values
    return jnp.clip(values, min=-limit, max=limit).astype(kind)


def setup_inputs(seed: int = 0) -> dict:
    splits = jax.random.split(jax.random.key(seed), 16)
    tokens = normal_values(splits[0], (TOKENS, D), 1.0, 6.0, ((0, 8), (1, 4)))
    cotangent = normal_values(splits[1], (TOKENS, D), 1.0, 6.0, ((0, 8), (1, 4)))
    attn_gain = jnp.clip(1.0 + 0.15 * jax.random.normal(splits[2], (D,), jnp.float32), 0.25, 1.75)
    w_query = normal_values(splits[3], (D, D), D ** -0.5, 0.125, ((1, 4),))
    w_key = normal_values(splits[4], (D, D), D ** -0.5, 0.125, ((1, 4),))
    w_value = normal_values(splits[5], (D, D), D ** -0.5, 0.125, ((1, 4),))
    query_gain = jnp.clip(1.0 + 0.15 * jax.random.normal(splits[6], (HEADS, HD), jnp.float32), 0.25, 1.75)
    key_gain = jnp.clip(1.0 + 0.15 * jax.random.normal(splits[7], (HEADS, HD), jnp.float32), 0.25, 1.75)
    w_output = normal_values(splits[8], (D, D), (D * 16 // LEN) ** -0.5, 1.0, ((0, 4),))
    ffn_gain = jnp.clip(1.0 + 0.15 * jax.random.normal(splits[9], (D,), jnp.float32), 0.25, 1.75)
    w_router = normal_values(splits[10], (D, EXPERTS), (4 * D) ** -0.5, 0.0625)
    w_gate = normal_values(splits[11], (EXPERTS, D, FF), D ** -0.5, 0.125, ((2, 4),))
    w_up = normal_values(splits[12], (EXPERTS, D, FF), D ** -0.5, 0.125, ((2, 4),))
    w_down = normal_values(splits[13], (EXPERTS, FF, D), (max(1, FF * TOPK // (3 * EXPERTS * EXPERTS))) ** -0.5, 2.0, ((1, 4),))
    expert_ids = choose_distinct(splits[14], TOKENS, EXPERTS, TOPK, 4096)
    return dict(tokens=tokens, cotangent=cotangent, attn_gain=attn_gain, w_query=w_query, w_key=w_key, w_value=w_value, query_gain=query_gain, key_gain=key_gain, w_output=w_output, ffn_gain=ffn_gain, w_router=w_router, w_gate=w_gate, w_up=w_up, w_down=w_down, expert_ids=expert_ids)


@jax.custom_vjp
def low(v):
    return lax.optimization_barrier(v.astype(jnp.bfloat16)).astype(jnp.float32)

@jax.custom_vjp
def low_back(v):
    return v

def low_keep(v):
    return (low(v), None)

def low_pass(kept, grad):
    return (grad,)

def back_keep(v):
    return (v, None)

def back_low(kept, grad):
    return (low(grad),)
low.defvjp(low_keep, low_pass)
low_back.defvjp(back_keep, back_low)
norm_eps = 1e-05
rope_base = 10000.0
big_negative = -1e+30

def hp_dot(left, right):
    return jnp.dot(left, right, precision=lax.Precision.HIGHEST)

def rms_scale(values):
    return values * lax.rsqrt(lax.optimization_barrier(jnp.mean(values * values, axis=-1, keepdims=True)) + norm_eps)

def rope_tables(length, width):
    half_width = width // 2
    inv_freq = rope_base ** (-(jnp.arange(half_width, dtype=jnp.float32) * 2.0) / width)
    angles = jnp.arange(length, dtype=jnp.float32)[:, None] * inv_freq[None, :]
    return (jnp.cos(angles), jnp.sin(angles))

def rotate(values, cosine, sine):
    half_width = values.shape[-1] // 2
    first_half = values[..., :half_width]
    second = values[..., half_width:]
    return jnp.concatenate([first_half * cosine - second * sine, second * cosine + first_half * sine], axis=-1)

def slot_table(expert_ids, experts, capacity):
    flat_ids = expert_ids.reshape(-1)
    onehot = (flat_ids[:, None] == jnp.arange(experts, dtype=jnp.int32)[None, :]).astype(jnp.int32)
    before = lax.optimization_barrier(jnp.sum((jnp.cumsum(onehot, axis=0) - onehot) * onehot, axis=1))
    pair_kept = before < capacity
    pair_slot = jnp.where(pair_kept, flat_ids * capacity + before, experts * capacity)
    pair_owner = jnp.arange(flat_ids.shape[0], dtype=jnp.int32) // expert_ids.shape[1]
    source = jnp.zeros((experts * capacity + 1,), jnp.int32).at[pair_slot].set(pair_owner)[:-1]
    return (pair_slot, pair_kept, source)

def shard_forward(weights, residual_in, routes):
    attn_gain, w_query, w_key, w_value, query_gain, key_gain, w_output, ffn_gain, w_router, w_gate, w_up, w_down = weights
    token_count = residual_in.shape[0]
    seq_count = token_count // LEN
    normed1 = low(rms_scale(residual_in) * attn_gain)

    def heads_of(values):
        return values.reshape(seq_count, LEN, HEADS, HD).transpose(0, 2, 1, 3)
    cosine, sine = rope_tables(LEN, HD)
    query = heads_of(low_back(hp_dot(normed1, w_query)))
    keys = heads_of(low_back(hp_dot(normed1, w_key)))
    values = heads_of(low(low_back(hp_dot(normed1, w_value))))
    query = low(rotate(rms_scale(query) * query_gain[None, :, None, :], cosine, sine))
    keys = low(rotate(rms_scale(keys) * key_gain[None, :, None, :], cosine, sine))
    scores = jnp.einsum('bhqd,bhkd->bhqk', query, keys, precision=lax.Precision.HIGHEST) / math.sqrt(HD)
    causal = jnp.arange(LEN, dtype=jnp.int32)[:, None] >= jnp.arange(LEN, dtype=jnp.int32)[None, :]
    scores = low_back(jnp.where(causal[None, None], scores, big_negative))
    row_max = lax.optimization_barrier(jnp.max(scores, axis=-1, keepdims=True))
    exp_vals = jnp.exp(scores - row_max)
    soft_probs = low(exp_vals / lax.optimization_barrier(jnp.sum(exp_vals, axis=-1, keepdims=True)))
    attended = jnp.einsum('bhqk,bhkd->bhqd', soft_probs, values, precision=lax.Precision.HIGHEST)
    attended = low(low_back(attended.transpose(0, 2, 1, 3).reshape(token_count, D)))
    stream = residual_in + low_back(hp_dot(attended, w_output))
    normed2 = low(rms_scale(stream) * ffn_gain)
    logits = low_back(hp_dot(normed2, w_router))
    logit_max = lax.optimization_barrier(jnp.max(logits, axis=-1, keepdims=True))
    logit_exp = jnp.exp(logits - logit_max)
    router_probs = logit_exp / lax.optimization_barrier(jnp.sum(logit_exp, axis=-1, keepdims=True))
    pair_slot, pair_kept, source = slot_table(routes, EXPERTS, CAP)
    pair_gate = jnp.take_along_axis(router_probs, routes, axis=1) * pair_kept.reshape(token_count, TOPK).astype(jnp.float32)
    entered = normed2[source].reshape(EXPERTS, CAP, D)
    gate_val = low_back(jnp.einsum('ecd,edf->ecf', entered, w_gate, precision=lax.Precision.HIGHEST))
    up_val = low_back(jnp.einsum('ecd,edf->ecf', entered, w_up, precision=lax.Precision.HIGHEST))
    hidden = low(gate_val * jax.nn.sigmoid(gate_val) * up_val)
    result = low_back(jnp.einsum('ecf,efd->ecd', hidden, w_down, precision=lax.Precision.HIGHEST))
    padded = jnp.concatenate([result.reshape(EXPERTS * CAP, D), jnp.zeros((1, D), jnp.float32)], axis=0)
    pair_out = padded[pair_slot].reshape(token_count, TOPK, D)
    expert_sum = lax.optimization_barrier(jnp.sum(pair_gate[:, :, None] * pair_out, axis=1))
    return stream + expert_sum

def reference(tokens, cotangent, attn_gain, w_query, w_key, w_value, query_gain, key_gain, w_output, ffn_gain, w_router, w_gate, w_up, w_down, expert_ids):
    weights = tuple((item.astype(jnp.float32) for item in (attn_gain, w_query, w_key, w_value, query_gain, key_gain, w_output, ffn_gain, w_router, w_gate, w_up, w_down)))
    inputs = tokens.astype(jnp.float32).reshape(N_DP, TOK_DP, D)
    routes = expert_ids.reshape(N_DP, TOK_DP, TOPK)
    stepper = jax.checkpoint(shard_forward)

    def layer(weights, inputs):
        return lax.map(lambda shard_pair: stepper(weights, shard_pair[0], shard_pair[1]), (inputs, routes))
    result, pullback = jax.vjp(layer, weights, inputs)
    weight_grads, input_grads = pullback(cotangent.astype(jnp.float32).reshape(N_DP, TOK_DP, D))
    return (result.reshape(TOKENS, D).astype(jnp.bfloat16), input_grads.reshape(TOKENS, D).astype(jnp.bfloat16), weight_grads[0], weight_grads[1], weight_grads[2], weight_grads[3], weight_grads[4], weight_grads[5], weight_grads[6], weight_grads[7], weight_grads[8], weight_grads[9], weight_grads[10], weight_grads[11])
```

```python
import functools
import math

import jax
import jax.numpy as jnp
import numpy as np
from jax import lax
from jax.experimental import pallas as pl
from jax.experimental.pallas import tpu as pltpu
from jax.sharding import PartitionSpec as P

LEN = 1024
EPS = 1e-05
ROPE_BASE = 10000.0
VMEM_LIMIT = 56 << 20
TB = 256
f32, bf16 = jnp.float32, jnp.bfloat16
NT = (((1,), (1,)), ((), ()))
TN = (((0,), (0,)), ((), ()))
NN = (((1,), (0,)), ((), ()))


def dot(left, right, dims=NN):
    return lax.dot_general(left, right, dims, preferred_element_type=f32)


def rope_constants(length, width):
    inv_freq = (ROPE_BASE ** (-(np.arange(width // 2, dtype=np.float32) * 2.0) / width)).astype(np.float32)
    angles = np.arange(length, dtype=np.float32)[:, None] * inv_freq[None, :]
    cosine, sine = np.cos(angles).astype(np.float32), np.sin(angles).astype(np.float32)
    return np.concatenate([cosine, cosine], axis=1), np.concatenate([-sine, sine], axis=1)


def bit_reverse(value, count):
    result, bit = 0, 1
    while bit < count:
        result = result * 2 + (value & 1)
        value >>= 1
        bit *= 2
    return result


def whole_spec():
    return pl.BlockSpec(memory_space=pltpu.VMEM)


def call(body, grid, scalars, ins, in_specs, outs, out_specs, scratch=(), flops=0, moved=0):
    return pl.pallas_call(
        body,
        out_shape=outs,
        grid_spec=pltpu.PrefetchScalarGridSpec(
            num_scalar_prefetch=1,
            grid=grid,
            in_specs=in_specs,
            out_specs=out_specs,
            scratch_shapes=list(scratch),
        ),
        compiler_params=pltpu.CompilerParams(vmem_limit_bytes=VMEM_LIMIT),
        cost_estimate=pl.CostEstimate(flops=int(flops), bytes_accessed=int(moved), transcendentals=0),
    )(scalars, *ins)


def struct(shape, dtype):
    return jax.ShapeDtypeStruct(shape, dtype)


def swap(value, axis, count, mask):
    return lax.ppermute(value, axis, [(i, i ^ mask) for i in range(count)])


def gather_pieces(value, axis, count):
    if count == 4:
        half = value.shape[0] // 2
        one, two = swap(value, axis, count, 1), swap(value, axis, count, 2)
        top, bottom = swap(two[:half], axis, count, 1), swap(one[half:], axis, count, 2)
        return [value, one, two, jnp.concatenate([top, bottom], axis=0)]
    pieces, mask = [value], 1
    while mask < count:
        pieces = pieces + [swap(piece, axis, count, mask) for piece in pieces]
        mask *= 2
    return pieces


def scatter_pieces(pieces, axis, count):
    return [pieces[0]] + [swap(pieces[r], axis, count, r) for r in range(1, count)]


def add_low(left, right):
    return (left.astype(f32) + right.astype(f32)).astype(bf16)


def halve(keep, send, count):
    mask = 1
    while True:
        total = add_low(keep, swap(send, "dp", count, mask))
        mask *= 2
        if mask >= count:
            return total[0]
        middle = total.shape[0] // 2
        keep, send = total[:middle], total[middle:]


def butterfly(value, counts):
    for axis, count in counts:
        mask = 1
        while mask < count:
            value = value + swap(value, axis, count, mask)
            mask *= 2
    return value


def after(value, *others):
    return lax.optimization_barrier((value, *others))[0]


def transpose_blocks(scalars, first, source, target, dp_count):
    width = source.shape[1] // dp_count
    for place in range(dp_count):
        cols = pl.ds(pl.multiple_of(scalars[first + place] * width, width), width)
        target[place * width : (place + 1) * width, :] = source[:, cols].T


def project_kernel(n_tp, heads, scalars, *refs):
    pieces = refs[:n_tp]
    gain, wq, wk, wv, q_gain, k_gain, cosine, sine = refs[n_tp : n_tp + 8]
    x_out, normed_out, factor_out, q_raw, k_raw, q_rot, k_rot, v_out = refs[n_tp + 8 :]
    width = pieces[0].shape[1]
    features = width * n_tp
    values = [piece[...].astype(f32) for piece in pieces]
    squares = sum(jnp.sum(value * value, axis=1, keepdims=True) for value in values)
    factor = lax.rsqrt(squares / features + EPS)
    factor_out[...] = factor
    for r in range(n_tp):
        cols = pl.ds(pl.multiple_of(scalars[r] * width, width), width)
        x_out[:, cols] = pieces[r][...]
        normed_out[:, cols] = (values[r] * factor * gain[:, cols]).astype(bf16)
    normed = normed_out[...]
    cos, sin = cosine[...], sine[...]
    hd = cos.shape[1]
    for weight, head_gain, raw, rotated in ((wq, q_gain, q_raw, q_rot), (wk, k_gain, k_raw, k_rot)):
        product = dot(normed, weight[...])
        raw[...] = product
        for h in range(heads):
            part = product[:, h * hd : (h + 1) * hd]
            scale = lax.rsqrt(jnp.mean(part * part, axis=1, keepdims=True) + EPS)
            part = part * scale * head_gain[h : h + 1, :]
            part = part * cos + pltpu.roll(part, hd // 2, 1) * sin
            rotated[:, h * hd : (h + 1) * hd] = part.astype(bf16)
    v_out[...] = dot(normed, wv[...]).astype(bf16)


def project(scalars, pieces, gain, wq, wk, wv, q_gain, k_gain, cosine, sine):
    n_tp = len(pieces)
    tokens, width = pieces[0].shape
    features = width * n_tp
    heads, hd = q_gain.shape
    local = heads * hd
    rows = lambda w: pl.BlockSpec((TB, w), lambda i, s: (i, 0))
    return call(
        functools.partial(project_kernel, n_tp, heads),
        (tokens // TB,),
        scalars,
        [*pieces, gain, wq, wk, wv, q_gain, k_gain, cosine, sine],
        [rows(width)] * n_tp + [whole_spec()] * 6 + [rows(hd)] * 2,
        [
            struct((tokens, features), bf16),
            struct((tokens, features), bf16),
            struct((tokens, 1), f32),
            struct((tokens, local), f32),
            struct((tokens, local), f32),
            struct((tokens, local), bf16),
            struct((tokens, local), bf16),
            struct((tokens, local), bf16),
        ],
        [rows(features), rows(features), rows(1)] + [rows(local)] * 5,
        flops=6 * tokens * features * local,
        moved=24 << 20,
    )


def attend_kernel(block, scalars, q_ref, k_ref, v_ref, out_ref, total_ref):
    tokens, hd = q_ref.shape
    scale = 1.0 / math.sqrt(hd)
    for i in range(tokens // block):
        rows = slice(i * block, (i + 1) * block)
        reach = (i + 1) * block
        scores = dot(q_ref[rows, :], k_ref[:reach, :], NT) * scale
        at_row = i * block + lax.broadcasted_iota(jnp.int32, scores.shape, 0)
        at_col = lax.broadcasted_iota(jnp.int32, scores.shape, 1)
        scores = jnp.where(at_row >= at_col, scores, -1e30)
        top = jnp.max(scores, axis=1, keepdims=True)
        weights = jnp.exp(scores - top)
        total = jnp.sum(weights, axis=1, keepdims=True)
        probs = (weights * (1.0 / total)).astype(bf16)
        out_ref[rows, :] = dot(probs, v_ref[:reach, :]).astype(bf16)
        total_ref[0, rows, :] = top + jnp.log(total)


def attend(scalars, q_rot, k_rot, value, heads):
    tokens, local = q_rot.shape
    hd = local // heads
    column = pl.BlockSpec((tokens, hd), lambda h, s: (0, h))
    return call(
        functools.partial(attend_kernel, min(256, tokens)),
        (heads,),
        scalars,
        [q_rot, k_rot, value],
        [column] * 3,
        [struct((tokens, local), bf16), struct((heads, tokens, 1), f32)],
        [column, pl.BlockSpec((1, tokens, 1), lambda h, s: (h, 0, 0))],
        flops=4 * tokens * tokens * local,
        moved=8 << 20,
    )


def attend_back_kernel(block, scalars, *refs):
    (q_ref, k_ref, v_ref, go_ref, total_ref, q_raw, k_raw, q_gain, k_gain, cosine, sine) = refs[:11]
    dq_out, dk_out, dv_out, dgain_out, dq_acc, dk_acc, dv_acc = refs[11:]
    tokens, hd = q_ref.shape
    scale = 1.0 / math.sqrt(hd)
    count = tokens // block
    for i in reversed(range(count)):
        rows = slice(i * block, (i + 1) * block)
        reach = (i + 1) * block
        query, grad = q_ref[rows, :], go_ref[rows, :]
        scores = dot(query, k_ref[:reach, :], NT) * scale
        at_row = i * block + lax.broadcasted_iota(jnp.int32, scores.shape, 0)
        at_col = lax.broadcasted_iota(jnp.int32, scores.shape, 1)
        scores = jnp.where(at_row >= at_col, scores, -1e30)
        probs = jnp.exp(scores - total_ref[0, rows, :])
        dprobs = dot(grad, v_ref[:reach, :], NT)
        delta = jnp.sum(dprobs * probs, axis=1, keepdims=True)
        dscores = (probs * (dprobs - delta)).astype(bf16)
        dq_acc[rows, :] = dot(dscores, k_ref[:reach, :]) * scale
        dk = dot(dscores, query, TN) * scale
        dv = dot(probs.astype(bf16), grad, TN)
        if i == count - 1:
            dk_acc[...] = dk
            dv_acc[...] = dv
        else:
            dk_acc[:reach, :] += dk
            dv_acc[:reach, :] += dv
    dv_out[...] = dv_acc[...].astype(bf16)
    cos, sin = cosine[...], sine[...]
    dgains = []
    for acc, raw_ref, gain_ref, out in ((dq_acc, q_raw, q_gain, dq_out), (dk_acc, k_raw, k_gain, dk_out)):
        grad = acc[...]
        grad = grad * cos - pltpu.roll(grad, hd // 2, 1) * sin
        raw = raw_ref[...]
        factor = lax.rsqrt(jnp.mean(raw * raw, axis=1, keepdims=True) + EPS)
        normal = raw * factor
        dgains.append(jnp.sum(grad * normal, axis=0, keepdims=True))
        scaled = grad * gain_ref[0]
        mean = jnp.mean(scaled * normal, axis=1, keepdims=True)
        out[...] = (factor * (scaled - normal * mean)).astype(bf16)
    dgain_out[0] = jnp.concatenate(dgains, axis=0)


def attend_back(scalars, q_rot, k_rot, value, grad, totals, q_raw, k_raw, q_gain, k_gain, cosine, sine):
    tokens, local = q_rot.shape
    heads, hd = q_gain.shape
    column = pl.BlockSpec((tokens, hd), lambda h, s: (0, h))
    gain_spec = pl.BlockSpec((1, 1, hd), lambda h, s: (h, 0, 0))
    table = pl.BlockSpec((tokens, hd), lambda h, s: (0, 0))
    return call(
        functools.partial(attend_back_kernel, min(256, tokens)),
        (heads,),
        scalars,
        [q_rot, k_rot, value, grad, totals, q_raw, k_raw, q_gain[:, None, :], k_gain[:, None, :], cosine, sine],
        [column] * 4
        + [pl.BlockSpec((1, tokens, 1), lambda h, s: (h, 0, 0))]
        + [column] * 2
        + [gain_spec] * 2
        + [table] * 2,
        [struct((tokens, local), bf16)] * 3 + [struct((heads, 2, hd), f32)],
        [column] * 3 + [pl.BlockSpec((1, 2, hd), lambda h, s: (h, 0, 0))],
        [pltpu.VMEM((tokens, hd), f32)] * 3,
        flops=10 * tokens * tokens * local,
        moved=16 << 20,
    )


def whole_grad_kernel(n_tp, dp_count, scalars, *refs):
    pieces = refs[:n_tp]
    whole_out, turned_out = refs[n_tp:]
    width = pieces[0].shape[1]
    for r in range(n_tp):
        cols = pl.ds(pl.multiple_of(scalars[r] * width, width), width)
        whole_out[:, cols] = pieces[r][...]
    transpose_blocks(scalars, n_tp, whole_out, turned_out, dp_count)


def whole_grad(scalars, pieces, dp_count):
    n_tp = len(pieces)
    tokens, width = pieces[0].shape
    features = width * n_tp
    return call(
        functools.partial(whole_grad_kernel, n_tp, dp_count),
        (tokens // TB,),
        scalars,
        pieces,
        [pl.BlockSpec((TB, width), lambda i, s: (i, 0))] * n_tp,
        [struct((tokens, features), bf16), struct((features, tokens), bf16)],
        [
            pl.BlockSpec((TB, features), lambda i, s: (i, 0)),
            pl.BlockSpec((features, TB), lambda i, s: (0, i)),
        ],
        moved=12 << 20,
    )


def stream_kernel(n_tp, dp_count, scalars, *refs):
    pieces = refs[:n_tp]
    x_ref, w_ref, gain, router, kept = refs[n_tp : n_tp + 5]
    stream_out, normed_out, turned_out, factor_out, probs_out, gates_out = refs[n_tp + 5 :]
    width = pieces[0].shape[1]
    total = x_ref[...].astype(f32)
    for r in range(n_tp):
        weight = w_ref[:, pl.ds(scalars[r], 1)]
        total += dot(pieces[r][...], weight.reshape(width, weight.shape[-1]))
    stream_out[...] = total
    factor = lax.rsqrt(jnp.mean(total * total, axis=1, keepdims=True) + EPS)
    factor_out[...] = factor
    normed = (total * factor * gain[...]).astype(bf16)
    normed_out[...] = normed
    logits = dot(normed, router[...])
    power = jnp.exp(logits - jnp.max(logits, axis=1, keepdims=True))
    probs = power / jnp.sum(power, axis=1, keepdims=True)
    probs_out[...] = probs
    gates_out[...] = probs * kept[...]
    transpose_blocks(scalars, n_tp, normed_out, turned_out, dp_count)


def stream_of(scalars, pieces, x, w_all, gain, router, kept, dp_count):
    n_tp = len(pieces)
    tokens, features = x.shape
    experts = router.shape[1]
    rows = lambda w: pl.BlockSpec((TB, w), lambda i, s: (i, 0))
    return call(
        functools.partial(stream_kernel, n_tp, dp_count),
        (tokens // TB,),
        scalars,
        [*pieces, x, w_all, gain, router, kept],
        [rows(pieces[0].shape[1])] * n_tp + [rows(features)] + [whole_spec()] * 3 + [rows(experts)],
        [
            struct((tokens, features), f32),
            struct((tokens, features), bf16),
            struct((features, tokens), bf16),
            struct((tokens, 1), f32),
            struct((tokens, experts), f32),
            struct((tokens, experts), f32),
        ],
        [
            rows(features),
            rows(features),
            pl.BlockSpec((features, TB), lambda i, s: (0, i)),
            rows(1),
            rows(experts),
            rows(experts),
        ],
        flops=2 * tokens * features * features,
        moved=32 << 20,
    )


def expert_kernel(first, scalars, n_ref, g_ref, gates_ref, wg, wu, wd, hidden_out, pair_out, dgate_out):
    step = pl.program_id(0)
    expert = first + step
    width = wg.shape[-1]

    @pl.when(step == 0)
    def _():
        dgate_out[...] = jnp.zeros_like(dgate_out)

    gate_val, up_val = dot(n_ref[...], wg[0]), dot(n_ref[...], wu[0])
    back = dot(g_ref[...], wd[0], NT)
    gates = gates_ref[...]
    here = lax.broadcasted_iota(jnp.int32, gates.shape, 1) == expert
    gate = jnp.sum(jnp.where(here, gates, 0.0), axis=1, keepdims=True)
    sigmoid = 1.0 / (1.0 + jnp.exp(-gate_val))
    swish = gate_val * sigmoid
    hidden = (swish * up_val).astype(bf16).astype(f32)
    hidden_out[0] = (hidden * gate).astype(bf16)
    dgate = jnp.sum(back * hidden, axis=1, keepdims=True)
    dgate_out[...] = jnp.where(here, dgate, dgate_out[...])
    dhidden = back * gate
    pair_out[0, :, :width] = (dhidden * up_val * sigmoid * (1.0 + gate_val * (1.0 - sigmoid))).astype(bf16)
    pair_out[0, :, width:] = (dhidden * swish).astype(bf16)


def run_experts(scalars, normed, grad, gates, wg, wu, wd, first, count):
    tokens, features = normed.shape
    experts, _, width = wg.shape
    weight = lambda shape: pl.BlockSpec((1, *shape), lambda i, s: (first + i, 0, 0))
    given = lambda shape: pl.BlockSpec((1, *shape), lambda i, s: (i, 0, 0))
    return call(
        functools.partial(expert_kernel, first),
        (count,),
        scalars,
        [normed, grad, gates, wg, wu, wd],
        [whole_spec()] * 3 + [weight((features, width))] * 2 + [weight((width, features))],
        [
            struct((count, tokens, width), bf16),
            struct((count, tokens, 2 * width), bf16),
            struct((tokens, experts), f32),
        ],
        [
            given((tokens, width)),
            given((tokens, 2 * width)),
            pl.BlockSpec((tokens, experts), lambda i, s: (0, 0)),
        ],
        flops=6 * count * tokens * features * width,
        moved=count * 5 << 20,
    )


def weight_grads_kernel(scalars, turned, g_turned, hidden, pair, keep_out, send_out):
    half, _, rows, _ = keep_out.shape
    width = hidden.shape[-1]
    first = dot(turned[...], pair[0]).astype(bf16).reshape(2 * half, rows, 2 * width)
    keep_out[:, 0, :, : 2 * width] = first[:half]
    send_out[:, 0, :, : 2 * width] = first[half:]
    second = dot(g_turned[...], hidden[0]).astype(bf16).reshape(2 * half, rows, width)
    keep_out[:, 0, :, 2 * width :] = second[:half]
    send_out[:, 0, :, 2 * width :] = second[half:]


def weight_grads(scalars, turned, g_turned, hidden, pair, offset, count, dp_count):
    features, tokens = turned.shape
    width = hidden.shape[-1]
    half, rows = dp_count // 2, features // dp_count
    out = struct((half, count, rows, 3 * width), bf16)
    out_spec = pl.BlockSpec((half, 1, rows, 3 * width), lambda i, s: (0, i, 0, 0))
    return call(
        weight_grads_kernel,
        (count,),
        scalars,
        [turned, g_turned, hidden, pair],
        [
            whole_spec(),
            whole_spec(),
            pl.BlockSpec((1, tokens, width), lambda i, s: (offset + i, 0, 0)),
            pl.BlockSpec((1, tokens, 2 * width), lambda i, s: (offset + i, 0, 0)),
        ],
        [out, out],
        [out_spec, out_spec],
        flops=6 * count * tokens * features * width,
        moved=count * 5 << 20,
    )


def chunk_specs(chunks, shape):
    specs, first = [], 0
    for chunk in chunks:
        count = chunk.shape[0]
        specs.append(
            pl.BlockSpec(
                (1, *shape), lambda i, s, first=first, count=count: (jnp.clip(i - first, 0, count - 1), 0, 0)
            )
        )
        first += count
    return specs


def input_grad_kernel(sizes, n_tp, scalars, *refs):
    pairs, (wg, wu) = refs[: len(sizes)], refs[len(sizes) : len(sizes) + 2]
    outs, acc = refs[len(sizes) + 2 : -1], refs[-1]
    step = pl.program_id(0)
    width = wg.shape[-1]
    first = 0
    for pair, size in zip(pairs, sizes):

        @pl.when((step >= first) & (step < first + size))
        def _(pair=pair, first=first):
            part = dot(pair[0, :, :width], wg[0], NT) + dot(pair[0, :, width:], wu[0], NT)
            if first == 0:

                @pl.when(step == 0)
                def _():
                    acc[...] = part

                @pl.when(step > 0)
                def _():
                    acc[...] += part

            else:
                acc[...] += part

        first += size

    @pl.when(step == pl.num_programs(0) - 1)
    def _():
        rows = acc.shape[0] // n_tp
        for r in range(n_tp):
            outs[r][...] = acc[pl.ds(pl.multiple_of(scalars[r] * rows, rows), rows), :].astype(bf16)


def input_grads(scalars, pairs, wg, wu, n_tp):
    experts, features, width = wg.shape
    tokens = pairs[0].shape[1]
    rows = tokens // n_tp
    weight = pl.BlockSpec((1, features, width), lambda i, s: (i, 0, 0))
    return call(
        functools.partial(input_grad_kernel, [pair.shape[0] for pair in pairs], n_tp),
        (experts,),
        scalars,
        [*pairs, wg, wu],
        chunk_specs(pairs, (tokens, 2 * width)) + [weight] * 2,
        [struct((rows, features), bf16)] * n_tp,
        [pl.BlockSpec((rows, features), lambda i, s: (0, 0))] * n_tp,
        [pltpu.VMEM((tokens, features), f32)],
        flops=4 * experts * tokens * features * width,
        moved=experts * 3 << 20,
    )


def result_kernel(sizes, n_tp, scalars, *refs):
    hiddens, wd = refs[: len(sizes)], refs[len(sizes)]
    outs, acc = refs[len(sizes) + 1 : -1], refs[-1]
    step = pl.program_id(0)
    first = 0
    for hidden, size in zip(hiddens, sizes):

        @pl.when((step >= first) & (step < first + size))
        def _(hidden=hidden, first=first):
            part = dot(hidden[0], wd[0])
            if first == 0:

                @pl.when(step == 0)
                def _():
                    acc[...] = part

                @pl.when(step > 0)
                def _():
                    acc[...] += part

            else:
                acc[...] += part

        first += size

    @pl.when(step == pl.num_programs(0) - 1)
    def _():
        cols = acc.shape[1] // n_tp
        for r in range(n_tp):
            outs[r][...] = acc[:, pl.ds(pl.multiple_of(scalars[r] * cols, cols), cols)].astype(bf16)


def results(scalars, hiddens, wd, n_tp):
    experts, width, features = wd.shape
    tokens = hiddens[0].shape[1]
    cols = features // n_tp
    return call(
        functools.partial(result_kernel, [hidden.shape[0] for hidden in hiddens], n_tp),
        (experts,),
        scalars,
        [*hiddens, wd],
        chunk_specs(hiddens, (tokens, width)) + [pl.BlockSpec((1, width, features), lambda i, s: (i, 0, 0))],
        [struct((tokens, cols), bf16)] * n_tp,
        [pl.BlockSpec((tokens, cols), lambda i, s: (0, 0))] * n_tp,
        [pltpu.VMEM((tokens, features), f32)],
        flops=2 * experts * tokens * features * width,
        moved=experts * 2 << 20,
    )


def rows_kernel(n_tp, scalars, *refs):
    parts, dgates = refs[:n_tp], refs[n_tp : 2 * n_tp]
    probs, kept, stream, normed, factor, upstream, gain, router = refs[2 * n_tp : 2 * n_tp + 8]
    grad_out, dgain_out, drouter_out = refs[2 * n_tp + 8 :]
    total = sum(part[...].astype(f32) for part in parts)
    dprobs = sum(part[...] for part in dgates) * kept[...]
    soft = probs[...]
    dlogits = soft * (dprobs - jnp.sum(dprobs * soft, axis=1, keepdims=True))
    dlogits = dlogits.astype(bf16)
    drouter_out[...] = dot(normed[...], dlogits, TN)
    total += dot(dlogits, router[...], NT)
    scale = factor[...]
    normal = stream[...] * scale
    dgain_out[...] = jnp.sum(total * normal, axis=0, keepdims=True)
    scaled = total * gain[...]
    mean = jnp.mean(scaled * normal, axis=1, keepdims=True)
    grad_out[...] = (upstream[...].astype(f32) + scale * (scaled - normal * mean)).astype(bf16)


def stream_grad_rows(scalars, parts, dgates, probs, kept, stream, normed, factor, upstream, gain, router):
    n_tp = len(parts)
    rows, features = parts[0].shape
    experts = router.shape[1]
    mine = lambda w: pl.BlockSpec((rows, w), lambda i, s: (s[0], 0))
    plain = lambda h, w: pl.BlockSpec((h, w), lambda i, s: (0, 0))
    return call(
        functools.partial(rows_kernel, n_tp),
        (1,),
        scalars,
        [*parts, *dgates, probs, kept, stream, normed, factor, upstream, gain, router],
        [plain(rows, features)] * n_tp
        + [plain(rows, experts)] * n_tp
        + [mine(experts), mine(experts), mine(features), mine(features), mine(1), mine(features)]
        + [plain(1, features), plain(features, experts)],
        [struct((rows, features), bf16), struct((1, features), f32), struct((features, experts), f32)],
        [plain(rows, features), plain(1, features), plain(features, experts)],
        flops=1 << 24,
        moved=10 << 20,
    )


def attended_grad_kernel(n_tp, scalars, *refs):
    pieces, w_ref = refs[:n_tp], refs[n_tp]
    whole_out, grad_out = refs[n_tp + 1 :]
    rows = pieces[0].shape[0]
    for r in range(n_tp):
        place = pl.ds(pl.multiple_of(scalars[r] * rows, rows), rows)
        whole_out[place, :] = pieces[r][...]
    grad_out[...] = dot(whole_out[...], w_ref[...], NT).astype(bf16)


def attended_grad(scalars, pieces, w_output):
    n_tp = len(pieces)
    rows, features = pieces[0].shape
    local = w_output.shape[0]
    tokens = rows * n_tp
    plain = lambda h, w: pl.BlockSpec((h, w), lambda i, s: (0, 0))
    return call(
        functools.partial(attended_grad_kernel, n_tp),
        (1,),
        scalars,
        [*pieces, w_output],
        [plain(rows, features)] * n_tp + [plain(local, features)],
        [struct((tokens, features), bf16), struct((tokens, local), bf16)],
        [plain(tokens, features), plain(tokens, local)],
        flops=2 * tokens * features * local,
        moved=11 << 20,
    )


def normed_grad_kernel(scalars, dq, dk, dv, wq, wk, wv, x_ref, factor, gain, out, dot_out, dgain_out):
    total = dot(dq[...], wq[...], NT) + dot(dk[...], wk[...], NT) + dot(dv[...], wv[...], NT)
    out[...] = total.astype(bf16)
    normal = x_ref[...].astype(f32) * factor[...]
    product = total * normal
    dgain_out[...] = jnp.sum(product, axis=0, keepdims=True)
    dot_out[...] = jnp.sum(product * gain[...], axis=1, keepdims=True)


def normed_grad(scalars, r, dq, dk, dv, wq, wk, wv, x, factor, gain, n_tp):
    tokens, local = dq.shape
    features = wq.shape[0]
    width = features // n_tp
    plain = lambda h, w: pl.BlockSpec((h, w), lambda i, s: (0, 0))
    weight = pl.BlockSpec((width, local), lambda i, s: (s[r], 0))
    return call(
        normed_grad_kernel,
        (1,),
        scalars,
        [dq, dk, dv, wq, wk, wv, x, factor, gain],
        [plain(tokens, local)] * 3
        + [weight] * 3
        + [
            pl.BlockSpec((tokens, width), lambda i, s: (0, s[r])),
            plain(tokens, 1),
            pl.BlockSpec((1, width), lambda i, s: (0, s[r])),
        ],
        [struct((tokens, width), bf16), struct((tokens, 1), f32), struct((1, width), f32)],
        [plain(tokens, width), plain(tokens, 1), plain(1, width)],
        flops=6 * tokens * local * width,
        moved=7 << 20,
    )


def kept_pairs(expert_ids, experts, capacity):
    tokens = expert_ids.shape[0]
    named = jnp.any(expert_ids[:, :, None] == jnp.arange(experts, dtype=jnp.int32), axis=1)
    earlier = jnp.arange(tokens)[:, None] > jnp.arange(tokens)[None, :]
    rank = dot(earlier.astype(bf16), named.astype(bf16))
    return (named & (rank < capacity)).astype(f32)


def body(n_dp, n_tp, cosine, sine, tokens, cotangent, attn_gain, w_query, w_key, w_value, query_gain, key_gain,
         w_output, ffn_gain, w_router, w_gate, w_up, w_down, expert_ids):
    tp, dp = lax.axis_index("tensor"), lax.axis_index("dp")
    scalars = jnp.stack(
        [tp ^ r for r in range(n_tp)] + [dp ^ bit_reverse(place, n_dp) for place in range(n_dp)]
    ).astype(jnp.int32)
    token_count, width = tokens.shape
    features = width * n_tp
    heads, hd = query_gain.shape
    local = heads * hd
    experts = w_router.shape[1]
    capacity = token_count * expert_ids.shape[1] // experts
    gain1, gain2 = attn_gain[None, :], ffn_gain[None, :]

    share = local // n_dp
    w_share = lax.dynamic_slice_in_dim(w_output, dp * share, share, 0)
    w_all = lax.all_gather(lax.all_gather(w_share, "tensor"), "dp")

    x_pieces = gather_pieces(tokens, "tensor", n_tp)
    x, normed1, factor1, q_raw, k_raw, q_rot, k_rot, value = project(
        scalars, x_pieces, gain1, w_query, w_key, w_value, query_gain, key_gain, cosine, sine
    )
    g_pieces = gather_pieces(after(cotangent, x_pieces[-1]), "tensor", n_tp)
    upstream, g_turned = whole_grad(scalars, g_pieces, n_dp)
    kept = kept_pairs(expert_ids, experts, capacity)
    attended, totals = attend(scalars, q_rot, k_rot, value, heads)
    stream, normed2, turned, factor2, probs, gates = stream_of(
        scalars, gather_pieces(attended, "tensor", n_tp), x, w_all, gain2, w_router, kept, n_dp
    )

    blocks = [(0, 2), (2, 4), (6, experts - 6)]
    hiddens, pairs, dgates, sums = [], [], [], []
    start = normed2
    for index, (first, count) in enumerate(blocks):
        hidden, pair, dgate = run_experts(scalars, start, upstream, gates, w_gate, w_up, w_down, first, count)
        hiddens.append(hidden)
        pairs.append(pair)
        dgates.append(dgate)
        if index < len(blocks) - 1:
            keep, send = weight_grads(scalars, turned, g_turned, hidden, pair, 0, count, n_dp)
            sums.append((first, count, keep, send))
            start = after(normed2, keep)
    dgate = sum(dgates)
    input_parts = input_grads(scalars, pairs, w_gate, w_up, n_tp)
    rows = token_count // n_tp
    dgate_rows = [lax.dynamic_slice_in_dim(dgate, (tp ^ r) * rows, rows, 0) for r in range(n_tp)]
    dgate_parts = scatter_pieces(dgate_rows, "tensor", n_tp)
    arrived = scatter_pieces(input_parts, "tensor", n_tp)

    first, count = blocks[-1]
    ready = input_parts[0]
    for offset in range(0, count, 4):
        size = min(4, count - offset)
        keep, send = weight_grads(
            scalars, after(turned, ready), g_turned, hiddens[-1], pairs[-1], offset, size, n_dp
        )
        ready = keep
        sums.append((first + offset, size, keep, send))
        if offset == 0:
            result_parts = results(scalars, hiddens, after(w_down, ready), n_tp)
            ready = result_parts[0]
    reduced = [halve(keep, send, n_dp) for _, _, keep, send in sums]

    dattn_rows, dgain2, drouter = stream_grad_rows(
        scalars, arrived, dgate_parts, probs, kept, stream, normed2, factor2, upstream, gain2, w_router
    )
    dattn, dattended = attended_grad(scalars, gather_pieces(dattn_rows, "tensor", n_tp), w_output)
    dq, dk, dv, dhead_gains = attend_back(
        scalars, q_rot, k_rot, value, dattended, totals, q_raw, k_raw, query_gain, key_gain, cosine, sine
    )
    slices, row_dots, dgain1 = [None] * n_tp, [None] * n_tp, [None] * n_tp
    for r in reversed(range(n_tp)):
        slices[r], row_dots[r], dgain1[r] = normed_grad(
            scalars, r, dq, dk, dv, w_query, w_key, w_value, x, factor1, gain1, n_tp
        )
    row_dot = butterfly(sum(row_dots).reshape(8, token_count // 8), [("tensor", n_tp)])
    arrived1 = scatter_pieces(slices, "tensor", n_tp)
    dnormed1 = sum(part.astype(f32) for part in arrived1)
    my_cols = lambda array: lax.dynamic_slice_in_dim(array, tp * width, width, 1)
    normal1 = tokens.astype(f32) * factor1
    input_grad = my_cols(dattn).astype(f32) + factor1 * (
        dnormed1 * my_cols(gain1) - normal1 * (row_dot.reshape(token_count, 1) / features)
    )
    arrived_y = scatter_pieces(result_parts, "tensor", n_tp)
    output = my_cols(stream) + sum(part.astype(f32) for part in arrived_y)

    def spread(value, dimension):
        return lax.psum_scatter(value.astype(bf16), "dp", scatter_dimension=dimension, tiled=True).astype(f32)

    grad_output = spread(dot(attended, dattn, TN), 1)
    dqkv = jnp.concatenate([dq, dk, dv], axis=1)
    grad_qkv = spread(dot(normed1, dqkv, TN), 0)

    everywhere = [("dp", n_dp), ("tensor", n_tp)]
    early = butterfly(jnp.concatenate([drouter.T, dgain2], axis=0), everywhere)
    gain_row = jnp.zeros((1, features), f32)
    for r in range(n_tp):
        gain_row = lax.dynamic_update_slice(gain_row, dgain1[r], (0, (tp ^ r) * width))
    gain_row = butterfly(gain_row, everywhere)
    head_gains = butterfly(dhead_gains, [("dp", n_dp)])
    mine = lambda array, dimension: lax.dynamic_slice_in_dim(
        array, dp * (array.shape[dimension] // n_dp), array.shape[dimension] // n_dp, dimension
    )
    early = mine(early, 1)
    head_gains = mine(head_gains, 2)

    expert_width = w_gate.shape[-1]
    stacked = jnp.concatenate(reduced, axis=0)
    grad_gate = stacked[:, :, :expert_width].astype(f32)
    grad_up = stacked[:, :, expert_width : 2 * expert_width].astype(f32)
    grad_down = jnp.swapaxes(stacked[:, :, 2 * expert_width :], 1, 2).astype(f32)
    return (
        output.astype(bf16),
        input_grad.astype(bf16),
        mine(gain_row, 1)[0],
        grad_qkv[:, :local],
        grad_qkv[:, local : 2 * local],
        grad_qkv[:, 2 * local :],
        head_gains[:, 0],
        head_gains[:, 1],
        grad_output,
        early[experts],
        early[:experts].T,
        grad_gate,
        grad_up,
        grad_down,
    )


def solution(mesh):
    placed = (
        P("dp", "tensor"),
        P("dp", "tensor"),
        P(),
        P(None, "tensor"),
        P(None, "tensor"),
        P(None, "tensor"),
        P("tensor", None),
        P("tensor", None),
        P("tensor", None),
        P(),
        P(),
        P(None, None, "tensor"),
        P(None, None, "tensor"),
        P(None, "tensor", None),
        P("dp", None),
    )
    n_dp, n_tp = mesh.shape["dp"], mesh.shape["tensor"]

    def layer(*args):
        cosine, sine = rope_constants(LEN, args[6].shape[1])
        return body(n_dp, n_tp, jnp.asarray(cosine), jnp.asarray(sine), *args)

    return jax.shard_map(
        layer,
        mesh=mesh,
        in_specs=placed,
        out_specs=(
            P("dp", "tensor"),
            P("dp", "tensor"),
            P("dp"),
            P("dp", "tensor"),
            P("dp", "tensor"),
            P("dp", "tensor"),
            P("tensor", "dp"),
            P("tensor", "dp"),
            P("tensor", "dp"),
            P("dp"),
            P("dp", None),
            P(None, "dp", "tensor"),
            P(None, "dp", "tensor"),
            P(None, "tensor", "dp"),
        ),
        check_vma=False,
    )
```

```python
import functools
import math

import jax
import jax.numpy as jnp
import numpy as np
from jax import lax
from jax.experimental import pallas as pl
from jax.experimental.pallas import tpu as pltpu
from jax.sharding import PartitionSpec as P

LEN = 1024
EPS = 1e-05
ROPE_BASE = 10000.0
VMEM_LIMIT = 56 << 20
TB = 256
f32, bf16 = jnp.float32, jnp.bfloat16
NT = (((1,), (1,)), ((), ()))
TN = (((0,), (0,)), ((), ()))
NN = (((1,), (0,)), ((), ()))


def dot(left, right, dims=NN):
    return lax.dot_general(left, right, dims, preferred_element_type=f32)


def rope_constants(length, width):
    inv_freq = (ROPE_BASE ** (-(np.arange(width // 2, dtype=np.float32) * 2.0) / width)).astype(np.float32)
    angles = np.arange(length, dtype=np.float32)[:, None] * inv_freq[None, :]
    cosine, sine = np.cos(angles).astype(np.float32), np.sin(angles).astype(np.float32)
    return np.concatenate([cosine, cosine], axis=1), np.concatenate([-sine, sine], axis=1)


def bit_reverse(value, count):
    result, bit = 0, 1
    while bit < count:
        result = result * 2 + (value & 1)
        value >>= 1
        bit *= 2
    return result


def whole_spec():
    return pl.BlockSpec(memory_space=pltpu.VMEM)


def call(body, grid, scalars, ins, in_specs, outs, out_specs, scratch=(), flops=0, moved=0):
    return pl.pallas_call(
        body,
        out_shape=outs,
        grid_spec=pltpu.PrefetchScalarGridSpec(
            num_scalar_prefetch=1,
            grid=grid,
            in_specs=in_specs,
            out_specs=out_specs,
            scratch_shapes=list(scratch),
        ),
        compiler_params=pltpu.CompilerParams(vmem_limit_bytes=VMEM_LIMIT),
        cost_estimate=pl.CostEstimate(flops=int(flops), bytes_accessed=int(moved), transcendentals=0),
    )(scalars, *ins)


def struct(shape, dtype):
    return jax.ShapeDtypeStruct(shape, dtype)


def swap(value, axis, count, mask):
    return lax.ppermute(value, axis, [(i, i ^ mask) for i in range(count)])


def gather_pieces(value, axis, count):
    if count == 4:
        half = value.shape[0] // 2
        one, two = swap(value, axis, count, 1), swap(value, axis, count, 2)
        top, bottom = swap(two[:half], axis, count, 1), swap(one[half:], axis, count, 2)
        return [value, one, two, jnp.concatenate([top, bottom], axis=0)]
    pieces, mask = [value], 1
    while mask < count:
        pieces = pieces + [swap(piece, axis, count, mask) for piece in pieces]
        mask *= 2
    return pieces


def scatter_pieces(pieces, axis, count):
    return [pieces[0]] + [swap(pieces[r], axis, count, r) for r in range(1, count)]


def add_low(left, right):
    return (left.astype(f32) + right.astype(f32)).astype(bf16)


def add_halves(keep, arrived):
    middle = keep.shape[0] // 2
    return add_low(keep[:middle], arrived[:middle]), add_low(keep[middle:], arrived[middle:])


def butterfly(value, counts):
    for axis, count in counts:
        mask = 1
        while mask < count:
            value = value + swap(value, axis, count, mask)
            mask *= 2
    return value


def after(value, *others):
    return lax.optimization_barrier((value, *others))[0]


def transpose_blocks(scalars, first, source, target, dp_count):
    width = source.shape[1] // dp_count
    for place in range(dp_count):
        cols = pl.ds(pl.multiple_of(scalars[first + place] * width, width), width)
        target[place * width : (place + 1) * width, :] = source[:, cols].T


def project_kernel(n_tp, heads, scalars, *refs):
    pieces = refs[:n_tp]
    gain, wq, wk, wv, q_gain, k_gain, cosine, sine = refs[n_tp : n_tp + 8]
    x_out, normed_out, factor_out, q_raw, k_raw, q_rot, k_rot, v_out = refs[n_tp + 8 :]
    width = pieces[0].shape[1]
    features = width * n_tp
    values = [piece[...].astype(f32) for piece in pieces]
    squares = sum(jnp.sum(value * value, axis=1, keepdims=True) for value in values)
    factor = lax.rsqrt(squares / features + EPS)
    factor_out[...] = factor
    for r in range(n_tp):
        cols = pl.ds(pl.multiple_of(scalars[r] * width, width), width)
        x_out[:, cols] = pieces[r][...]
        normed_out[:, cols] = (values[r] * factor * gain[:, cols]).astype(bf16)
    normed = normed_out[...]
    cos, sin = cosine[...], sine[...]
    hd = cos.shape[1]
    for weight, head_gain, raw, rotated in ((wq, q_gain, q_raw, q_rot), (wk, k_gain, k_raw, k_rot)):
        product = dot(normed, weight[...])
        raw[...] = product
        for h in range(heads):
            part = product[:, h * hd : (h + 1) * hd]
            scale = lax.rsqrt(jnp.mean(part * part, axis=1, keepdims=True) + EPS)
            part = part * scale * head_gain[h : h + 1, :]
            part = part * cos + pltpu.roll(part, hd // 2, 1) * sin
            rotated[:, h * hd : (h + 1) * hd] = part.astype(bf16)
    v_out[...] = dot(normed, wv[...]).astype(bf16)


def project(scalars, pieces, gain, wq, wk, wv, q_gain, k_gain, cosine, sine):
    n_tp = len(pieces)
    tokens, width = pieces[0].shape
    features = width * n_tp
    heads, hd = q_gain.shape
    local = heads * hd
    rows = lambda w: pl.BlockSpec((TB, w), lambda i, s: (i, 0))
    return call(
        functools.partial(project_kernel, n_tp, heads),
        (tokens // TB,),
        scalars,
        [*pieces, gain, wq, wk, wv, q_gain, k_gain, cosine, sine],
        [rows(width)] * n_tp + [whole_spec()] * 6 + [rows(hd)] * 2,
        [
            struct((tokens, features), bf16),
            struct((tokens, features), bf16),
            struct((tokens, 1), f32),
            struct((tokens, local), f32),
            struct((tokens, local), f32),
            struct((tokens, local), bf16),
            struct((tokens, local), bf16),
            struct((tokens, local), bf16),
        ],
        [rows(features), rows(features), rows(1)] + [rows(local)] * 5,
        flops=6 * tokens * features * local,
        moved=24 << 20,
    )


def attend_kernel(block, scalars, q_ref, k_ref, v_ref, out_ref, total_ref):
    tokens, hd = q_ref.shape
    scale = 1.0 / math.sqrt(hd)
    for i in range(tokens // block):
        rows = slice(i * block, (i + 1) * block)
        reach = (i + 1) * block
        scores = dot(q_ref[rows, :], k_ref[:reach, :], NT) * scale
        at_row = i * block + lax.broadcasted_iota(jnp.int32, scores.shape, 0)
        at_col = lax.broadcasted_iota(jnp.int32, scores.shape, 1)
        scores = jnp.where(at_row >= at_col, scores, -1e30)
        top = jnp.max(scores, axis=1, keepdims=True)
        weights = jnp.exp(scores - top)
        total = jnp.sum(weights, axis=1, keepdims=True)
        probs = (weights * (1.0 / total)).astype(bf16)
        out_ref[rows, :] = dot(probs, v_ref[:reach, :]).astype(bf16)
        total_ref[0, rows, :] = top + jnp.log(total)


def attend(scalars, q_rot, k_rot, value, heads):
    tokens, local = q_rot.shape
    hd = local // heads
    column = pl.BlockSpec((tokens, hd), lambda h, s: (0, h))
    return call(
        functools.partial(attend_kernel, min(256, tokens)),
        (heads,),
        scalars,
        [q_rot, k_rot, value],
        [column] * 3,
        [struct((tokens, local), bf16), struct((heads, tokens, 1), f32)],
        [column, pl.BlockSpec((1, tokens, 1), lambda h, s: (h, 0, 0))],
        flops=4 * tokens * tokens * local,
        moved=8 << 20,
    )


def attend_back_kernel(block, scalars, *refs):
    (q_ref, k_ref, v_ref, go_ref, total_ref, q_raw, k_raw, q_gain, k_gain, cosine, sine) = refs[:11]
    dq_out, dk_out, dv_out, dgain_out, dq_acc, dk_acc, dv_acc = refs[11:]
    tokens, hd = q_ref.shape
    scale = 1.0 / math.sqrt(hd)
    count = tokens // block
    for i in reversed(range(count)):
        rows = slice(i * block, (i + 1) * block)
        reach = (i + 1) * block
        query, grad = q_ref[rows, :], go_ref[rows, :]
        scores = dot(query, k_ref[:reach, :], NT) * scale
        at_row = i * block + lax.broadcasted_iota(jnp.int32, scores.shape, 0)
        at_col = lax.broadcasted_iota(jnp.int32, scores.shape, 1)
        scores = jnp.where(at_row >= at_col, scores, -1e30)
        probs = jnp.exp(scores - total_ref[0, rows, :])
        dprobs = dot(grad, v_ref[:reach, :], NT)
        delta = jnp.sum(dprobs * probs, axis=1, keepdims=True)
        dscores = (probs * (dprobs - delta)).astype(bf16)
        dq_acc[rows, :] = dot(dscores, k_ref[:reach, :]) * scale
        dk = dot(dscores, query, TN) * scale
        dv = dot(probs.astype(bf16), grad, TN)
        if i == count - 1:
            dk_acc[...] = dk
            dv_acc[...] = dv
        else:
            dk_acc[:reach, :] += dk
            dv_acc[:reach, :] += dv
    dv_out[...] = dv_acc[...].astype(bf16)
    cos, sin = cosine[...], sine[...]
    dgains = []
    for acc, raw_ref, gain_ref, out in ((dq_acc, q_raw, q_gain, dq_out), (dk_acc, k_raw, k_gain, dk_out)):
        grad = acc[...]
        grad = grad * cos - pltpu.roll(grad, hd // 2, 1) * sin
        raw = raw_ref[...]
        factor = lax.rsqrt(jnp.mean(raw * raw, axis=1, keepdims=True) + EPS)
        normal = raw * factor
        dgains.append(jnp.sum(grad * normal, axis=0, keepdims=True))
        scaled = grad * gain_ref[0]
        mean = jnp.mean(scaled * normal, axis=1, keepdims=True)
        out[...] = (factor * (scaled - normal * mean)).astype(bf16)
    dgain_out[0] = jnp.concatenate(dgains, axis=0)


def attend_back(scalars, q_rot, k_rot, value, grad, totals, q_raw, k_raw, q_gain, k_gain, cosine, sine):
    tokens, local = q_rot.shape
    heads, hd = q_gain.shape
    column = pl.BlockSpec((tokens, hd), lambda h, s: (0, h))
    gain_spec = pl.BlockSpec((1, 1, hd), lambda h, s: (h, 0, 0))
    table = pl.BlockSpec((tokens, hd), lambda h, s: (0, 0))
    return call(
        functools.partial(attend_back_kernel, min(256, tokens)),
        (heads,),
        scalars,
        [q_rot, k_rot, value, grad, totals, q_raw, k_raw, q_gain[:, None, :], k_gain[:, None, :], cosine, sine],
        [column] * 4
        + [pl.BlockSpec((1, tokens, 1), lambda h, s: (h, 0, 0))]
        + [column] * 2
        + [gain_spec] * 2
        + [table] * 2,
        [struct((tokens, local), bf16)] * 3 + [struct((heads, 2, hd), f32)],
        [column] * 3 + [pl.BlockSpec((1, 2, hd), lambda h, s: (h, 0, 0))],
        [pltpu.VMEM((tokens, hd), f32)] * 3,
        flops=10 * tokens * tokens * local,
        moved=16 << 20,
    )


def whole_grad_kernel(n_tp, dp_count, scalars, *refs):
    pieces = refs[:n_tp]
    whole_out, turned_out = refs[n_tp:]
    width = pieces[0].shape[1]
    for r in range(n_tp):
        cols = pl.ds(pl.multiple_of(scalars[r] * width, width), width)
        whole_out[:, cols] = pieces[r][...]
    transpose_blocks(scalars, n_tp, whole_out, turned_out, dp_count)


def whole_grad(scalars, pieces, dp_count):
    n_tp = len(pieces)
    tokens, width = pieces[0].shape
    features = width * n_tp
    return call(
        functools.partial(whole_grad_kernel, n_tp, dp_count),
        (tokens // TB,),
        scalars,
        pieces,
        [pl.BlockSpec((TB, width), lambda i, s: (i, 0))] * n_tp,
        [struct((tokens, features), bf16), struct((features, tokens), bf16)],
        [
            pl.BlockSpec((TB, features), lambda i, s: (i, 0)),
            pl.BlockSpec((features, TB), lambda i, s: (0, i)),
        ],
        moved=12 << 20,
    )


def stream_kernel(n_tp, dp_count, scalars, *refs):
    pieces = refs[:n_tp]
    x_ref, w_ref, gain, router, kept = refs[n_tp : n_tp + 5]
    stream_out, normed_out, mine_out, turned_out, factor_out, probs_out, gates_out = refs[n_tp + 5 :]
    width = pieces[0].shape[1]
    total = x_ref[...].astype(f32)
    for r in range(n_tp):
        weight = w_ref[:, pl.ds(scalars[r], 1)]
        total += dot(pieces[r][...], weight.reshape(width, weight.shape[-1]))
    stream_out[...] = total
    factor = lax.rsqrt(jnp.mean(total * total, axis=1, keepdims=True) + EPS)
    factor_out[...] = factor
    normed = (total * factor * gain[...]).astype(bf16)
    normed_out[...] = normed
    mine_out[...] = normed_out[:, pl.ds(pl.multiple_of(scalars[0] * width, width), width)]
    logits = dot(normed, router[...])
    power = jnp.exp(logits - jnp.max(logits, axis=1, keepdims=True))
    probs = power / jnp.sum(power, axis=1, keepdims=True)
    probs_out[...] = probs
    gates_out[...] = probs * kept[...]
    transpose_blocks(scalars, n_tp, normed_out, turned_out, dp_count)


def stream_of(scalars, pieces, x, w_all, gain, router, kept, dp_count):
    n_tp = len(pieces)
    tokens, features = x.shape
    experts = router.shape[1]
    rows = lambda w: pl.BlockSpec((TB, w), lambda i, s: (i, 0))
    return call(
        functools.partial(stream_kernel, n_tp, dp_count),
        (tokens // TB,),
        scalars,
        [*pieces, x, w_all, gain, router, kept],
        [rows(pieces[0].shape[1])] * n_tp + [rows(features)] + [whole_spec()] * 3 + [rows(experts)],
        [
            struct((tokens, features), f32),
            struct((tokens, features), bf16),
            struct((tokens, features // n_tp), bf16),
            struct((features, tokens), bf16),
            struct((tokens, 1), f32),
            struct((tokens, experts), f32),
            struct((tokens, experts), f32),
        ],
        [
            rows(features),
            rows(features),
            rows(features // n_tp),
            pl.BlockSpec((features, TB), lambda i, s: (0, i)),
            rows(1),
            rows(experts),
            rows(experts),
        ],
        flops=2 * tokens * features * features,
        moved=32 << 20,
    )


def expert_kernel(first, shift, scalars, n_ref, g_ref, gates_ref, wg, wu, wd, hidden_out, pair_out, dgate_out):
    step = pl.program_id(0)
    expert = first + step + (0 if shift is None else scalars[shift])
    width = wg.shape[-1]

    @pl.when(step == 0)
    def _():
        dgate_out[...] = jnp.zeros_like(dgate_out)

    gate_val, up_val = dot(n_ref[...], wg[0]), dot(n_ref[...], wu[0])
    back = dot(g_ref[...], wd[0], NT)
    gates = gates_ref[...]
    here = lax.broadcasted_iota(jnp.int32, gates.shape, 1) == expert
    gate = jnp.sum(jnp.where(here, gates, 0.0), axis=1, keepdims=True)
    sigmoid = 1.0 / (1.0 + jnp.exp(-gate_val))
    swish = gate_val * sigmoid
    hidden = (swish * up_val).astype(bf16).astype(f32)
    hidden_out[0] = (hidden * gate).astype(bf16)
    dgate = jnp.sum(back * hidden, axis=1, keepdims=True)
    dgate_out[...] = jnp.where(here, dgate, dgate_out[...])
    dhidden = back * gate
    pair_out[0, :, :width] = (dhidden * up_val * sigmoid * (1.0 + gate_val * (1.0 - sigmoid))).astype(bf16)
    pair_out[0, :, width:] = (dhidden * swish).astype(bf16)


def run_experts(scalars, normed, grad, gates, wg, wu, wd, first, count, shift=None):
    tokens, features = normed.shape
    experts, _, width = wg.shape
    place = lambda i, s: first + i + (0 if shift is None else s[shift])
    weight = lambda shape: pl.BlockSpec((1, *shape), lambda i, s: (place(i, s), 0, 0))
    given = lambda shape: pl.BlockSpec((1, *shape), lambda i, s: (i, 0, 0))
    return call(
        functools.partial(expert_kernel, first, shift),
        (count,),
        scalars,
        [normed, grad, gates, wg, wu, wd],
        [whole_spec()] * 3 + [weight((features, width))] * 2 + [weight((width, features))],
        [
            struct((count, tokens, width), bf16),
            struct((count, tokens, 2 * width), bf16),
            struct((tokens, experts), f32),
        ],
        [
            given((tokens, width)),
            given((tokens, 2 * width)),
            pl.BlockSpec((tokens, experts), lambda i, s: (0, 0)),
        ],
        flops=6 * count * tokens * features * width,
        moved=count * 5 << 20,
    )


def weight_grads_kernel(scalars, turned, g_turned, hidden, pair, keep_out, send_out):
    half, _, rows, _ = keep_out.shape
    width = hidden.shape[-1]
    first = dot(turned[...], pair[0]).astype(bf16).reshape(2 * half, rows, 2 * width)
    keep_out[:, 0, :, : 2 * width] = first[:half]
    send_out[:, 0, :, : 2 * width] = first[half:]
    second = dot(g_turned[...], hidden[0]).astype(bf16).reshape(2 * half, rows, width)
    keep_out[:, 0, :, 2 * width :] = second[:half]
    send_out[:, 0, :, 2 * width :] = second[half:]


def weight_grads(scalars, turned, g_turned, hidden, pair, offset, count, dp_count):
    features, tokens = turned.shape
    width = hidden.shape[-1]
    half, rows = dp_count // 2, features // dp_count
    out = struct((half, count, rows, 3 * width), bf16)
    out_spec = pl.BlockSpec((half, 1, rows, 3 * width), lambda i, s: (0, i, 0, 0))
    return call(
        weight_grads_kernel,
        (count,),
        scalars,
        [turned, g_turned, hidden, pair],
        [
            whole_spec(),
            whole_spec(),
            pl.BlockSpec((1, tokens, width), lambda i, s: (offset + i, 0, 0)),
            pl.BlockSpec((1, tokens, 2 * width), lambda i, s: (offset + i, 0, 0)),
        ],
        [out, out],
        [out_spec, out_spec],
        flops=6 * count * tokens * features * width,
        moved=count * 5 << 20,
    )


def inner_swap(index):
    return (index & ~3) | ((index & 1) << 1) | ((index >> 1) & 1)


def shared_grads_kernel(scalars, *refs):
    turned, turned2, g_turned, g_turned2, hidden, hidden2, pair, pair2, keep_out, send_out = refs
    half, _, rows, _ = keep_out.shape
    width = hidden.shape[-1]
    first = dot(turned[...], pair[0]) + dot(turned2[...], pair2[0])
    first = first.astype(bf16).reshape(2 * half, rows, 2 * width)
    second = dot(g_turned[...], hidden[0]) + dot(g_turned2[...], hidden2[0])
    second = second.astype(bf16).reshape(2 * half, rows, width)
    for out, base in ((keep_out, 0), (send_out, half)):
        for place in range(half):
            out[inner_swap(place), 0, :, : 2 * width] = first[base + place]
            out[inner_swap(place), 0, :, 2 * width :] = second[base + place]


def shared_grads(scalars, turned, turned2, g_turned, g_turned2, hidden, hidden2, pair, pair2, shift, offset, count,
                 dp_count):
    features, tokens = turned.shape
    width = hidden.shape[-1]
    half, rows = dp_count // 2, features // dp_count
    out = struct((half, count, rows, 3 * width), bf16)
    out_spec = pl.BlockSpec((half, 1, rows, 3 * width), lambda i, s: (0, i, 0, 0))
    mine = lambda w: pl.BlockSpec((1, tokens, w), lambda i, s: (s[shift] + offset + i, 0, 0))
    other = lambda w: pl.BlockSpec((1, tokens, w), lambda i, s: (offset + i, 0, 0))
    return call(
        shared_grads_kernel,
        (count,),
        scalars,
        [turned, turned2, g_turned, g_turned2, hidden, hidden2, pair, pair2],
        [whole_spec()] * 4 + [mine(width), other(width), mine(2 * width), other(2 * width)],
        [out, out],
        [out_spec, out_spec],
        flops=12 * count * tokens * features * width,
        moved=(16 + count * 6) << 20,
    )


def finish_kernel(n_parts, n_old, scalars, *refs):
    parts = refs[:n_parts]
    gate_out, up_out, down_out = refs[n_parts + n_old :]
    width = gate_out.shape[-1]
    total = sum(part[0].astype(f32) for part in parts)
    gate_out[0] = total[:, :width]
    up_out[0] = total[:, width : 2 * width]
    down_out[0] = total[:, 2 * width :].T


def finish(scalars, parts, old, first, shift, experts):
    count, rows, wide = parts[0].shape
    width = wide // 3
    place = lambda i, s: (first + i + (0 if shift is None else s[shift]), 0, 0)
    spec = pl.BlockSpec((1, rows, width), place)
    down_spec = pl.BlockSpec((1, width, rows), place)
    shapes = [struct((experts, rows, width), f32)] * 2 + [struct((experts, width, rows), f32)]
    return pl.pallas_call(
        functools.partial(finish_kernel, len(parts), len(old)),
        out_shape=shapes,
        grid_spec=pltpu.PrefetchScalarGridSpec(
            num_scalar_prefetch=1,
            grid=(count,),
            in_specs=[pl.BlockSpec((1, rows, wide), lambda i, s: (i, 0, 0))] * len(parts)
            + [pl.BlockSpec(memory_space=pl.ANY)] * len(old),
            out_specs=[spec, spec, down_spec],
        ),
        input_output_aliases={1 + len(parts) + k: k for k in range(len(old))},
        compiler_params=pltpu.CompilerParams(vmem_limit_bytes=VMEM_LIMIT),
        cost_estimate=pl.CostEstimate(flops=0, bytes_accessed=count << 20, transcendentals=0),
    )(scalars, *parts, *old)


def chunk_specs(chunks, shape):
    specs, first = [], 0
    for chunk in chunks:
        count = chunk.shape[0]
        specs.append(
            pl.BlockSpec(
                (1, *shape), lambda i, s, first=first, count=count: (jnp.clip(i - first, 0, count - 1), 0, 0)
            )
        )
        first += count
    return specs


def input_grad_kernel(sizes, n_tp, scalars, *refs):
    pairs, (wg, wu) = refs[: len(sizes)], refs[len(sizes) : len(sizes) + 2]
    outs, acc = refs[len(sizes) + 2 : -1], refs[-1]
    step = pl.program_id(0)
    width = wg.shape[-1]
    first = 0
    for pair, size in zip(pairs, sizes):

        @pl.when((step >= first) & (step < first + size))
        def _(pair=pair, first=first):
            part = dot(pair[0, :, :width], wg[0], NT) + dot(pair[0, :, width:], wu[0], NT)
            if first == 0:

                @pl.when(step == 0)
                def _():
                    acc[...] = part

                @pl.when(step > 0)
                def _():
                    acc[...] += part

            else:
                acc[...] += part

        first += size

    @pl.when(step == pl.num_programs(0) - 1)
    def _():
        rows = acc.shape[0] // n_tp
        for r in range(n_tp):
            outs[r][...] = acc[pl.ds(pl.multiple_of(scalars[r] * rows, rows), rows), :].astype(bf16)


def input_grads(scalars, pairs, wg, wu, n_tp):
    experts, features, width = wg.shape
    tokens = pairs[0].shape[1]
    rows = tokens // n_tp
    weight = pl.BlockSpec((1, features, width), lambda i, s: (i, 0, 0))
    return call(
        functools.partial(input_grad_kernel, [pair.shape[0] for pair in pairs], n_tp),
        (experts,),
        scalars,
        [*pairs, wg, wu],
        chunk_specs(pairs, (tokens, 2 * width)) + [weight] * 2,
        [struct((rows, features), bf16)] * n_tp,
        [pl.BlockSpec((rows, features), lambda i, s: (0, 0))] * n_tp,
        [pltpu.VMEM((tokens, features), f32)],
        flops=4 * experts * tokens * features * width,
        moved=experts * 3 << 20,
    )


def result_kernel(sizes, n_tp, scalars, *refs):
    hiddens, wd = refs[: len(sizes)], refs[len(sizes)]
    outs, acc = refs[len(sizes) + 1 : -1], refs[-1]
    step = pl.program_id(0)
    first = 0
    for hidden, size in zip(hiddens, sizes):

        @pl.when((step >= first) & (step < first + size))
        def _(hidden=hidden, first=first):
            part = dot(hidden[0], wd[0])
            if first == 0:

                @pl.when(step == 0)
                def _():
                    acc[...] = part

                @pl.when(step > 0)
                def _():
                    acc[...] += part

            else:
                acc[...] += part

        first += size

    @pl.when(step == pl.num_programs(0) - 1)
    def _():
        cols = acc.shape[1] // n_tp
        for r in range(n_tp):
            outs[r][...] = acc[:, pl.ds(pl.multiple_of(scalars[r] * cols, cols), cols)].astype(bf16)


def results(scalars, hiddens, wd, n_tp):
    experts, width, features = wd.shape
    tokens = hiddens[0].shape[1]
    cols = features // n_tp
    return call(
        functools.partial(result_kernel, [hidden.shape[0] for hidden in hiddens], n_tp),
        (experts,),
        scalars,
        [*hiddens, wd],
        chunk_specs(hiddens, (tokens, width)) + [pl.BlockSpec((1, width, features), lambda i, s: (i, 0, 0))],
        [struct((tokens, cols), bf16)] * n_tp,
        [pl.BlockSpec((tokens, cols), lambda i, s: (0, 0))] * n_tp,
        [pltpu.VMEM((tokens, features), f32)],
        flops=2 * experts * tokens * features * width,
        moved=experts * 2 << 20,
    )


def rows_kernel(n_tp, scalars, *refs):
    parts, dgates = refs[:n_tp], refs[n_tp : 2 * n_tp]
    probs, kept, stream, normed, factor, upstream, gain, router = refs[2 * n_tp : 2 * n_tp + 8]
    grad_out, dgain_out, drouter_out = refs[2 * n_tp + 8 :]
    total = sum(part[...].astype(f32) for part in parts)
    dprobs = sum(part[...] for part in dgates) * kept[...]
    soft = probs[...]
    dlogits = soft * (dprobs - jnp.sum(dprobs * soft, axis=1, keepdims=True))
    dlogits = dlogits.astype(bf16)
    drouter_out[...] = dot(normed[...], dlogits, TN)
    total += dot(dlogits, router[...], NT)
    scale = factor[...]
    normal = stream[...] * scale
    dgain_out[...] = jnp.sum(total * normal, axis=0, keepdims=True)
    scaled = total * gain[...]
    mean = jnp.mean(scaled * normal, axis=1, keepdims=True)
    grad_out[...] = (upstream[...].astype(f32) + scale * (scaled - normal * mean)).astype(bf16)


def stream_grad_rows(scalars, parts, dgates, probs, kept, stream, normed, factor, upstream, gain, router):
    n_tp = len(parts)
    rows, features = parts[0].shape
    experts = router.shape[1]
    mine = lambda w: pl.BlockSpec((rows, w), lambda i, s: (s[0], 0))
    plain = lambda h, w: pl.BlockSpec((h, w), lambda i, s: (0, 0))
    return call(
        functools.partial(rows_kernel, n_tp),
        (1,),
        scalars,
        [*parts, *dgates, probs, kept, stream, normed, factor, upstream, gain, router],
        [plain(rows, features)] * n_tp
        + [plain(rows, experts)] * n_tp
        + [mine(experts), mine(experts), mine(features), mine(features), mine(1), mine(features)]
        + [plain(1, features), plain(features, experts)],
        [struct((rows, features), bf16), struct((1, features), f32), struct((features, experts), f32)],
        [plain(rows, features), plain(1, features), plain(features, experts)],
        flops=1 << 24,
        moved=10 << 20,
    )


def attended_grad_kernel(n_tp, scalars, *refs):
    pieces, w_ref = refs[:n_tp], refs[n_tp]
    whole_out, grad_out = refs[n_tp + 1 :]
    rows = pieces[0].shape[0]
    for r in range(n_tp):
        place = pl.ds(pl.multiple_of(scalars[r] * rows, rows), rows)
        whole_out[place, :] = pieces[r][...]
    grad_out[...] = dot(whole_out[...], w_ref[...], NT).astype(bf16)


def attended_grad(scalars, pieces, w_output):
    n_tp = len(pieces)
    rows, features = pieces[0].shape
    local = w_output.shape[0]
    tokens = rows * n_tp
    plain = lambda h, w: pl.BlockSpec((h, w), lambda i, s: (0, 0))
    return call(
        functools.partial(attended_grad_kernel, n_tp),
        (1,),
        scalars,
        [*pieces, w_output],
        [plain(rows, features)] * n_tp + [plain(local, features)],
        [struct((tokens, features), bf16), struct((tokens, local), bf16)],
        [plain(tokens, features), plain(tokens, local)],
        flops=2 * tokens * features * local,
        moved=11 << 20,
    )


def normed_grad_kernel(scalars, dq, dk, dv, wq, wk, wv, x_ref, factor, gain, out, dot_out, dgain_out):
    total = dot(dq[...], wq[...], NT) + dot(dk[...], wk[...], NT) + dot(dv[...], wv[...], NT)
    out[...] = total.astype(bf16)
    normal = x_ref[...].astype(f32) * factor[...]
    product = total * normal
    dgain_out[...] = jnp.sum(product, axis=0, keepdims=True)
    dot_out[...] = jnp.sum(product * gain[...], axis=1, keepdims=True)


def normed_grad(scalars, r, dq, dk, dv, wq, wk, wv, x, factor, gain, n_tp):
    tokens, local = dq.shape
    features = wq.shape[0]
    width = features // n_tp
    plain = lambda h, w: pl.BlockSpec((h, w), lambda i, s: (0, 0))
    weight = pl.BlockSpec((width, local), lambda i, s: (s[r], 0))
    return call(
        normed_grad_kernel,
        (1,),
        scalars,
        [dq, dk, dv, wq, wk, wv, x, factor, gain],
        [plain(tokens, local)] * 3
        + [weight] * 3
        + [
            pl.BlockSpec((tokens, width), lambda i, s: (0, s[r])),
            plain(tokens, 1),
            pl.BlockSpec((1, width), lambda i, s: (0, s[r])),
        ],
        [struct((tokens, width), bf16), struct((tokens, 1), f32), struct((1, width), f32)],
        [plain(tokens, width), plain(tokens, 1), plain(1, width)],
        flops=6 * tokens * local * width,
        moved=7 << 20,
    )


def kept_pairs(expert_ids, experts, capacity):
    tokens = expert_ids.shape[0]
    named = jnp.any(expert_ids[:, :, None] == jnp.arange(experts, dtype=jnp.int32), axis=1)
    earlier = jnp.arange(tokens)[:, None] > jnp.arange(tokens)[None, :]
    rank = dot(earlier.astype(bf16), named.astype(bf16))
    return (named & (rank < capacity)).astype(f32)


def body(n_dp, n_tp, cosine, sine, tokens, cotangent, attn_gain, w_query, w_key, w_value, query_gain, key_gain,
         w_output, ffn_gain, w_router, w_gate, w_up, w_down, expert_ids):
    tp, dp = lax.axis_index("tensor"), lax.axis_index("dp")
    far, near = n_dp // 2, n_dp // 4
    side = (dp // near) % 2
    token_count, width = tokens.shape
    features = width * n_tp
    heads, hd = query_gain.shape
    local = heads * hd
    experts = w_router.shape[1]
    capacity = token_count * expert_ids.shape[1] // experts
    gain1, gain2 = attn_gain[None, :], ffn_gain[None, :]
    lead = 6
    shared = (experts - lead) // 2
    first_block, second_block = 2, lead - 2
    shift, other_shift = n_tp + n_dp, n_tp + n_dp + 1
    scalars = jnp.stack(
        [tp ^ r for r in range(n_tp)]
        + [dp ^ bit_reverse(place, n_dp) for place in range(n_dp)]
        + [side * shared, (1 - side) * shared]
    ).astype(jnp.int32)

    share = local // n_dp
    w_share = lax.dynamic_slice_in_dim(w_output, dp * share, share, 0)
    w_all = lax.all_gather(w_share, ("dp", "tensor")).reshape(n_dp, n_tp, share, features)

    x_pieces = gather_pieces(tokens, "tensor", n_tp)
    kept = kept_pairs(expert_ids, experts, capacity)
    x_pieces[0] = after(x_pieces[0], kept)
    x, normed1, factor1, q_raw, k_raw, q_rot, k_rot, value = project(
        scalars, x_pieces, gain1, w_query, w_key, w_value, query_gain, key_gain, cosine, sine
    )
    g_pieces = gather_pieces(after(cotangent, x_pieces[-1]), "tensor", n_tp)
    attended, totals = attend(scalars, q_rot, k_rot, value, heads)
    attended_pieces = gather_pieces(attended, "tensor", n_tp)
    g_pieces[0] = after(g_pieces[0], attended)
    upstream, g_turned = whole_grad(scalars, g_pieces, n_dp)
    stream, normed2, normed2_mine, turned, factor2, probs, gates = stream_of(
        scalars, attended_pieces, after(x, upstream), w_all, gain2, w_router, kept, n_dp
    )
    g_near = swap(after(cotangent, g_pieces[-1]), "dp", n_dp, near)
    normed_near = swap(normed2_mine, "dp", n_dp, near)
    gates_near = swap(gates, "dp", n_dp, near)
    g_near_pieces = gather_pieces(after(g_near, attended_pieces[-1]), "tensor", n_tp)
    normed_near_pieces = gather_pieces(normed_near, "tensor", n_tp)

    run = lambda normed, first, count: run_experts(
        scalars, normed, upstream, gates, w_gate, w_up, w_down, first, count
    )
    hidden0, pair0, dgate0 = run(normed2, 0, first_block)
    keep0, send0 = weight_grads(scalars, turned, g_turned, hidden0, pair0, 0, first_block, n_dp)
    hidden1, pair1, dgate1 = run(after(normed2, send0), first_block, second_block)
    arrived0 = swap(send0, "dp", n_dp, 1)
    keep0, send0 = add_halves(after(keep0, pair1), arrived0)
    keep1, send1 = weight_grads(scalars, after(turned, send0), g_turned, hidden1, pair1, 0, second_block, n_dp)
    hidden2, pair2, dgate2 = run(after(normed2, send1), lead, experts - lead)
    arrived1 = swap(send1, "dp", n_dp, 1)
    keep1, send1 = add_halves(after(keep1, pair2), arrived1)
    masks, mask = [], 2
    while mask < n_dp:
        masks.append(mask)
        mask *= 2
    last = send1
    for mask in masks[:-1]:
        arrived0 = swap(send0, "dp", n_dp, mask)
        keep0, send0 = add_halves(after(keep0, last), arrived0)
    last = send0

    hiddens, pairs = [hidden0, hidden1, hidden2], [pair0, pair1, pair2]
    dgate = dgate0 + dgate1 + dgate2
    input_parts = input_grads(scalars, [*pairs[:-1], after(pair2, last)], w_gate, w_up, n_tp)
    rows = token_count // n_tp
    dgate_rows = [lax.dynamic_slice_in_dim(dgate, (tp ^ r) * rows, rows, 0) for r in range(n_tp)]
    dgate_parts = scatter_pieces(dgate_rows, "tensor", n_tp)
    input_arrived = scatter_pieces(input_parts, "tensor", n_tp)

    g_near_pieces[0] = after(g_near_pieces[0], input_parts[0])
    upstream_near, g_turned_near = whole_grad(scalars, g_near_pieces, n_dp)
    normed_near_pieces[0] = after(normed_near_pieces[0], g_turned_near)
    normed2_near, turned_near = whole_grad(scalars, normed_near_pieces, n_dp)
    hidden_near, pair_near, _ = run_experts(
        scalars, normed2_near, upstream_near, gates_near, w_gate, w_up, w_down, lead, shared, shift
    )
    last = pair_near
    for mask in masks[:-1]:
        arrived1 = swap(send1, "dp", n_dp, mask)
        keep1, send1 = add_halves(after(keep1, last), arrived1)
        last = send1
    chunk = (shared + 1) // 2
    shares = []
    for offset in range(0, shared, chunk):
        size = min(chunk, shared - offset)
        shares.append(
            shared_grads(
                scalars, after(turned, last), turned_near, g_turned, g_turned_near, hidden2, hidden_near, pair2,
                pair_near, shift, offset, size, n_dp,
            )
        )
        last = shares[-1][1]
        if offset == 0:
            input_arrived[0] = after(input_arrived[0], last)
            dattn_rows, dgain2, drouter = stream_grad_rows(
                scalars, input_arrived, dgate_parts, probs, kept, stream, normed2, factor2, upstream, gain2, w_router
            )
            dattn_pieces = gather_pieces(dattn_rows, "tensor", n_tp)
            last = dattn_rows
            keep, send = shares[0]
            for mask in [1] + [m for m in masks if m not in (near, far)]:
                keep, send = add_halves(after(keep, last), swap(send, "dp", n_dp, mask))
                last = send
            shares[0] = keep, send
    result_parts = results(scalars, hiddens, after(w_down, last), n_tp)
    last = result_parts[0]
    keep, send = shares[1]
    for mask in [1] + [m for m in masks if m not in (near, far)]:
        keep, send = add_halves(after(keep, last), swap(send, "dp", n_dp, mask))
        last = send
    shares[1] = keep, send
    result_arrived = scatter_pieces(result_parts, "tensor", n_tp)

    dattn_pieces[0] = after(dattn_pieces[0], last)
    dattn, dattended = attended_grad(scalars, dattn_pieces, w_output)
    dq, dk, dv, dhead_gains = attend_back(
        scalars, q_rot, k_rot, value, dattended, totals, q_raw, k_raw, query_gain, key_gain, cosine, sine
    )
    slices, row_dots, dgain1 = [None] * n_tp, [None] * n_tp, [None] * n_tp
    last = dq
    for r in reversed(range(n_tp)):
        slices[r], row_dots[r], dgain1[r] = normed_grad(
            scalars, r, after(dq, last), dk, dv, w_query, w_key, w_value, x, factor1, gain1, n_tp
        )
        last = slices[r]

    def spread(value, dimension):
        return lax.psum_scatter(value.astype(bf16), "dp", scatter_dimension=dimension, tiled=True).astype(f32)

    grad_output = spread(dot(attended, after(dattn, dq), TN), 1)
    dqkv = jnp.concatenate([dq, dk, after(dv, last)], axis=1)
    grad_qkv = spread(dot(normed1, dqkv, TN), 0)

    row_dot = butterfly(sum(row_dots).reshape(8, token_count // 8), [("tensor", n_tp)])
    arrived1n = scatter_pieces(slices, "tensor", n_tp)
    dnormed1 = sum(part.astype(f32) for part in arrived1n)
    my_cols = lambda array: lax.dynamic_slice_in_dim(array, tp * width, width, 1)
    normal1 = tokens.astype(f32) * factor1
    input_grad = my_cols(dattn).astype(f32) + factor1 * (
        dnormed1 * my_cols(gain1) - normal1 * (row_dot.reshape(token_count, 1) / features)
    )
    output = my_cols(stream) + sum(part.astype(f32) for part in result_arrived)

    old = []
    arrived0 = swap(send0, "dp", n_dp, far)
    old = finish(scalars, [after(keep0, last)[0], arrived0[0]], old, 0, None, experts)
    arrived1 = swap(send1, "dp", n_dp, far)
    old = finish(scalars, [keep1[0], arrived1[0]], old, first_block, None, experts)
    offset = lead
    for keep, send in shares:
        size = keep.shape[1]
        keep, send = add_halves(keep, swap(send, "dp", n_dp, far))
        given = swap(send, "dp", n_dp, near)
        old = finish(scalars, [keep[0]], old, offset, shift, experts)
        old = finish(scalars, [given[0]], old, offset, other_shift, experts)
        offset += size
    grad_gate, grad_up, grad_down = old

    everywhere = [("dp", n_dp), ("tensor", n_tp)]
    early = jnp.concatenate([drouter.T, dgain2], axis=0)
    early = lax.psum_scatter(early, "dp", scatter_dimension=1, tiled=True)
    early = jnp.sum(lax.all_gather(early, "tensor"), axis=0)
    gain_row = jnp.zeros((1, features), f32)
    for r in range(n_tp):
        gain_row = lax.dynamic_update_slice(gain_row, dgain1[r], (0, (tp ^ r) * width))
    gain_row = butterfly(gain_row, everywhere)
    head_gains = butterfly(dhead_gains, [("dp", n_dp)])
    mine = lambda array, dimension: lax.dynamic_slice_in_dim(
        array, dp * (array.shape[dimension] // n_dp), array.shape[dimension] // n_dp, dimension
    )
    head_gains = mine(head_gains, 2)
    return (
        output.astype(bf16),
        input_grad.astype(bf16),
        mine(gain_row, 1)[0],
        grad_qkv[:, :local],
        grad_qkv[:, local : 2 * local],
        grad_qkv[:, 2 * local :],
        head_gains[:, 0],
        head_gains[:, 1],
        grad_output,
        early[experts],
        early[:experts].T,
        grad_gate,
        grad_up,
        grad_down,
    )


def solution(mesh):
    placed = (
        P("dp", "tensor"),
        P("dp", "tensor"),
        P(),
        P(None, "tensor"),
        P(None, "tensor"),
        P(None, "tensor"),
        P("tensor", None),
        P("tensor", None),
        P("tensor", None),
        P(),
        P(),
        P(None, None, "tensor"),
        P(None, None, "tensor"),
        P(None, "tensor", None),
        P("dp", None),
    )
    n_dp, n_tp = mesh.shape["dp"], mesh.shape["tensor"]

    def layer(*args):
        cosine, sine = rope_constants(LEN, args[6].shape[1])
        return body(n_dp, n_tp, jnp.asarray(cosine), jnp.asarray(sine), *args)

    return jax.shard_map(
        layer,
        mesh=mesh,
        in_specs=placed,
        out_specs=(
            P("dp", "tensor"),
            P("dp", "tensor"),
            P("dp"),
            P("dp", "tensor"),
            P("dp", "tensor"),
            P("dp", "tensor"),
            P("tensor", "dp"),
            P("tensor", "dp"),
            P("tensor", "dp"),
            P("dp"),
            P("dp", None),
            P(None, "dp", "tensor"),
            P(None, "dp", "tensor"),
            P(None, "tensor", "dp"),
        ),
        check_vma=False,
    )
```

```python
import functools
import math

import jax
import jax.numpy as jnp
import numpy as np
from jax import lax
from jax.experimental import pallas as pl
from jax.experimental.pallas import tpu as pltpu
from jax.sharding import PartitionSpec as P

LEN = 1024
EPS = 1e-05
ROPE_BASE = 10000.0
VMEM_LIMIT = 56 << 20
TB = 256
MARKS = 4
HEAVY = 10**12
f32, bf16 = jnp.float32, jnp.bfloat16
NT = (((1,), (1,)), ((), ()))
TN = (((0,), (0,)), ((), ()))
NN = (((1,), (0,)), ((), ()))


def dot(left, right, dims=NN):
    return lax.dot_general(left, right, dims, preferred_element_type=f32)


def rope_constants(length, width):
    inv_freq = (ROPE_BASE ** (-(np.arange(width // 2, dtype=np.float32) * 2.0) / width)).astype(np.float32)
    angles = np.arange(length, dtype=np.float32)[:, None] * inv_freq[None, :]
    cosine, sine = np.cos(angles).astype(np.float32), np.sin(angles).astype(np.float32)
    return np.concatenate([cosine, cosine], axis=1), np.concatenate([-sine, sine], axis=1)


def bit_reverse(value, count):
    result, bit = 0, 1
    while bit < count:
        result = result * 2 + (value & 1)
        value >>= 1
        bit *= 2
    return result


def whole_spec():
    return pl.BlockSpec(memory_space=pltpu.VMEM)


class Line:
    def __init__(self):
        self.last = []

    def tick(self, axis, count):
        self.sent = swap(self.last[0], axis, count, 1)

    def take(self):
        self.last = [*self.last, self.sent]

    def pin(self, value):
        return lax.optimization_barrier((value, *self.last))[0]


line = Line()


def call(body, grid, scalars, ins, in_specs, outs, out_specs, scratch=(), aliases=None):
    deps, n_in, n_out = line.last, len(ins), len(outs)

    def without_deps(scalars, *refs):
        ins_outs = refs[len(deps) : n_in + n_out + len(deps)]
        body(scalars, *ins_outs, *refs[n_in + n_out + len(deps) + MARKS :])

    outs, out_specs = list(outs), list(out_specs)
    any_place = pl.BlockSpec(memory_space=pl.ANY)

    result = pl.pallas_call(
        without_deps,
        out_shape=outs + [struct((8, 128), f32)] * MARKS,
        grid_spec=pltpu.PrefetchScalarGridSpec(
            num_scalar_prefetch=1,
            grid=grid,
            in_specs=[any_place] * len(deps) + list(in_specs),
            out_specs=out_specs + [any_place] * MARKS,
            scratch_shapes=list(scratch),
        ),
        input_output_aliases={1 + len(deps) + k: v for k, v in (aliases or {}).items()},
        compiler_params=pltpu.CompilerParams(vmem_limit_bytes=VMEM_LIMIT),
        cost_estimate=pl.CostEstimate(flops=HEAVY, bytes_accessed=1, transcendentals=0),
    )(scalars, *deps, *ins)
    line.last = result[len(outs) :]
    return result[: len(outs)]


def struct(shape, dtype):
    return jax.ShapeDtypeStruct(shape, dtype)


def swap(value, axis, count, mask):
    return lax.ppermute(value, axis, [(i, i ^ mask) for i in range(count)])


def gather_pieces(value, axis, count, pin=lambda v: v):
    if count == 4:
        half = value.shape[0] // 2
        one, two = swap(value, axis, count, 1), swap(value, axis, count, 2)
        one, two = pin((one, two))
        top, bottom = swap(two[:half], axis, count, 1), swap(one[half:], axis, count, 2)
        return [value, one, two, (top, bottom)]
    pieces, mask = [value], 1
    while mask < count:
        pieces = pieces + [swap(piece, axis, count, mask) for piece in pieces]
        mask *= 2
    return pieces


def direct_pieces(value, axis, count):
    return [value] + [swap(value, axis, count, r) for r in range(1, count)]


def flat(pieces):
    return [part for piece in pieces for part in (piece if isinstance(piece, tuple) else (piece,))]


def piece_specs(pieces, block, width):
    specs = []
    for piece in pieces:
        if isinstance(piece, tuple):
            count = piece[0].shape[0] // block
            specs.append(pl.BlockSpec((block, width), lambda i, s, n=count: (jnp.minimum(i, n - 1), 0)))
            specs.append(pl.BlockSpec((block, width), lambda i, s, n=count: (jnp.maximum(i - n, 0), 0)))
        else:
            specs.append(pl.BlockSpec((block, width), lambda i, s: (i, 0)))
    return specs


def read_pieces(refs, n_tp):
    values = [ref[...] for ref in refs]
    if len(refs) == n_tp:
        return values
    early = pl.program_id(0) < pl.num_programs(0) // 2
    return values[: n_tp - 1] + [jnp.where(early, values[n_tp - 1], values[n_tp])]


def trade(pieces, axis):
    return lax.all_to_all(pieces, axis, 0, 0, tiled=True)


def halves_kernel(scalars, keep, keep2, arrived, arrived2, keep_out, send_out):
    keep_out[...] = (keep[...].astype(f32) + arrived[...].astype(f32)).astype(bf16)
    send_out[...] = (keep2[...].astype(f32) + arrived2[...].astype(f32)).astype(bf16)


def add_halves(scalars, keep, arrived):
    blocks, count, rows, width = keep.shape
    half = blocks // 2
    low = pl.BlockSpec((half, 1, rows, width), lambda i, s: (0, i, 0, 0))
    high = pl.BlockSpec((half, 1, rows, width), lambda i, s: (1, i, 0, 0))
    out = struct((half, count, rows, width), bf16)
    return call(halves_kernel, (count,), scalars, [keep, keep, arrived, arrived], [low, high] * 2, [out] * 2, [low] * 2)


def sum_kernel(scalars, left, right, out):
    out[...] = left[...] + right[...]


def add_to(scalars, left, right):
    whole = pl.BlockSpec(left.shape, lambda i, s: (0, 0))
    return call(sum_kernel, (1,), scalars, [left, right], [whole] * 2, [struct(left.shape, f32)], [whole])[0]


def two_terms(value, width):
    high = value.astype(bf16)
    low = (value - high.astype(f32)).astype(bf16)
    rest = jnp.zeros((value.shape[0], width - 2 * value.shape[1]), bf16)
    return jnp.concatenate([high, low, rest], axis=1)


def transpose_blocks(scalars, first, source, target, dp_count):
    width = source.shape[1] // dp_count
    for place in range(dp_count):
        cols = pl.ds(pl.multiple_of(scalars[first + place] * width, width), width)
        target[place * width : (place + 1) * width, :] = source[:, cols].T


def project_kernel(n_tp, n_in, heads, scalars, *refs):
    pieces = read_pieces(refs[:n_in], n_tp)
    gain, wq, wk, wv, q_gain, k_gain, cosine, sine = refs[n_in : n_in + 8]
    x_out, normed_out, factor_out, q_raw, k_raw, q_rot, k_rot, v_out = refs[n_in + 8 :]
    width = pieces[0].shape[1]
    features = width * n_tp
    values = [piece.astype(f32) for piece in pieces]
    squares = sum(jnp.sum(value * value, axis=1, keepdims=True) for value in values)
    factor = lax.rsqrt(squares / features + EPS)
    factor_out[...] = factor
    for r in range(n_tp):
        cols = pl.ds(pl.multiple_of(scalars[r] * width, width), width)
        x_out[:, cols] = pieces[r]
        normed_out[:, cols] = (values[r] * factor * gain[:, cols]).astype(bf16)
    normed = normed_out[...]
    cos, sin = cosine[...], sine[...]
    hd = cos.shape[1]
    for weight, head_gain, raw, rotated in ((wq, q_gain, q_raw, q_rot), (wk, k_gain, k_raw, k_rot)):
        product = dot(normed, weight[...])
        raw[...] = product
        for h in range(heads):
            part = product[:, h * hd : (h + 1) * hd]
            scale = lax.rsqrt(jnp.mean(part * part, axis=1, keepdims=True) + EPS)
            part = part * scale * head_gain[h : h + 1, :]
            part = part * cos + pltpu.roll(part, hd // 2, 1) * sin
            rotated[:, h * hd : (h + 1) * hd] = part.astype(bf16)
    v_out[...] = dot(normed, wv[...]).astype(bf16)


def project(scalars, pieces, gain, wq, wk, wv, q_gain, k_gain, cosine, sine):
    n_tp = len(pieces)
    tokens, width = pieces[0].shape
    features = width * n_tp
    heads, hd = q_gain.shape
    local = heads * hd
    rows = lambda w: pl.BlockSpec((TB, w), lambda i, s: (i, 0))
    return call(
        functools.partial(project_kernel, n_tp, len(flat(pieces)), heads),
        (tokens // TB,),
        scalars,
        [*flat(pieces), gain, wq, wk, wv, q_gain, k_gain, cosine, sine],
        piece_specs(pieces, TB, width) + [whole_spec()] * 6 + [rows(hd)] * 2,
        [
            struct((tokens, features), bf16),
            struct((tokens, features), bf16),
            struct((tokens, 1), f32),
            struct((tokens, local), f32),
            struct((tokens, local), f32),
            struct((tokens, local), bf16),
            struct((tokens, local), bf16),
            struct((tokens, local), bf16),
        ],
        [rows(features), rows(features), rows(1)] + [rows(local)] * 5,
    )


def attend_kernel(block, scalars, q_ref, k_ref, v_ref, out_ref, total_ref):
    tokens, hd = q_ref.shape
    scale = 1.0 / math.sqrt(hd)
    for i in range(tokens // block):
        rows = slice(i * block, (i + 1) * block)
        reach = (i + 1) * block
        scores = dot(q_ref[rows, :], k_ref[:reach, :], NT) * scale
        at_row = i * block + lax.broadcasted_iota(jnp.int32, scores.shape, 0)
        at_col = lax.broadcasted_iota(jnp.int32, scores.shape, 1)
        scores = jnp.where(at_row >= at_col, scores, -1e30)
        top = jnp.max(scores, axis=1, keepdims=True)
        weights = jnp.exp(scores - top)
        total = jnp.sum(weights, axis=1, keepdims=True)
        probs = (weights * (1.0 / total)).astype(bf16)
        out_ref[rows, :] = dot(probs, v_ref[:reach, :]).astype(bf16)
        total_ref[0, rows, :] = top + jnp.log(total)


def attend(scalars, q_rot, k_rot, value, heads):
    tokens, local = q_rot.shape
    hd = local // heads
    column = pl.BlockSpec((tokens, hd), lambda h, s: (0, h))
    return call(
        functools.partial(attend_kernel, min(256, tokens)),
        (heads,),
        scalars,
        [q_rot, k_rot, value],
        [column] * 3,
        [struct((tokens, local), bf16), struct((heads, tokens, 1), f32)],
        [column, pl.BlockSpec((1, tokens, 1), lambda h, s: (h, 0, 0))],
    )


def attend_back_kernel(block, scalars, *refs):
    (q_ref, k_ref, v_ref, go_ref, total_ref, q_raw, k_raw, q_gain, k_gain, cosine, sine) = refs[:11]
    grads_out, dgain_out, dq_acc, dk_acc, dv_acc = refs[11:]
    tokens, hd = q_ref.shape
    scale = 1.0 / math.sqrt(hd)
    count = tokens // block
    for i in reversed(range(count)):
        rows = slice(i * block, (i + 1) * block)
        reach = (i + 1) * block
        query, grad = q_ref[rows, :], go_ref[rows, :]
        scores = dot(query, k_ref[:reach, :], NT) * scale
        at_row = i * block + lax.broadcasted_iota(jnp.int32, scores.shape, 0)
        at_col = lax.broadcasted_iota(jnp.int32, scores.shape, 1)
        scores = jnp.where(at_row >= at_col, scores, -1e30)
        probs = jnp.exp(scores - total_ref[0, rows, :])
        dprobs = dot(grad, v_ref[:reach, :], NT)
        delta = jnp.sum(dprobs * probs, axis=1, keepdims=True)
        dscores = (probs * (dprobs - delta)).astype(bf16)
        dq_acc[rows, :] = dot(dscores, k_ref[:reach, :]) * scale
        dk = dot(dscores, query, TN) * scale
        dv = dot(probs.astype(bf16), grad, TN)
        if i == count - 1:
            dk_acc[...] = dk
            dv_acc[...] = dv
        else:
            dk_acc[:reach, :] += dk
            dv_acc[:reach, :] += dv
    grads_out[2] = dv_acc[...].astype(bf16)
    cos, sin = cosine[...], sine[...]
    dgains = []
    for j, acc, raw_ref, gain_ref in ((0, dq_acc, q_raw, q_gain), (1, dk_acc, k_raw, k_gain)):
        grad = acc[...]
        grad = grad * cos - pltpu.roll(grad, hd // 2, 1) * sin
        raw = raw_ref[...]
        factor = lax.rsqrt(jnp.mean(raw * raw, axis=1, keepdims=True) + EPS)
        normal = raw * factor
        dgains.append(jnp.sum(grad * normal, axis=0, keepdims=True))
        scaled = grad * gain_ref[0]
        mean = jnp.mean(scaled * normal, axis=1, keepdims=True)
        grads_out[j] = (factor * (scaled - normal * mean)).astype(bf16)
    dgain_out[0] = jnp.concatenate(dgains, axis=0)


def attend_back(scalars, q_rot, k_rot, value, grad, totals, q_raw, k_raw, q_gain, k_gain, cosine, sine):
    tokens, local = q_rot.shape
    heads, hd = q_gain.shape
    column = pl.BlockSpec((tokens, hd), lambda h, s: (0, h))
    gain_spec = pl.BlockSpec((1, 1, hd), lambda h, s: (h, 0, 0))
    table = pl.BlockSpec((tokens, hd), lambda h, s: (0, 0))
    return call(
        functools.partial(attend_back_kernel, min(256, tokens)),
        (heads,),
        scalars,
        [q_rot, k_rot, value, grad, totals, q_raw, k_raw, q_gain[:, None, :], k_gain[:, None, :], cosine, sine],
        [column] * 4
        + [pl.BlockSpec((1, tokens, 1), lambda h, s: (h, 0, 0))]
        + [column] * 2
        + [gain_spec] * 2
        + [table] * 2,
        [struct((3, tokens, local), bf16), struct((heads, 2, hd), f32)],
        [
            pl.BlockSpec((3, tokens, hd), lambda h, s: (0, 0, h)),
            pl.BlockSpec((1, 2, hd), lambda h, s: (h, 0, 0)),
        ],
        [pltpu.VMEM((tokens, hd), f32)] * 3,
    )


def whole_grad_kernel(n_tp, n_in, dp_count, scalars, *refs):
    pieces = read_pieces(refs[:n_in], n_tp)
    whole_out, turned_out = refs[n_in:]
    width = pieces[0].shape[1]
    for r in range(n_tp):
        cols = pl.ds(pl.multiple_of(scalars[r] * width, width), width)
        whole_out[:, cols] = pieces[r]
    transpose_blocks(scalars, n_tp, whole_out, turned_out, dp_count)


def whole_grad(scalars, pieces, dp_count):
    n_tp = len(pieces)
    tokens, width = pieces[0].shape
    features = width * n_tp
    return call(
        functools.partial(whole_grad_kernel, n_tp, len(flat(pieces)), dp_count),
        (tokens // TB,),
        scalars,
        flat(pieces),
        piece_specs(pieces, TB, width),
        [struct((tokens, features), bf16), struct((features, tokens), bf16)],
        [
            pl.BlockSpec((TB, features), lambda i, s: (i, 0)),
            pl.BlockSpec((features, TB), lambda i, s: (0, i)),
        ],
    )


def stream_kernel(n_tp, n_in, dp_count, scalars, *refs):
    pieces = read_pieces(refs[:n_in], n_tp)
    x_ref, w_ref, gain, router, kept = refs[n_in : n_in + 5]
    stream_out, normed_out, mine_out, turned_out, factor_out, probs_out, gates_out = refs[n_in + 5 :]
    width = pieces[0].shape[1]
    total = x_ref[...].astype(f32)
    for r in range(n_tp):
        weight = w_ref[:, pl.ds(scalars[r], 1)]
        total += dot(pieces[r], weight.reshape(width, weight.shape[-1]))
    stream_out[...] = total
    factor = lax.rsqrt(jnp.mean(total * total, axis=1, keepdims=True) + EPS)
    factor_out[...] = factor
    normed = (total * factor * gain[...]).astype(bf16)
    normed_out[...] = normed
    mine_out[:, :width] = normed_out[:, pl.ds(pl.multiple_of(scalars[0] * width, width), width)]
    logits = dot(normed, router[...])
    power = jnp.exp(logits - jnp.max(logits, axis=1, keepdims=True))
    probs = power / jnp.sum(power, axis=1, keepdims=True)
    probs_out[...] = probs
    gates = probs * kept[...]
    gates_out[...] = gates
    mine_out[:, width:] = two_terms(gates, mine_out.shape[1] - width)
    transpose_blocks(scalars, n_tp, normed_out, turned_out, dp_count)


def stream_of(scalars, pieces, x, w_all, gain, router, kept, dp_count):
    n_tp = len(pieces)
    tokens, features = x.shape
    experts = router.shape[1]
    rows = lambda w: pl.BlockSpec((TB, w), lambda i, s: (i, 0))
    return call(
        functools.partial(stream_kernel, n_tp, len(flat(pieces)), dp_count),
        (tokens // TB,),
        scalars,
        [*flat(pieces), x, w_all, gain, router, kept],
        piece_specs(pieces, TB, pieces[0].shape[1]) + [rows(features)] + [whole_spec()] * 3 + [rows(experts)],
        [
            struct((tokens, features), f32),
            struct((tokens, features), bf16),
            struct((tokens, features // n_tp + 128), bf16),
            struct((features, tokens), bf16),
            struct((tokens, 1), f32),
            struct((tokens, experts), f32),
            struct((tokens, experts), f32),
        ],
        [
            rows(features),
            rows(features),
            rows(features // n_tp + 128),
            pl.BlockSpec((features, TB), lambda i, s: (0, i)),
            rows(1),
            rows(experts),
            rows(experts),
        ],
    )


def expert_kernel(first, shift, scalars, n_ref, g_ref, gates_ref, wg, wu, wd, hidden_out, pair_out, dgate_out):
    step = pl.program_id(0)
    expert = first + step + (0 if shift is None else scalars[shift])
    width = wg.shape[-1]

    @pl.when(step == 0)
    def _():
        dgate_out[...] = jnp.zeros_like(dgate_out)

    gate_val, up_val = dot(n_ref[...], wg[0]), dot(n_ref[...], wu[0])
    back = dot(g_ref[...], wd[0], NT)
    gates = gates_ref[...]
    here = lax.broadcasted_iota(jnp.int32, gates.shape, 1) == expert
    gate = jnp.sum(jnp.where(here, gates, 0.0), axis=1, keepdims=True)
    sigmoid = 1.0 / (1.0 + jnp.exp(-gate_val))
    swish = gate_val * sigmoid
    hidden = (swish * up_val).astype(bf16).astype(f32)
    hidden_out[0] = (hidden * gate).astype(bf16)
    dgate = jnp.sum(back * hidden, axis=1, keepdims=True)
    dgate_out[...] = jnp.where(here, dgate, dgate_out[...])
    dhidden = back * gate
    pair_out[0, :, :width] = (dhidden * up_val * sigmoid * (1.0 + gate_val * (1.0 - sigmoid))).astype(bf16)
    pair_out[0, :, width:] = (dhidden * swish).astype(bf16)


def run_experts(scalars, normed, grad, gates, wg, wu, wd, first, count, shift=None):
    tokens, features = normed.shape
    experts, _, width = wg.shape
    place = lambda i, s: first + i + (0 if shift is None else s[shift])
    weight = lambda shape: pl.BlockSpec((1, *shape), lambda i, s: (place(i, s), 0, 0))
    given = lambda shape: pl.BlockSpec((1, *shape), lambda i, s: (i, 0, 0))
    return call(
        functools.partial(expert_kernel, first, shift),
        (count,),
        scalars,
        [normed, grad, gates, wg, wu, wd],
        [whole_spec()] * 3 + [weight((features, width))] * 2 + [weight((width, features))],
        [
            struct((count, tokens, width), bf16),
            struct((count, tokens, 2 * width), bf16),
            struct((tokens, experts), f32),
        ],
        [
            given((tokens, width)),
            given((tokens, 2 * width)),
            pl.BlockSpec((tokens, experts), lambda i, s: (0, 0)),
        ],
    )


def weight_grads_kernel(scalars, turned, g_turned, hidden, pair, keep_out, send_out):
    half, _, rows, _ = keep_out.shape
    width = hidden.shape[-1]
    first = dot(turned[...], pair[0]).astype(bf16).reshape(2 * half, rows, 2 * width)
    keep_out[:, 0, :, : 2 * width] = first[:half]
    send_out[:, 0, :, : 2 * width] = first[half:]
    second = dot(g_turned[...], hidden[0]).astype(bf16).reshape(2 * half, rows, width)
    keep_out[:, 0, :, 2 * width :] = second[:half]
    send_out[:, 0, :, 2 * width :] = second[half:]


def weight_grads(scalars, turned, g_turned, hidden, pair, offset, count, dp_count):
    features, tokens = turned.shape
    width = hidden.shape[-1]
    half, rows = dp_count // 2, features // dp_count
    out = struct((half, count, rows, 3 * width), bf16)
    out_spec = pl.BlockSpec((half, 1, rows, 3 * width), lambda i, s: (0, i, 0, 0))
    return call(
        weight_grads_kernel,
        (count,),
        scalars,
        [turned, g_turned, hidden, pair],
        [
            whole_spec(),
            whole_spec(),
            pl.BlockSpec((1, tokens, width), lambda i, s: (offset + i, 0, 0)),
            pl.BlockSpec((1, tokens, 2 * width), lambda i, s: (offset + i, 0, 0)),
        ],
        [out, out],
        [out_spec, out_spec],
    )


def inner_swap(index):
    return (index & ~3) | ((index & 1) << 1) | ((index >> 1) & 1)


def shared_grads_kernel(shift, scalars, *refs):
    turned, turned2, g_turned, g_turned2, hidden_a, hidden_b, hidden2, pair_a, pair_b, pair2 = refs[:10]
    keep_out, send_out = refs[10:]
    here = scalars[shift] == 0
    hidden = jnp.where(here, hidden_a[0], hidden_b[0])
    pair = jnp.where(here, pair_a[0], pair_b[0])
    half, _, rows, _ = keep_out.shape
    width = hidden.shape[-1]
    first = dot(turned[...], pair) + dot(turned2[...], pair2[0])
    first = first.astype(bf16).reshape(2 * half, rows, 2 * width)
    second = dot(g_turned[...], hidden) + dot(g_turned2[...], hidden2[0])
    second = second.astype(bf16).reshape(2 * half, rows, width)
    for out, base in ((keep_out, 0), (send_out, half)):
        for place in range(half):
            out[inner_swap(place), 0, :, : 2 * width] = first[base + place]
            out[inner_swap(place), 0, :, 2 * width :] = second[base + place]


def shared_grads(scalars, turned, turned2, g_turned, g_turned2, hidden, hidden2, pair, pair2, shift, offset, count,
                 dp_count):
    features, tokens = turned.shape
    width = hidden2.shape[-1]
    half, rows = dp_count // 2, features // dp_count
    out = struct((half, count, rows, 3 * width), bf16)
    out_spec = pl.BlockSpec((half, 1, rows, 3 * width), lambda i, s: (0, i, 0, 0))
    block = lambda w: pl.BlockSpec((1, tokens, w), lambda i, s: (offset + i, 0, 0))
    return call(
        functools.partial(shared_grads_kernel, shift),
        (count,),
        scalars,
        [turned, turned2, g_turned, g_turned2, *hidden, hidden2, *pair, pair2],
        [whole_spec()] * 4 + [block(width)] * 3 + [block(2 * width)] * 3,
        [out, out],
        [out_spec, out_spec],
    )


def finish_kernel(n_parts, n_old, scalars, *refs):
    parts = refs[:n_parts]
    gate_out, up_out, down_out = refs[n_parts + n_old :]
    width = gate_out.shape[-1]
    total = sum(part[0].astype(f32) for part in parts)
    gate_out[0] = total[:, :width]
    up_out[0] = total[:, width : 2 * width]
    down_out[0] = total[:, 2 * width :].T


def finish(scalars, parts, old, first, shift, experts):
    count, rows, wide = parts[0].shape
    width = wide // 3
    place = lambda i, s: (first + i + (0 if shift is None else s[shift]), 0, 0)
    spec = pl.BlockSpec((1, rows, width), place)
    down_spec = pl.BlockSpec((1, width, rows), place)
    return call(
        functools.partial(finish_kernel, len(parts), len(old)),
        (count,),
        scalars,
        [*parts, *old],
        [pl.BlockSpec((1, rows, wide), lambda i, s: (i, 0, 0))] * len(parts)
        + [pl.BlockSpec(memory_space=pl.ANY)] * len(old),
        [struct((experts, rows, width), f32)] * 2 + [struct((experts, width, rows), f32)],
        [spec, spec, down_spec],
        aliases={len(parts) + k: k for k in range(len(old))},
    )


def chunk_specs(chunks, shape):
    specs, first = [], 0
    for chunk in chunks:
        count = chunk.shape[0]
        specs.append(
            pl.BlockSpec(
                (1, *shape), lambda i, s, first=first, count=count: (jnp.clip(i - first, 0, count - 1), 0, 0)
            )
        )
        first += count
    return specs


def input_grad_kernel(sizes, n_tp, scalars, *refs):
    n = len(sizes)
    pairs, (wg, wu), dgates = refs[:n], refs[n : n + 2], refs[n + 2 : 2 * n + 2]
    out, acc = refs[-2:]
    step = pl.program_id(0)
    width = wg.shape[-1]
    first = 0
    for pair, size in zip(pairs, sizes):

        @pl.when((step >= first) & (step < first + size))
        def _(pair=pair, first=first):
            part = dot(pair[0, :, :width], wg[0], NT) + dot(pair[0, :, width:], wu[0], NT)
            if first == 0:

                @pl.when(step == 0)
                def _():
                    acc[...] = part

                @pl.when(step > 0)
                def _():
                    acc[...] += part

            else:
                acc[...] += part

        first += size

    @pl.when(step == pl.num_programs(0) - 1)
    def _():
        rows, features = acc.shape[0] // n_tp, acc.shape[1]
        for k in range(n_tp):
            place = slice(k * rows, (k + 1) * rows)
            out[k, :, :features] = acc[place, :].astype(bf16)
            dgate = sum(ref[place, :] for ref in dgates)
            out[k, :, features:] = two_terms(dgate, out.shape[2] - features)


def input_grads(scalars, pairs, wg, wu, dgates, n_tp):
    experts, features, width = wg.shape
    tokens = pairs[0].shape[1]
    rows = tokens // n_tp
    weight = pl.BlockSpec((1, features, width), lambda i, s: (i, 0, 0))
    return call(
        functools.partial(input_grad_kernel, [pair.shape[0] for pair in pairs], n_tp),
        (experts,),
        scalars,
        [*pairs, wg, wu, *dgates],
        chunk_specs(pairs, (tokens, 2 * width)) + [weight] * 2 + [whole_spec()] * len(dgates),
        [struct((n_tp, rows, features + 128), bf16)],
        [pl.BlockSpec((n_tp, rows, features + 128), lambda i, s: (0, 0, 0))],
        [pltpu.VMEM((tokens, features), f32)],
    )


def result_kernel(sizes, n_tp, scalars, *refs):
    hiddens, wd = refs[: len(sizes)], refs[len(sizes)]
    out, acc = refs[-2:]
    step = pl.program_id(0)
    first = 0
    for hidden, size in zip(hiddens, sizes):

        @pl.when((step >= first) & (step < first + size))
        def _(hidden=hidden, first=first):
            part = dot(hidden[0], wd[0])
            if first == 0:

                @pl.when(step == 0)
                def _():
                    acc[...] = part

                @pl.when(step > 0)
                def _():
                    acc[...] += part

            else:
                acc[...] += part

        first += size

    @pl.when(step == pl.num_programs(0) - 1)
    def _():
        cols = acc.shape[1] // n_tp
        for k in range(n_tp):
            out[k] = acc[:, k * cols : (k + 1) * cols].astype(bf16)


def results(scalars, hiddens, wd, n_tp):
    experts, width, features = wd.shape
    tokens = hiddens[0].shape[1]
    cols = features // n_tp
    return call(
        functools.partial(result_kernel, [hidden.shape[0] for hidden in hiddens], n_tp),
        (experts,),
        scalars,
        [*hiddens, wd],
        chunk_specs(hiddens, (tokens, width)) + [pl.BlockSpec((1, width, features), lambda i, s: (i, 0, 0))],
        [struct((n_tp, tokens, cols), bf16)],
        [pl.BlockSpec((n_tp, tokens, cols), lambda i, s: (0, 0, 0))],
        [pltpu.VMEM((tokens, features), f32)],
    )


def rows_kernel(n_tp, scalars, *refs):
    parts, probs, kept, stream, normed, factor, upstream, gain, router = refs[:9]
    grad_out, dgain_out, drouter_out = refs[9:]
    features, experts = router.shape
    total = sum(parts[k, :, :features].astype(f32) for k in range(n_tp))
    both = sum(parts[k, :, features:].astype(f32) for k in range(n_tp))
    dprobs = (both[:, :experts] + both[:, experts : 2 * experts]) * kept[...]
    soft = probs[...]
    dlogits = soft * (dprobs - jnp.sum(dprobs * soft, axis=1, keepdims=True))
    dlogits = dlogits.astype(bf16)
    drouter_out[...] = dot(normed[...], dlogits, TN)
    total += dot(dlogits, router[...], NT)
    scale = factor[...]
    normal = stream[...] * scale
    dgain_out[...] = jnp.sum(total * normal, axis=0, keepdims=True)
    scaled = total * gain[...]
    mean = jnp.mean(scaled * normal, axis=1, keepdims=True)
    grad_out[...] = (upstream[...].astype(f32) + scale * (scaled - normal * mean)).astype(bf16)


def stream_grad_rows(scalars, parts, probs, kept, stream, normed, factor, upstream, gain, router):
    n_tp, rows, _ = parts.shape
    features, experts = router.shape
    mine = lambda w: pl.BlockSpec((rows, w), lambda i, s: (s[0], 0))
    plain = lambda h, w: pl.BlockSpec((h, w), lambda i, s: (0, 0))
    return call(
        functools.partial(rows_kernel, n_tp),
        (1,),
        scalars,
        [parts, probs, kept, stream, normed, factor, upstream, gain, router],
        [pl.BlockSpec(parts.shape, lambda i, s: (0, 0, 0))]
        + [mine(experts), mine(experts), mine(features), mine(features), mine(1), mine(features)]
        + [plain(1, features), plain(features, experts)],
        [struct((rows, features), bf16), struct((1, features), f32), struct((features, experts), f32)],
        [plain(rows, features), plain(1, features), plain(features, experts)],
    )


def attended_grad_kernel(scalars, grad, w_ref, out):
    out[...] = dot(grad[...], w_ref[...], NT).astype(bf16)


def attended_grad(scalars, grad, w_output):
    tokens, features = grad.shape
    local = w_output.shape[0]
    rows = lambda w: pl.BlockSpec((tokens // 2, w), lambda i, s: (i, 0))
    return call(
        attended_grad_kernel,
        (2,),
        scalars,
        [grad, w_output],
        [rows(features), whole_spec()],
        [struct((tokens, local), bf16)],
        [rows(local)],
    )[0]


def normed_grad_kernel(scalars, grads, wq, wk, wv, x_ref, factor, gain, out, dot_out, dgain_out):
    total = sum(dot(grads[j], weight[...], NT) for j, weight in enumerate((wq, wk, wv)))
    out[0] = total.astype(bf16)
    normal = x_ref[...].astype(f32) * factor[...]
    product = total * normal
    dgain_out[...] = jnp.sum(product, axis=0, keepdims=True)
    part = jnp.sum(product * gain[...], axis=1, keepdims=True)

    @pl.when(pl.program_id(0) == 0)
    def _():
        dot_out[...] = part

    @pl.when(pl.program_id(0) > 0)
    def _():
        dot_out[...] += part


def normed_grad(scalars, grads, wq, wk, wv, x, factor, gain, n_tp):
    _, tokens, local = grads.shape
    features = wq.shape[0]
    width = features // n_tp
    weight = pl.BlockSpec((width, local), lambda i, s: (i, 0))
    column = lambda h: pl.BlockSpec((h, width), lambda i, s: (0, i))
    whole = pl.BlockSpec((tokens, 1), lambda i, s: (0, 0))
    return call(
        normed_grad_kernel,
        (n_tp,),
        scalars,
        [grads, wq, wk, wv, x, factor, gain],
        [pl.BlockSpec(grads.shape, lambda i, s: (0, 0, 0))] + [weight] * 3 + [column(tokens), whole, column(1)],
        [struct((n_tp, tokens, width), bf16), struct((tokens, 1), f32), struct((1, features), f32)],
        [pl.BlockSpec((1, tokens, width), lambda i, s: (i, 0, 0)), whole, column(1)],
    )


def turn_kernel(first, dp_count, scalars, source, target):
    transpose_blocks(scalars, first, source, target, dp_count)


def turn(scalars, value, n_tp, dp_count):
    tokens, features = value.shape
    return call(
        functools.partial(turn_kernel, n_tp, dp_count),
        (tokens // TB,),
        scalars,
        [value],
        [pl.BlockSpec((TB, features), lambda i, s: (i, 0))],
        [struct((features, tokens), bf16)],
        [pl.BlockSpec((features, TB), lambda i, s: (0, i))],
    )[0]


def output_kernel(scalars, stream, parts, out):
    out[...] = (stream[...] + sum(parts[k].astype(f32) for k in range(parts.shape[0]))).astype(bf16)


def output_of(scalars, stream, parts):
    n_tp, tokens, width = parts.shape
    return call(
        output_kernel,
        (tokens // TB,),
        scalars,
        [stream, parts],
        [
            pl.BlockSpec((TB, width), lambda i, s: (i, s[0])),
            pl.BlockSpec((n_tp, TB, width), lambda i, s: (0, i, 0)),
        ],
        [struct((tokens, width), bf16)],
        [pl.BlockSpec((TB, width), lambda i, s: (i, 0))],
    )[0]


def final_kernel(features, scalars, dattn, x_ref, factor, row_dot, gain, parts, out):
    total = sum(parts[k].astype(f32) for k in range(parts.shape[0]))
    scale = factor[...]
    normal = x_ref[...].astype(f32) * scale
    back = scale * (total * gain[...] - normal * (row_dot[...] / features))
    out[...] = (dattn[...].astype(f32) + back).astype(bf16)


def final_grad(scalars, dattn, x, factor, row_dot, gain, parts):
    n_tp, tokens, width = parts.shape
    plain = lambda w: pl.BlockSpec((TB, w), lambda i, s: (i, 0))
    mine = pl.BlockSpec((TB, width), lambda i, s: (i, s[0]))
    return call(
        functools.partial(final_kernel, dattn.shape[1]),
        (tokens // TB,),
        scalars,
        [dattn, x, factor, row_dot, gain, parts],
        [mine, mine, plain(1), plain(1), pl.BlockSpec((1, width), lambda i, s: (0, s[0]))]
        + [pl.BlockSpec((n_tp, TB, width), lambda i, s: (0, i, 0))],
        [struct((tokens, width), bf16)],
        [plain(width)],
    )[0]


def kept_pairs(expert_ids, experts, capacity):
    tokens = expert_ids.shape[0]
    named = jnp.any(expert_ids[:, :, None] == jnp.arange(experts, dtype=jnp.int32), axis=1)
    earlier = jnp.arange(tokens)[:, None] > jnp.arange(tokens)[None, :]
    rank = dot(earlier.astype(bf16), named.astype(bf16))
    return (named & (rank < capacity)).astype(f32)


def body(n_dp, n_tp, cosine, sine, tokens, cotangent, attn_gain, w_query, w_key, w_value, query_gain, key_gain,
         w_output, ffn_gain, w_router, w_gate, w_up, w_down, expert_ids):
    tp, dp = lax.axis_index("tensor"), lax.axis_index("dp")
    far, near = n_dp // 2, n_dp // 4
    side = (dp // near) % 2
    token_count, width = tokens.shape
    features = width * n_tp
    heads, hd = query_gain.shape
    local = heads * hd
    experts = w_router.shape[1]
    capacity = token_count * expert_ids.shape[1] // experts
    gain1, gain2 = attn_gain[None, :], ffn_gain[None, :]
    blocks = (2, 3, 3)
    lead = sum(blocks)
    shared = (experts - lead) // 2
    shift, other_shift = n_tp + n_dp, n_tp + n_dp + 1
    scalars = jnp.stack(
        [tp ^ r for r in range(n_tp)]
        + [dp ^ bit_reverse(place, n_dp) for place in range(n_dp)]
        + [side * shared, (1 - side) * shared]
    ).astype(jnp.int32)

    line.last = []

    share = local // n_dp
    w_share = lax.dynamic_slice_in_dim(w_output, dp * share, share, 0)
    w_all = lax.all_gather(w_share, ("dp", "tensor")).reshape(n_dp, n_tp, share, features)

    x_pieces = gather_pieces(tokens, "tensor", n_tp)
    kept = kept_pairs(expert_ids, experts, capacity)
    x_pieces, g_mine, kept = lax.optimization_barrier((x_pieces, cotangent, kept))
    g_near = swap(g_mine, "dp", n_dp, near)
    g_pieces = [g_mine, swap(g_mine, "tensor", n_tp, 1), swap(g_mine, "tensor", n_tp, 2)]
    x, normed1, factor1, q_raw, k_raw, q_rot, k_rot, value = project(
        scalars, x_pieces, gain1, w_query, w_key, w_value, query_gain, key_gain, cosine, sine
    )
    attended, totals = attend(scalars, q_rot, k_rot, value, heads)
    attended, g_pieces = lax.optimization_barrier((attended, g_pieces))
    attended_pieces = gather_pieces(attended, "tensor", n_tp)
    attended_pieces, g_pieces, g_near = lax.optimization_barrier((attended_pieces, g_pieces, g_near))
    if n_tp == 4:
        half = token_count // 2
        one, two = g_pieces[1], g_pieces[2]
        g_pieces.append((swap(two[:half], "tensor", n_tp, 1), swap(one[half:], "tensor", n_tp, 2)))
    else:
        g_pieces = direct_pieces(g_pieces[0], "tensor", n_tp)
    stream, normed2, normed2_mine, turned, factor2, probs, gates = stream_of(
        scalars, attended_pieces, x, w_all, gain2, w_router, kept, n_dp
    )
    upstream, g_turned = whole_grad(scalars, g_pieces, n_dp)
    normed_near = swap(normed2_mine, "dp", n_dp, near)
    g_near, _ = lax.optimization_barrier((g_near, upstream))
    upstream_near = lax.all_gather(g_near, "tensor", axis=1, tiled=True)
    gates_near = normed_near[:, width : width + experts].astype(f32)
    gates_near += normed_near[:, width + experts : width + 2 * experts].astype(f32)
    normed2_near = lax.all_gather(normed_near[:, :width], "tensor", axis=1, tiled=True)

    hiddens, pairs, dgates = [], [], []

    def run(first, count):
        out = run_experts(scalars, normed2, upstream, gates, w_gate, w_up, w_down, first, count)
        for kind, array in zip((hiddens, pairs, dgates), out):
            kind.append(array)

    def sum_step(keep, send, mask):
        arrived = swap(send, "dp", n_dp, mask)
        return lambda: add_halves(scalars, keep, arrived)

    lower = [mask for mask in (2, 4, 8, 16) if mask < far]

    def own_sums(index):
        first, count = sum(blocks[:index]), blocks[index]
        keep, send = weight_grads(scalars, turned, g_turned, hiddens[index], pairs[index], 0, count, n_dp)
        return sum_step(keep, send, 1)

    def last_step(take):
        keep, send = take()
        for mask in lower[1:]:
            keep, send = sum_step(keep, send, mask)()
        return [keep[0], swap(send, "dp", n_dp, far)[0]]

    run(0, blocks[0])
    take0 = own_sums(0)
    run(blocks[0], blocks[1])
    take0 = sum_step(*take0(), lower[0])
    take1 = own_sums(1)
    run(blocks[0] + blocks[1], blocks[2])
    parts0 = last_step(take0)
    take1 = sum_step(*take1(), lower[0])
    take2 = own_sums(2)
    run(lead, shared)
    take2 = sum_step(*take2(), lower[0])
    parts1 = last_step(take1)
    line.tick("dp", n_dp)
    run(lead + shared, shared)
    old = finish(scalars, parts0, [], 0, None, experts)
    line.take()
    input_parts = input_grads(scalars, pairs, w_gate, w_up, dgates, n_tp)[0]
    input_arrived = trade(input_parts, "tensor")
    parts2 = last_step(take2)
    g_turned_near = turn(scalars, upstream_near, n_tp, n_dp)
    turned_near = turn(scalars, normed2_near, n_tp, n_dp)
    old = finish(scalars, parts1, old, blocks[0], None, experts)
    hidden_near, pair_near, _ = run_experts(
        scalars, normed2_near, upstream_near, gates_near, w_gate, w_up, w_down, lead, shared, shift
    )

    def shared_sums(offset, size):
        keep, send = shared_grads(
            scalars, turned, turned_near, g_turned, g_turned_near, hiddens[3:], hidden_near, pairs[3:], pair_near,
            shift, offset, size, n_dp,
        )
        return sum_step(keep, send, 1)

    def shared_next(take):
        keep, send = take()
        for mask in lower:
            if mask != near:
                keep, send = sum_step(keep, send, mask)()
        return sum_step(keep, send, far)

    first_share = (shared + 1) // 2
    take3 = shared_sums(0, first_share)
    dattn_rows, dgain2, drouter = stream_grad_rows(
        scalars, input_arrived, probs, kept, stream, normed2, factor2, upstream, gain2, w_router
    )
    dattn = lax.all_gather(dattn_rows, "tensor", axis=0, tiled=True)
    take3 = shared_next(take3)
    line.tick("dp", n_dp)
    old = finish(scalars, parts2, old, blocks[0] + blocks[1], None, experts)
    line.take()
    take4 = shared_sums(first_share, shared - first_share)
    result_arrived = trade(results(scalars, hiddens, w_down, n_tp)[0], "tensor")
    take4 = shared_next(take4)

    def spread(value, dimension):
        value = value.astype(bf16)
        line.last = [value]
        return lax.psum_scatter(value, "dp", scatter_dimension=dimension, tiled=True).astype(f32)

    dattended = attended_grad(scalars, dattn, w_output)
    grad_output = spread(dot(attended, line.pin(dattn), TN), 1)
    grads, dhead_gains = attend_back(
        scalars, q_rot, k_rot, value, dattended, totals, q_raw, k_raw, query_gain, key_gain, cosine, sine
    )
    keep3, send3 = take3()
    given3 = swap(send3, "dp", n_dp, near)
    grad_qkv = spread(jnp.einsum("td,jtc->jdc", line.pin(normed1), grads, preferred_element_type=f32), 1)
    slices, row_dot, dgain1 = normed_grad(scalars, grads, w_query, w_key, w_value, x, factor1, gain1, n_tp)
    slices_arrived = trade(slices, "tensor")

    mine = lambda array, dimension: lax.dynamic_slice_in_dim(
        array, dp * (array.shape[dimension] // n_dp), array.shape[dimension] // n_dp, dimension
    )
    flat_heads = dhead_gains.reshape(1, -1)
    flat_heads = jnp.pad(flat_heads, ((0, 0), (0, features - flat_heads.shape[1])))
    small = jnp.concatenate([drouter.T, dgain2, dgain1, flat_heads], axis=0)
    row_dot = row_dot.reshape(8, token_count // 8)

    def chain(value, axis, count):
        mask = 1
        while mask < count:
            arrived = swap(value, axis, count, mask)
            yield
            value = add_to(scalars, value, arrived)
            mask *= 2
        return value

    def small_chain():
        total = yield from chain(small, "dp", n_dp)
        own = yield from chain(mine(total[: experts + 2], 1), "tensor", n_tp)
        return total[experts + 2], own

    done = {}

    def advance(name, steps):
        if name not in done:
            try:
                next(steps)
            except StopIteration as end:
                done[name] = end.value

    rows_chain, small_chain = chain(row_dot, "tensor", n_tp), small_chain()
    advance("rows", rows_chain)
    advance("small", small_chain)
    output = output_of(scalars, stream, result_arrived)
    advance("rows", rows_chain)
    advance("small", small_chain)
    old = finish(scalars, [keep3[0]], old, lead, shift, experts)
    advance("rows", rows_chain)
    keep4, send4 = take4()
    given4 = swap(send4, "dp", n_dp, near)
    advance("small", small_chain)
    old = finish(scalars, [given3[0]], old, lead, other_shift, experts)
    advance("small", small_chain)
    old = finish(scalars, [keep4[0]], old, lead + first_share, shift, experts)
    while "rows" not in done:
        advance("rows", rows_chain)
    advance("small", small_chain)
    row_dot = done["rows"].reshape(token_count, 1)
    input_grad = final_grad(scalars, dattn, x, factor1, row_dot, gain1, slices_arrived)
    while "small" not in done:
        advance("small", small_chain)
    head_gains, small = done["small"]
    head_gains = mine(head_gains[: dhead_gains.size].reshape(dhead_gains.shape), 2)
    grad_gate, grad_up, grad_down = finish(scalars, [given4[0]], old, lead + first_share, other_shift, experts)
    return (
        output,
        input_grad,
        small[experts + 1],
        grad_qkv[0],
        grad_qkv[1],
        grad_qkv[2],
        head_gains[:, 0],
        head_gains[:, 1],
        grad_output,
        small[experts],
        small[:experts].T,
        grad_gate,
        grad_up,
        grad_down,
    )


def solution(mesh):
    placed = (
        P("dp", "tensor"),
        P("dp", "tensor"),
        P(),
        P(None, "tensor"),
        P(None, "tensor"),
        P(None, "tensor"),
        P("tensor", None),
        P("tensor", None),
        P("tensor", None),
        P(),
        P(),
        P(None, None, "tensor"),
        P(None, None, "tensor"),
        P(None, "tensor", None),
        P("dp", None),
    )
    n_dp, n_tp = mesh.shape["dp"], mesh.shape["tensor"]

    def layer(*args):
        cosine, sine = rope_constants(LEN, args[6].shape[1])
        return body(n_dp, n_tp, jnp.asarray(cosine), jnp.asarray(sine), *args)

    return jax.shard_map(
        layer,
        mesh=mesh,
        in_specs=placed,
        out_specs=(
            P("dp", "tensor"),
            P("dp", "tensor"),
            P("dp"),
            P("dp", "tensor"),
            P("dp", "tensor"),
            P("dp", "tensor"),
            P("tensor", "dp"),
            P("tensor", "dp"),
            P("tensor", "dp"),
            P("dp"),
            P("dp", None),
            P(None, "dp", "tensor"),
            P(None, "dp", "tensor"),
            P(None, "tensor", "dp"),
        ),
        check_vma=False,
    )
```

```python
import functools
import math

import jax
import jax.numpy as jnp
import numpy as np
from jax import lax
from jax.experimental import pallas as pl
from jax.experimental.pallas import tpu as pltpu
from jax.sharding import PartitionSpec as P

LEN = 1024
EPS = 1e-05
ROPE_BASE = 10000.0
VMEM_MIB = 60
TB = 256
MARKS = 4
PARTS = 1
HEAVY = 10**12
f32, bf16 = jnp.float32, jnp.bfloat16
NT = (((1,), (1,)), ((), ()))
TN = (((0,), (0,)), ((), ()))
NN = (((1,), (0,)), ((), ()))


def dot(left, right, dims=NN):
    return lax.dot_general(left, right, dims, preferred_element_type=f32)


def rope_constants(length, width):
    inv_freq = (ROPE_BASE ** (-(np.arange(width // 2, dtype=np.float32) * 2.0) / width)).astype(np.float32)
    angles = np.arange(length, dtype=np.float32)[:, None] * inv_freq[None, :]
    cosine, sine = np.cos(angles).astype(np.float32), np.sin(angles).astype(np.float32)
    return np.concatenate([cosine, cosine], axis=1), np.concatenate([-sine, sine], axis=1)


def bit_reverse(value, count):
    result, bit = 0, 1
    while bit < count:
        result = result * 2 + (value & 1)
        value >>= 1
        bit *= 2
    return result


def whole_spec():
    return pl.BlockSpec(memory_space=pltpu.VMEM)


class Line:
    def __init__(self):
        self.last = []

    def tick(self, axis, count):
        self.sent = swap(self.last[0], axis, count, 1)

    def take(self):
        self.last = [*self.last, self.sent]

    def pin(self, value):
        value, *self.last = lax.optimization_barrier((value, *self.last))
        return value


line = Line()


def call(body, grid, scalars, ins, in_specs, outs, out_specs, scratch=(), aliases=None, vmem=VMEM_MIB):
    deps, n_in, n_out = line.last, len(ins), len(outs)

    def without_deps(scalars, *refs):
        ins_outs = refs[len(deps) : n_in + n_out + len(deps)]
        body(scalars, *ins_outs, *refs[n_in + n_out + len(deps) + MARKS :])

    outs, out_specs = list(outs), list(out_specs)
    any_place = pl.BlockSpec(memory_space=pl.ANY)

    result = pl.pallas_call(
        without_deps,
        out_shape=outs + [struct((8, 128), f32)] * MARKS,
        grid_spec=pltpu.PrefetchScalarGridSpec(
            num_scalar_prefetch=1,
            grid=grid,
            in_specs=[any_place] * len(deps) + list(in_specs),
            out_specs=out_specs + [any_place] * MARKS,
            scratch_shapes=list(scratch),
        ),
        input_output_aliases={1 + len(deps) + k: v for k, v in (aliases or {}).items()},
        compiler_params=pltpu.CompilerParams(vmem_limit_bytes=vmem << 20),
        cost_estimate=pl.CostEstimate(flops=HEAVY, bytes_accessed=1, transcendentals=0),
    )(scalars, *deps, *ins)
    line.last = result[len(outs) :]
    return result[: len(outs)]


def struct(shape, dtype):
    return jax.ShapeDtypeStruct(shape, dtype)


def swap(value, axis, count, mask):
    return lax.ppermute(value, axis, [(i, i ^ mask) for i in range(count)])


def gather_pieces(value, axis, count, pin=lambda v: v):
    if count == 4 and isinstance(value, tuple):
        one, two = (tuple(swap(half, axis, count, mask) for half in value) for mask in (1, 2))
        one, two = pin((one, two))
        return [value, one, two, (swap(two[0], axis, count, 1), swap(one[1], axis, count, 2))]
    if isinstance(value, tuple):
        value = jnp.concatenate(value, axis=0)
    if count == 4:
        half = value.shape[0] // 2
        one, two = swap(value, axis, count, 1), swap(value, axis, count, 2)
        one, two = pin((one, two))
        return [value, one, two, (swap(two[:half], axis, count, 1), swap(one[half:], axis, count, 2))]
    pieces, mask = [value], 1
    while mask < count:
        pieces = pieces + [swap(piece, axis, count, mask) for piece in pieces]
        mask *= 2
    return pieces


def direct_pieces(value, axis, count):
    return [value] + [swap(value, axis, count, r) for r in range(1, count)]


def flat(pieces):
    return [part for piece in pieces for part in (piece if isinstance(piece, tuple) else (piece,))]


def piece_specs(pieces, block, width):
    specs = []
    for piece in pieces:
        if isinstance(piece, tuple):
            count = piece[0].shape[0] // block
            specs.append(pl.BlockSpec((block, width), lambda i, s, n=count: (jnp.minimum(i, n - 1), 0)))
            specs.append(pl.BlockSpec((block, width), lambda i, s, n=count: (jnp.maximum(i - n, 0), 0)))
        else:
            specs.append(pl.BlockSpec((block, width), lambda i, s: (i, 0)))
    return specs


def halved(pieces):
    return [isinstance(piece, tuple) for piece in pieces]


def read_pieces(refs, halves):
    refs, values = list(refs), []
    early = pl.program_id(0) < pl.num_programs(0) // 2
    for in_halves in halves:
        value = refs.pop(0)[...]
        values.append(jnp.where(early, value, refs.pop(0)[...]) if in_halves else value)
    return values


def trade(pieces, axis):
    return lax.all_to_all(pieces, axis, 0, 0, tiled=True)


def halves_kernel(scalars, keep, keep2, arrived, arrived2, keep_out, send_out):
    keep_out[...] = (keep[...].astype(f32) + arrived[...].astype(f32)).astype(bf16)
    send_out[...] = (keep2[...].astype(f32) + arrived2[...].astype(f32)).astype(bf16)


def add_halves(scalars, keep, arrived):
    keep, arrived = line.pin((keep, arrived))
    half = keep.shape[0] // 2
    low = lambda left, right: (left.astype(f32) + right.astype(f32)).astype(bf16)
    out = low(keep[:half], arrived[:half]), low(keep[half:], arrived[half:])
    line.last = [*line.last, out[1]]
    return out


def sum_kernel(scalars, left, right, out):
    out[...] = left[...] + right[...]


def add_to(scalars, left, right):
    whole = pl.BlockSpec(left.shape, lambda i, s: (0, 0))
    return call(sum_kernel, (1,), scalars, [left, right], [whole] * 2, [struct(left.shape, f32)], [whole])[0]


def two_terms(value, width):
    high = value.astype(bf16)
    low = (value - high.astype(f32)).astype(bf16)
    rest = jnp.zeros((value.shape[0], width - 2 * value.shape[1]), bf16)
    return jnp.concatenate([high, low, rest], axis=1)


def transpose_blocks(scalars, first, source, target, dp_count):
    width = source.shape[1] // dp_count
    for place in range(dp_count):
        cols = pl.ds(pl.multiple_of(scalars[first + place] * width, width), width)
        target[place * width : (place + 1) * width, :] = source[:, cols].T


def named_kernel(scalars, ids, *refs):
    *shares, out, shares_out = refs
    for r, share in enumerate(shares):
        shares_out[scalars[r]] = share[...]
    named = jnp.zeros(out.shape, jnp.bool_)
    lanes = lax.broadcasted_iota(jnp.int32, out.shape, 1)
    for choice in range(ids.shape[1]):
        named = named | (ids[:, choice : choice + 1] == lanes)
    out[...] = named.astype(f32)


def kept_kernel(capacity, scalars, named, out):
    tokens = named.shape[0]
    earlier = lax.broadcasted_iota(jnp.int32, (tokens, tokens), 0) > lax.broadcasted_iota(
        jnp.int32, (tokens, tokens), 1
    )
    rank = dot(jnp.where(earlier, 1.0, 0.0).astype(bf16), named[...].astype(bf16))
    out[...] = jnp.where(rank < capacity, named[...], 0.0)


def named_pairs(scalars, expert_ids, shares, experts):
    tokens, chosen = expert_ids.shape
    plain = lambda h, w: pl.BlockSpec((h, w), lambda i, s: (0, 0))
    rows, features = shares[0].shape
    whole = (len(shares), rows, features)
    return call(
        named_kernel,
        (1,),
        scalars,
        [expert_ids, *shares],
        [plain(tokens, chosen)] + [plain(rows, features)] * len(shares),
        [struct((tokens, experts), f32), struct(whole, shares[0].dtype)],
        [plain(tokens, experts), pl.BlockSpec(whole, lambda i, s: (0, 0, 0))],
    )


def kept_pairs(scalars, named, capacity):
    plain = pl.BlockSpec(named.shape, lambda i, s: (0, 0))
    out = [struct(named.shape, f32)]
    return call(functools.partial(kept_kernel, capacity), (1,), scalars, [named], [plain], out, [plain])[0]


def project_kernel(n_tp, halves, heads, scalars, *refs):
    n_in = len(halves) + sum(halves)
    pieces = read_pieces(refs[:n_in], halves)
    gain, wq, wk, wv, q_gain, k_gain, cosine, sine = refs[n_in : n_in + 8]
    x_out, normed_out, factor_out, q_raw, k_raw, q_rot, k_rot, v_out = refs[n_in + 8 :]
    width = pieces[0].shape[1]
    features = width * n_tp
    values = [piece.astype(f32) for piece in pieces]
    squares = sum(jnp.sum(value * value, axis=1, keepdims=True) for value in values)
    factor = lax.rsqrt(squares / features + EPS)
    factor_out[...] = factor
    for r in range(n_tp):
        cols = pl.ds(pl.multiple_of(scalars[r] * width, width), width)
        x_out[:, cols] = pieces[r]
        normed_out[:, cols] = (values[r] * factor * gain[:, cols]).astype(bf16)
    normed = normed_out[...]
    cos, sin = cosine[...], sine[...]
    hd = cos.shape[1]
    for weight, head_gain, raw, rotated in ((wq, q_gain, q_raw, q_rot), (wk, k_gain, k_raw, k_rot)):
        product = dot(normed, weight[...])
        raw[...] = product
        for h in range(heads):
            part = product[:, h * hd : (h + 1) * hd]
            scale = lax.rsqrt(jnp.mean(part * part, axis=1, keepdims=True) + EPS)
            part = part * scale * head_gain[h : h + 1, :]
            part = part * cos + pltpu.roll(part, hd // 2, 1) * sin
            rotated[:, h * hd : (h + 1) * hd] = part.astype(bf16)
    v_out[...] = dot(normed, wv[...]).astype(bf16)


def project(scalars, pieces, gain, wq, wk, wv, q_gain, k_gain, cosine, sine):
    n_tp = len(pieces)
    tokens, width = pieces[0].shape
    features = width * n_tp
    heads, hd = q_gain.shape
    local = heads * hd
    rows = lambda w: pl.BlockSpec((TB, w), lambda i, s: (i, 0))
    return call(
        functools.partial(project_kernel, n_tp, halved(pieces), heads),
        (tokens // TB,),
        scalars,
        [*flat(pieces), gain, wq, wk, wv, q_gain, k_gain, cosine, sine],
        piece_specs(pieces, TB, width) + [whole_spec()] * 6 + [rows(hd)] * 2,
        [
            struct((tokens, features), bf16),
            struct((tokens, features), bf16),
            struct((tokens, 1), f32),
            struct((tokens, local), f32),
            struct((tokens, local), f32),
            struct((tokens, local), bf16),
            struct((tokens, local), bf16),
            struct((tokens, local), bf16),
        ],
        [rows(features), rows(features), rows(1)] + [rows(local)] * 5,
    )


def attend_kernel(block, scalars, q_ref, k_ref, v_ref, top_ref, bottom_ref, total_ref):
    tokens, hd = q_ref.shape
    scale = 1.0 / math.sqrt(hd)
    for i in range(tokens // block):
        rows = slice(i * block, (i + 1) * block)
        reach = (i + 1) * block
        scores = dot(q_ref[rows, :], k_ref[:reach, :], NT) * scale
        at_row = i * block + lax.broadcasted_iota(jnp.int32, scores.shape, 0)
        at_col = lax.broadcasted_iota(jnp.int32, scores.shape, 1)
        scores = jnp.where(at_row >= at_col, scores, -1e30)
        top = jnp.max(scores, axis=1, keepdims=True)
        weights = jnp.exp(scores - top)
        total = jnp.sum(weights, axis=1, keepdims=True)
        probs = (weights * (1.0 / total)).astype(bf16)
        half = tokens // 2
        out_ref, first = (top_ref, 0) if reach <= half else (bottom_ref, half)
        out_ref[i * block - first : reach - first, :] = dot(probs, v_ref[:reach, :]).astype(bf16)
        total_ref[0, rows, :] = top + jnp.log(total)


def attend(scalars, q_rot, k_rot, value, heads):
    tokens, local = q_rot.shape
    hd = local // heads
    column = pl.BlockSpec((tokens, hd), lambda h, s: (0, h))
    return call(
        functools.partial(attend_kernel, min(256, tokens // 2)),
        (heads,),
        scalars,
        [q_rot, k_rot, value],
        [column] * 3,
        [struct((tokens // 2, local), bf16)] * 2 + [struct((heads, tokens, 1), f32)],
        [pl.BlockSpec((tokens // 2, hd), lambda h, s: (0, h))] * 2
        + [pl.BlockSpec((1, tokens, 1), lambda h, s: (h, 0, 0))],
    )


def attend_back_kernel(block, scalars, *refs):
    (q_ref, k_ref, v_ref, go_ref, total_ref, q_raw, k_raw, q_gain, k_gain, cosine, sine) = refs[:11]
    grads_out, dgain_out, dq_acc, dk_acc, dv_acc = refs[11:]
    tokens, hd = q_ref.shape
    scale = 1.0 / math.sqrt(hd)
    count = tokens // block
    for i in reversed(range(count)):
        rows = slice(i * block, (i + 1) * block)
        reach = (i + 1) * block
        query, grad = q_ref[rows, :], go_ref[rows, :]
        scores = dot(query, k_ref[:reach, :], NT) * scale
        at_row = i * block + lax.broadcasted_iota(jnp.int32, scores.shape, 0)
        at_col = lax.broadcasted_iota(jnp.int32, scores.shape, 1)
        scores = jnp.where(at_row >= at_col, scores, -1e30)
        probs = jnp.exp(scores - total_ref[0, rows, :])
        dprobs = dot(grad, v_ref[:reach, :], NT)
        delta = jnp.sum(dprobs * probs, axis=1, keepdims=True)
        dscores = (probs * (dprobs - delta)).astype(bf16)
        dq_acc[rows, :] = dot(dscores, k_ref[:reach, :]) * scale
        dk = dot(dscores, query, TN) * scale
        dv = dot(probs.astype(bf16), grad, TN)
        if i == count - 1:
            dk_acc[...] = dk
            dv_acc[...] = dv
        else:
            dk_acc[:reach, :] += dk
            dv_acc[:reach, :] += dv
    grads_out[2] = dv_acc[...].astype(bf16)
    cos, sin = cosine[...], sine[...]
    dgains = []
    for j, acc, raw_ref, gain_ref in ((0, dq_acc, q_raw, q_gain), (1, dk_acc, k_raw, k_gain)):
        grad = acc[...]
        grad = grad * cos - pltpu.roll(grad, hd // 2, 1) * sin
        raw = raw_ref[...]
        factor = lax.rsqrt(jnp.mean(raw * raw, axis=1, keepdims=True) + EPS)
        normal = raw * factor
        dgains.append(jnp.sum(grad * normal, axis=0, keepdims=True))
        scaled = grad * gain_ref[0]
        mean = jnp.mean(scaled * normal, axis=1, keepdims=True)
        grads_out[j] = (factor * (scaled - normal * mean)).astype(bf16)
    dgain_out[0] = jnp.concatenate(dgains, axis=0)


def attend_back(scalars, q_rot, k_rot, value, grad, totals, q_raw, k_raw, q_gain, k_gain, cosine, sine):
    tokens, local = q_rot.shape
    heads, hd = q_gain.shape
    column = pl.BlockSpec((tokens, hd), lambda h, s: (0, h))
    gain_spec = pl.BlockSpec((1, 1, hd), lambda h, s: (h, 0, 0))
    table = pl.BlockSpec((tokens, hd), lambda h, s: (0, 0))
    return call(
        functools.partial(attend_back_kernel, min(256, tokens)),
        (heads,),
        scalars,
        [q_rot, k_rot, value, grad, totals, q_raw, k_raw, q_gain[:, None, :], k_gain[:, None, :], cosine, sine],
        [column] * 4
        + [pl.BlockSpec((1, tokens, 1), lambda h, s: (h, 0, 0))]
        + [column] * 2
        + [gain_spec] * 2
        + [table] * 2,
        [struct((3, tokens, local), bf16), struct((heads, 2, hd), f32)],
        [
            pl.BlockSpec((3, tokens, hd), lambda h, s: (0, 0, h)),
            pl.BlockSpec((1, 2, hd), lambda h, s: (h, 0, 0)),
        ],
        [pltpu.VMEM((tokens, hd), f32)] * 3,
    )


def whole_first_kernel(n_in, each, base, scalars, *refs):
    pieces, (whole_out, turned_out) = refs[:n_in], refs[n_in:]
    width = pieces[0].shape[1]
    part = width // each
    for r in range(n_in):
        cols = pl.ds(pl.multiple_of(scalars[r] * width, width), width)
        whole_out[:, cols] = pieces[r][...]
        for q in range(each):
            rows = pl.ds(pl.multiple_of(scalars[base + r * each + q] * part, part), part)
            turned_out[rows, :] = pieces[r][:, q * part : (q + 1) * part].T


def whole_last_kernel(scalars, piece, old_whole, old_turned, whole_out, turned_out):
    whole_out[...] = piece[...]
    turned_out[...] = piece[...].T


def whole_first(scalars, pieces, n_tp, dp_count, base):
    tokens, width = pieces[0].shape
    features = width * n_tp
    return call(
        functools.partial(whole_first_kernel, len(pieces), dp_count // n_tp, base),
        (tokens // TB,),
        scalars,
        pieces,
        [pl.BlockSpec((TB, width), lambda i, s: (i, 0))] * len(pieces),
        [struct((tokens, features), bf16), struct((features, tokens), bf16)],
        [
            pl.BlockSpec((TB, features), lambda i, s: (i, 0)),
            pl.BlockSpec((features, TB), lambda i, s: (0, i)),
        ],
    )


def whole_last(scalars, piece, r, whole, turned, dp_count, n_tp, base):
    tokens, width = piece.shape
    each = dp_count // n_tp
    part = width // each
    place = lambda s, q: s[base + r * each + q]
    return call(
        whole_last_kernel,
        (tokens // TB, each),
        scalars,
        [piece, whole, turned],
        [pl.BlockSpec((TB, part), lambda i, q, s: (i, q))] + [pl.BlockSpec(memory_space=pl.ANY)] * 2,
        [struct(whole.shape, bf16), struct(turned.shape, bf16)],
        [
            pl.BlockSpec((TB, part), lambda i, q, s: (i, s[r] * each + q)),
            pl.BlockSpec((part, TB), lambda i, q, s: (place(s, q), i)),
        ],
        aliases={1: 0, 2: 1},
    )


def add_products(total, pieces, weights):
    for piece, weight in zip(pieces, weights):
        total += dot(piece, weight[...].reshape(piece.shape[1], weight.shape[-1]))
    return total


def stream_first_kernel(halves, scalars, x_ref, *refs):
    n_in = len(halves) + sum(halves)
    pieces, weights, out = read_pieces(refs[:n_in], halves), refs[n_in:-1], refs[-1]
    out[...] = add_products(x_ref[...].astype(f32), pieces, weights)


def weight_specs(w_all, places):
    n_dp, _, share, features = w_all.shape
    return [pl.BlockSpec((n_dp, 1, share, features), lambda i, s, r=r: (0, s[r], 0, 0)) for r in places]


def stream_first(scalars, pieces, x, w_all):
    tokens, features = x.shape
    rows = pl.BlockSpec((TB, features), lambda i, s: (i, 0))
    return call(
        functools.partial(stream_first_kernel, halved(pieces)),
        (tokens // TB,),
        scalars,
        [x, *flat(pieces)] + [w_all] * len(pieces),
        [rows] + piece_specs(pieces, TB, flat(pieces)[0].shape[1]) + weight_specs(w_all, range(len(pieces))),
        [struct((tokens, features), f32)],
        [rows],
    )[0]


def stream_kernel(n_tp, halves, dp_count, scalars, *refs):
    n_last, n_in = len(halves), len(halves) + sum(halves)
    pieces = read_pieces(refs[:n_in], halves)
    weights = refs[n_in : n_in + n_last]
    first, gain, router, kept = refs[n_in + n_last : n_in + n_last + 4]
    stream_out, normed_out, mine_out, turned_out, factor_out, probs_out, gates_out = refs[n_in + n_last + 4 :]
    total = add_products(first[...], pieces, weights)
    width = total.shape[1] // n_tp
    stream_out[...] = total
    factor = lax.rsqrt(jnp.mean(total * total, axis=1, keepdims=True) + EPS)
    factor_out[...] = factor
    normed = (total * factor * gain[...]).astype(bf16)
    normed_out[...] = normed
    mine_out[:, :width] = normed_out[:, pl.ds(pl.multiple_of(scalars[0] * width, width), width)]
    logits = dot(normed, router[...])
    power = jnp.exp(logits - jnp.max(logits, axis=1, keepdims=True))
    probs = power / jnp.sum(power, axis=1, keepdims=True)
    probs_out[...] = probs
    gates = probs * kept[...]
    gates_out[...] = gates
    mine_out[:, width:] = two_terms(gates, mine_out.shape[1] - width)
    transpose_blocks(scalars, n_tp, normed_out, turned_out, dp_count)


def stream_of(scalars, pieces, first, w_all, gain, router, kept, n_tp, dp_count):
    tokens, features = first.shape
    experts = router.shape[1]
    width = features // n_tp
    rows = lambda w: pl.BlockSpec((TB, w), lambda i, s: (i, 0))
    places = range(n_tp - len(pieces), n_tp)
    return call(
        functools.partial(stream_kernel, n_tp, halved(pieces), dp_count),
        (tokens // TB,),
        scalars,
        [*flat(pieces)] + [w_all] * len(pieces) + [first, gain, router, kept],
        piece_specs(pieces, TB, flat(pieces)[0].shape[1])
        + weight_specs(w_all, places)
        + [rows(features), whole_spec(), whole_spec(), rows(experts)],
        [
            struct((tokens, features), f32),
            struct((tokens, features), bf16),
            struct((tokens, width + 128), bf16),
            struct((features, tokens), bf16),
            struct((tokens, 1), f32),
            struct((tokens, experts), f32),
            struct((tokens, experts), f32),
        ],
        [
            rows(features),
            rows(features),
            rows(width + 128),
            pl.BlockSpec((features, TB), lambda i, s: (0, i)),
            rows(1),
            rows(experts),
            rows(experts),
        ],
    )


def expert_kernel(first, shift, scalars, n_ref, g_ref, gates_ref, wg, wu, wd, hidden_out, pair_out, dgate_out):
    step = pl.program_id(0)
    expert = first + step + (0 if shift is None else scalars[shift])
    width = wg.shape[-1]

    @pl.when(step == 0)
    def _():
        dgate_out[...] = jnp.zeros_like(dgate_out)

    gate_val, up_val = dot(n_ref[...], wg[0]), dot(n_ref[...], wu[0])
    back = dot(g_ref[...], wd[0], NT)
    gates = gates_ref[...]
    here = lax.broadcasted_iota(jnp.int32, gates.shape, 1) == expert
    gate = jnp.sum(jnp.where(here, gates, 0.0), axis=1, keepdims=True)
    sigmoid = 1.0 / (1.0 + jnp.exp(-gate_val))
    swish = gate_val * sigmoid
    hidden = (swish * up_val).astype(bf16).astype(f32)
    hidden_out[0] = (hidden * gate).astype(bf16)
    dgate = jnp.sum(back * hidden, axis=1, keepdims=True)
    dgate_out[...] = jnp.where(here, dgate, dgate_out[...])
    dhidden = back * gate
    pair_out[0, :, :width] = (dhidden * up_val * sigmoid * (1.0 + gate_val * (1.0 - sigmoid))).astype(bf16)
    pair_out[0, :, width:] = (dhidden * swish).astype(bf16)


def run_experts(scalars, normed, grad, gates, wg, wu, wd, first, count, shift=None):
    tokens, features = normed.shape
    experts, _, width = wg.shape
    place = lambda i, s: first + i + (0 if shift is None else s[shift])
    weight = lambda shape: pl.BlockSpec((1, *shape), lambda i, s: (place(i, s), 0, 0))
    given = lambda shape: pl.BlockSpec((1, *shape), lambda i, s: (i, 0, 0))
    return call(
        functools.partial(expert_kernel, first, shift),
        (count,),
        scalars,
        [normed, grad, gates, wg, wu, wd],
        [whole_spec()] * 3 + [weight((features, width))] * 2 + [weight((width, features))],
        [
            struct((count, tokens, width), bf16),
            struct((count, tokens, 2 * width), bf16),
            struct((tokens, experts), f32),
        ],
        [
            given((tokens, width)),
            given((tokens, 2 * width)),
            pl.BlockSpec((tokens, experts), lambda i, s: (0, 0)),
        ],
    )


def weight_grads_kernel(scalars, turned, g_turned, hidden, pair, keep_out, send_out):
    half, _, rows, _ = keep_out.shape
    width = hidden.shape[-1]
    first = dot(turned[...], pair[0]).astype(bf16).reshape(2 * half, rows, 2 * width)
    keep_out[:, 0, :, : 2 * width] = first[:half]
    send_out[:, 0, :, : 2 * width] = first[half:]
    second = dot(g_turned[...], hidden[0]).astype(bf16).reshape(2 * half, rows, width)
    keep_out[:, 0, :, 2 * width :] = second[:half]
    send_out[:, 0, :, 2 * width :] = second[half:]


def weight_grads(scalars, turned, g_turned, hidden, pair, offset, count, dp_count):
    features, tokens = turned.shape
    width = hidden.shape[-1]
    half, rows = dp_count // 2, features // dp_count
    out = struct((half, count, rows, 3 * width), bf16)
    out_spec = pl.BlockSpec((half, 1, rows, 3 * width), lambda i, s: (0, i, 0, 0))
    return call(
        weight_grads_kernel,
        (count,),
        scalars,
        [turned, g_turned, hidden, pair],
        [
            whole_spec(),
            whole_spec(),
            pl.BlockSpec((1, tokens, width), lambda i, s: (offset + i, 0, 0)),
            pl.BlockSpec((1, tokens, 2 * width), lambda i, s: (offset + i, 0, 0)),
        ],
        [out, out],
        [out_spec, out_spec],
    )


def inner_swap(index):
    return (index & ~3) | ((index & 1) << 1) | ((index >> 1) & 1)


def shared_grads_kernel(scalars, *refs):
    turned, turned2, g_turned, g_turned2, hidden, hidden2, pair, pair2, keep_out, send_out = refs
    half, _, rows, _ = keep_out.shape
    width = hidden.shape[-1]
    first = dot(turned[...], pair[0]) + dot(turned2[...], pair2[0])
    first = first.astype(bf16).reshape(2 * half, rows, 2 * width)
    second = dot(g_turned[...], hidden[0]) + dot(g_turned2[...], hidden2[0])
    second = second.astype(bf16).reshape(2 * half, rows, width)
    for out, base in ((keep_out, 0), (send_out, half)):
        for place in range(half):
            out[inner_swap(place), 0, :, : 2 * width] = first[base + place]
            out[inner_swap(place), 0, :, 2 * width :] = second[base + place]


def shared_grads(scalars, turned, turned2, g_turned, g_turned2, hidden, hidden2, pair, pair2, shift, base, offset, count,
                 dp_count):
    features, tokens = turned.shape
    width = hidden2.shape[-1]
    half, rows = dp_count // 2, features // dp_count
    out = struct((half, count, rows, 3 * width), bf16)
    out_spec = pl.BlockSpec((half, 1, rows, 3 * width), lambda i, s: (0, i, 0, 0))
    mine = lambda w: pl.BlockSpec((1, tokens, w), lambda i, s: (base + s[shift] + offset + i, 0, 0))
    other = lambda w: pl.BlockSpec((1, tokens, w), lambda i, s: (offset + i, 0, 0))
    return call(
        shared_grads_kernel,
        (count,),
        scalars,
        [turned, turned2, g_turned, g_turned2, hidden, hidden2, pair, pair2],
        [whole_spec()] * 4 + [mine(width), other(width), mine(2 * width), other(2 * width)],
        [out, out],
        [out_spec, out_spec],
    )


def finish_kernel(n_parts, n_old, scalars, *refs):
    parts = refs[:n_parts]
    gate_out, up_out, down_out = refs[n_parts + n_old :]
    width = gate_out.shape[-1]
    total = sum(part[0].astype(f32) for part in parts)
    gate_out[0] = total[:, :width]
    up_out[0] = total[:, width : 2 * width]
    down_out[0] = total[:, 2 * width :].T


def finish(scalars, parts, old, first, shift, experts):
    count, rows, wide = parts[0].shape
    width = wide // 3
    place = lambda i, s: (first + i + (0 if shift is None else s[shift]), 0, 0)
    spec = pl.BlockSpec((1, rows, width), place)
    down_spec = pl.BlockSpec((1, width, rows), place)
    return call(
        functools.partial(finish_kernel, len(parts), len(old)),
        (count,),
        scalars,
        [*parts, *old],
        [pl.BlockSpec((1, rows, wide), lambda i, s: (i, 0, 0))] * len(parts)
        + [pl.BlockSpec(memory_space=pl.ANY)] * len(old),
        [struct((experts, rows, width), f32)] * 2 + [struct((experts, width, rows), f32)],
        [spec, spec, down_spec],
        aliases={len(parts) + k: k for k in range(len(old))},
    )


def chunk_specs(chunks, shape):
    specs, first = [], 0
    for chunk in chunks:
        count = chunk.shape[0]
        specs.append(
            pl.BlockSpec(
                (1, *shape), lambda i, s, first=first, count=count: (jnp.clip(i - first, 0, count - 1), 0, 0)
            )
        )
        first += count
    return specs


def input_grad_kernel(sizes, n_tp, scalars, *refs):
    n = len(sizes)
    pairs, (wg, wu), dgates = refs[:n], refs[n : n + 2], refs[n + 2 : 2 * n + 2]
    out, acc = refs[-2:]
    step = pl.program_id(0)
    width = wg.shape[-1]
    first = 0
    for pair, size in zip(pairs, sizes):

        def product(pair=pair):
            return dot(pair[0, :, :width], wg[0], NT) + dot(pair[0, :, width:], wu[0], NT)

        if first == 0:

            @pl.when(step == 0)
            def _(product=product):
                acc[...] = product()

        @pl.when((step >= max(first, 1)) & (step < first + size))
        def _(product=product):
            acc[...] += product()

        first += size

    @pl.when(step == pl.num_programs(0) - 1)
    def _():
        rows, features = acc.shape[0] // n_tp, acc.shape[1]
        for k in range(n_tp):
            place = slice(k * rows, (k + 1) * rows)
            out[k, :, :features] = acc[place, :].astype(bf16)
            dgate = sum(ref[place, :] for ref in dgates)
            out[k, :, features:] = two_terms(dgate, out.shape[2] - features)


def input_grads(scalars, pairs, wg, wu, dgates, n_tp):
    experts, features, width = wg.shape
    tokens = pairs[0].shape[1]
    rows = tokens // n_tp
    weight = pl.BlockSpec((1, features, width), lambda i, s: (i, 0, 0))
    return call(
        functools.partial(input_grad_kernel, [pair.shape[0] for pair in pairs], n_tp),
        (experts,),
        scalars,
        [*pairs, wg, wu, *dgates],
        chunk_specs(pairs, (tokens, 2 * width)) + [weight] * 2 + [whole_spec()] * len(dgates),
        [struct((n_tp, rows, features + 128), bf16)],
        [pl.BlockSpec((n_tp, rows, features + 128), lambda i, s: (0, 0, 0))],
        [pltpu.VMEM((tokens, features), f32)],
    )


def result_kernel(sizes, n_tp, scalars, *refs):
    hiddens, wd = refs[: len(sizes)], refs[len(sizes)]
    out, acc = refs[-2:]
    step = pl.program_id(0)
    first = 0
    for hidden, size in zip(hiddens, sizes):

        if first == 0:

            @pl.when(step == 0)
            def _(hidden=hidden):
                acc[...] = dot(hidden[0], wd[0])

        @pl.when((step >= max(first, 1)) & (step < first + size))
        def _(hidden=hidden):
            acc[...] += dot(hidden[0], wd[0])

        first += size

    @pl.when(step == pl.num_programs(0) - 1)
    def _():
        cols = acc.shape[1] // n_tp
        for k in range(n_tp):
            out[k] = acc[:, k * cols : (k + 1) * cols].astype(bf16)


def results(scalars, hiddens, wd, n_tp):
    experts, width, features = wd.shape
    tokens = hiddens[0].shape[1]
    cols = features // n_tp
    return call(
        functools.partial(result_kernel, [hidden.shape[0] for hidden in hiddens], n_tp),
        (experts,),
        scalars,
        [*hiddens, wd],
        chunk_specs(hiddens, (tokens, width)) + [pl.BlockSpec((1, width, features), lambda i, s: (i, 0, 0))],
        [struct((n_tp, tokens, cols), bf16)],
        [pl.BlockSpec((n_tp, tokens, cols), lambda i, s: (0, 0, 0))],
        [pltpu.VMEM((tokens, features), f32)],
    )


def rows_kernel(n_tp, scalars, *refs):
    parts, probs, kept, stream, normed, factor, upstream, gain, router = refs[:9]
    grad_out, dgain_out, drouter_out = refs[9:]
    features, experts = router.shape
    total = sum(parts[k, :, :features].astype(f32) for k in range(n_tp))
    both = sum(parts[k, :, features:].astype(f32) for k in range(n_tp))
    dprobs = (both[:, :experts] + both[:, experts : 2 * experts]) * kept[...]
    soft = probs[...]
    dlogits = soft * (dprobs - jnp.sum(dprobs * soft, axis=1, keepdims=True))
    dlogits = dlogits.astype(bf16)
    drouter_out[...] = dot(normed[...], dlogits, TN)
    total += dot(dlogits, router[...], NT)
    scale = factor[...]
    normal = stream[...] * scale
    dgain_out[...] = jnp.sum(total * normal, axis=0, keepdims=True)
    scaled = total * gain[...]
    mean = jnp.mean(scaled * normal, axis=1, keepdims=True)
    grad_out[...] = (upstream[...].astype(f32) + scale * (scaled - normal * mean)).astype(bf16)


def stream_grad_rows(scalars, parts, probs, kept, stream, normed, factor, upstream, gain, router):
    n_tp, rows, _ = parts.shape
    features, experts = router.shape
    mine = lambda w: pl.BlockSpec((rows, w), lambda i, s: (s[0], 0))
    plain = lambda h, w: pl.BlockSpec((h, w), lambda i, s: (0, 0))
    return call(
        functools.partial(rows_kernel, n_tp),
        (1,),
        scalars,
        [parts, probs, kept, stream, normed, factor, upstream, gain, router],
        [pl.BlockSpec(parts.shape, lambda i, s: (0, 0, 0))]
        + [mine(experts), mine(experts), mine(features), mine(features), mine(1), mine(features)]
        + [plain(1, features), plain(features, experts)],
        [struct((rows, features), bf16), struct((1, features), f32), struct((features, experts), f32)],
        [plain(rows, features), plain(1, features), plain(features, experts)],
    )


def attended_grad_kernel(scalars, grad, w_ref, out):
    out[...] = dot(grad[...], w_ref[...], NT).astype(bf16)


def attended_grad(scalars, grad, w_output):
    tokens, features = grad.shape
    local = w_output.shape[0]
    rows = lambda w: pl.BlockSpec((tokens // 2, w), lambda i, s: (i, 0))
    return call(
        attended_grad_kernel,
        (2,),
        scalars,
        [grad, w_output],
        [rows(features), whole_spec()],
        [struct((tokens, local), bf16)],
        [rows(local)],
    )[0]


def normed_grad_kernel(scalars, grads, wq, wk, wv, x_ref, factor, gain, out, dot_out, dgain_out):
    total = sum(dot(grads[j], weight[...], NT) for j, weight in enumerate((wq, wk, wv)))
    out[0] = total.astype(bf16)
    normal = x_ref[...].astype(f32) * factor[...]
    product = total * normal
    dgain_out[...] = jnp.sum(product, axis=0, keepdims=True)
    part = jnp.sum(product * gain[...], axis=1, keepdims=True)

    @pl.when(pl.program_id(0) == 0)
    def _():
        dot_out[...] = part

    @pl.when(pl.program_id(0) > 0)
    def _():
        dot_out[...] += part


def normed_grad(scalars, grads, wq, wk, wv, x, factor, gain, n_tp):
    _, tokens, local = grads.shape
    features = wq.shape[0]
    width = features // n_tp
    weight = pl.BlockSpec((width, local), lambda i, s: (i, 0))
    column = lambda h: pl.BlockSpec((h, width), lambda i, s: (0, i))
    whole = pl.BlockSpec((tokens, 1), lambda i, s: (0, 0))
    return call(
        normed_grad_kernel,
        (n_tp,),
        scalars,
        [grads, wq, wk, wv, x, factor, gain],
        [pl.BlockSpec(grads.shape, lambda i, s: (0, 0, 0))] + [weight] * 3 + [column(tokens), whole, column(1)],
        [struct((n_tp, tokens, width), bf16), struct((tokens, 1), f32), struct((1, features), f32)],
        [pl.BlockSpec((1, tokens, width), lambda i, s: (i, 0, 0)), whole, column(1)],
    )


def flip_kernel(source, target):
    target[...] = source[...].T


def flip(scalars, value):
    tokens, features = value.shape
    return call(
        lambda scalars, source, target: flip_kernel(source, target),
        (tokens // TB,),
        scalars,
        [value],
        [pl.BlockSpec((TB, features), lambda i, s: (i, 0))],
        [struct((features, tokens), bf16)],
        [pl.BlockSpec((features, TB), lambda i, s: (0, i))],
    )[0]


def head_weight_grads(scalars, flipped, grads):
    features, tokens = flipped.shape
    count, _, local = grads.shape

    def kernel(scalars, flipped, grad, out):
        out[0] = dot(flipped[...], grad[0]).astype(bf16)

    return call(
        kernel,
        (count,),
        scalars,
        [flipped, grads],
        [whole_spec(), pl.BlockSpec((1, tokens, local), lambda i, s: (i, 0, 0))],
        [struct((count, features, local), bf16)],
        [pl.BlockSpec((1, features, local), lambda i, s: (i, 0, 0))],
    )[0]


def output_weight_grads(scalars, top, bottom, grad, first, dp_count):
    half, local = top.shape
    width = grad.shape[1] // dp_count

    def kernel(scalars, top, bottom, keep, send, keep_out, send_out):
        for grad, out in ((keep, keep_out), (send, send_out)):
            product = dot(top[...], grad[:half, :], TN) + dot(bottom[...], grad[half:, :], TN)
            out[0, 0] = product.astype(bf16)

    column = lambda base: pl.BlockSpec((2 * half, width), lambda i, s: (0, s[base + i]))
    block = pl.BlockSpec((1, 1, local, width), lambda i, s: (i, 0, 0, 0))
    return call(
        kernel,
        (dp_count // 2,),
        scalars,
        [top, bottom, grad, grad],
        [whole_spec(), whole_spec(), column(first), column(first + dp_count // 2)],
        [struct((dp_count // 2, 1, local, width), bf16)] * 2,
        [block] * 2,
    )


def turn_kernel(first, dp_count, scalars, source, target):
    transpose_blocks(scalars, first, source, target, dp_count)


def turn(scalars, value, n_tp, dp_count):
    tokens, features = value.shape
    return call(
        functools.partial(turn_kernel, n_tp, dp_count),
        (tokens // TB,),
        scalars,
        [value],
        [pl.BlockSpec((TB, features), lambda i, s: (i, 0))],
        [struct((features, tokens), bf16)],
        [pl.BlockSpec((features, TB), lambda i, s: (0, i))],
    )[0]


def output_kernel(scalars, stream, parts, out):
    out[...] = (stream[...] + sum(parts[k].astype(f32) for k in range(parts.shape[0]))).astype(bf16)


def output_of(scalars, stream, parts):
    n_tp, tokens, width = parts.shape
    return call(
        output_kernel,
        (tokens // TB,),
        scalars,
        [stream, parts],
        [
            pl.BlockSpec((TB, width), lambda i, s: (i, s[0])),
            pl.BlockSpec((n_tp, TB, width), lambda i, s: (0, i, 0)),
        ],
        [struct((tokens, width), bf16)],
        [pl.BlockSpec((TB, width), lambda i, s: (i, 0))],
    )[0]


def final_kernel(features, scalars, dattn, x_ref, factor, row_dot, gain, parts, out):
    total = sum(parts[k].astype(f32) for k in range(parts.shape[0]))
    scale = factor[...]
    normal = x_ref[...].astype(f32) * scale
    back = scale * (total * gain[...] - normal * (row_dot[...] / features))
    out[...] = (dattn[...].astype(f32) + back).astype(bf16)


def final_grad(scalars, dattn, x, factor, row_dot, gain, parts):
    n_tp, tokens, width = parts.shape
    plain = lambda w: pl.BlockSpec((TB, w), lambda i, s: (i, 0))
    mine = pl.BlockSpec((TB, width), lambda i, s: (i, s[0]))
    return call(
        functools.partial(final_kernel, dattn.shape[1]),
        (tokens // TB,),
        scalars,
        [dattn, x, factor, row_dot, gain, parts],
        [mine, mine, plain(1), plain(1), pl.BlockSpec((1, width), lambda i, s: (0, s[0]))]
        + [pl.BlockSpec((n_tp, TB, width), lambda i, s: (0, i, 0))],
        [struct((tokens, width), bf16)],
        [plain(width)],
    )[0]


def body(n_dp, n_tp, cosine, sine, tokens, cotangent, attn_gain, w_query, w_key, w_value, query_gain, key_gain,
         w_output, ffn_gain, w_router, w_gate, w_up, w_down, expert_ids):
    tp, dp = lax.axis_index("tensor"), lax.axis_index("dp")
    far, near = n_dp // 2, n_dp // 4
    side = (dp // near) % 2
    token_count, width = tokens.shape
    features = width * n_tp
    heads, hd = query_gain.shape
    local = heads * hd
    experts = w_router.shape[1]
    capacity = token_count * expert_ids.shape[1] // experts
    gain1, gain2 = attn_gain[None, :], ffn_gain[None, :]
    blocks = (2, 3, 3)
    lead = sum(blocks)
    shared = (experts - lead) // 2
    shift, other_shift = n_tp + n_dp, n_tp + n_dp + 1
    each = n_dp // n_tp
    scalars = jnp.stack(
        [tp ^ r for r in range(n_tp)]
        + [dp ^ bit_reverse(place, n_dp) for place in range(n_dp)]
        + [side * shared, (1 - side) * shared]
        + [bit_reverse(((tp ^ r) * each + q) ^ dp, n_dp) for r in range(n_tp) for q in range(each)]
    ).astype(jnp.int32)
    turned_base = n_tp + n_dp + 2

    line.last = []

    share = local // n_dp
    w_share = lax.dynamic_slice_in_dim(w_output, dp * share, share, 0)
    w_shares = direct_pieces(w_share, "tensor", n_tp)

    named, w_some = named_pairs(scalars, expert_ids, w_shares, experts)
    w_all = lax.all_gather(w_some, "dp")
    x_pieces = gather_pieces(tokens, "tensor", n_tp, pin=line.pin)
    kept = kept_pairs(scalars, named, capacity)
    x_pieces, g_mine = lax.optimization_barrier((x_pieces, cotangent))
    early = n_tp - 1 if n_tp == 4 else n_tp // 2
    g_pieces = [g_mine] + [swap(g_mine, "tensor", n_tp, r) for r in range(1, early)]
    x, normed1, factor1, q_raw, k_raw, q_rot, k_rot, value = project(
        scalars, x_pieces, gain1, w_query, w_key, w_value, query_gain, key_gain, cosine, sine
    )
    *attended, totals = attend(scalars, q_rot, k_rot, value, heads)
    attended, g_pieces = lax.optimization_barrier((tuple(attended), g_pieces))
    upstream, g_turned = whole_first(scalars, g_pieces, n_tp, n_dp, turned_base)
    flipped = flip(scalars, normed1)
    attended_pieces = gather_pieces(attended, "tensor", n_tp, pin=line.pin)
    stream = stream_first(scalars, attended_pieces[:early], x, w_all)
    g_mine = line.pin(g_mine)
    g_last = [swap(g_mine, "tensor", n_tp, r) for r in range(early, n_tp)]
    g_near = swap(g_mine, "dp", n_dp, near)
    stream, normed2, normed2_mine, turned, factor2, probs, gates = stream_of(
        scalars, attended_pieces[early:], stream, w_all, gain2, w_router, kept, n_tp, n_dp
    )
    for r in range(early, n_tp):
        upstream, g_turned = whole_last(
            scalars, g_last[r - early], r, upstream, g_turned, n_dp, n_tp, turned_base
        )
    normed_near = swap(normed2_mine, "dp", n_dp, near)
    g_near, _ = lax.optimization_barrier((g_near, upstream))
    upstream_near = lax.all_gather(g_near, "tensor", axis=1, tiled=True)
    gates_near = normed_near[:, width : width + experts].astype(f32)
    gates_near += normed_near[:, width + experts : width + 2 * experts].astype(f32)
    normed2_near = lax.all_gather(normed_near[:, :width], "tensor", axis=1, tiled=True)

    hiddens, pairs, dgates = [], [], []

    def run(first, count):
        out = run_experts(scalars, normed2, upstream, gates, w_gate, w_up, w_down, first, count)
        for kind, array in zip((hiddens, pairs, dgates), out):
            kind.append(array)

    def sum_step(keep, send, mask):
        arrived = swap(send, "dp", n_dp, mask)
        return lambda: add_halves(scalars, keep, arrived)

    lower = [mask for mask in (2, 4, 8, 16) if mask < far]

    def own_sums(index):
        keep, send = weight_grads(scalars, turned, g_turned, hiddens[index], pairs[index], 0, blocks[index], n_dp)
        return sum_step(keep, send, 1)

    def next_step(take):
        return sum_step(*take(), lower[0])

    def last_step(take):
        keep, send = take()
        for mask in lower[1:]:
            keep, send = sum_step(keep, send, mask)()
        return [keep[0], swap(send, "dp", n_dp, far)[0]]

    def complete(parts, old, index):
        return finish(scalars, parts, old, sum(blocks[:index]), None, experts)

    run(0, blocks[0])
    take0 = own_sums(0)
    run(blocks[0], blocks[1])
    take0 = next_step(take0)
    take1 = own_sums(1)
    run(blocks[0] + blocks[1], blocks[2])
    parts0 = last_step(take0)
    take1 = next_step(take1)
    line.tick("dp", n_dp)
    run(sum(blocks[:3]), experts - sum(blocks[:3]))
    line.take()
    take2 = own_sums(2)
    g_turned_near = turn(scalars, upstream_near, n_tp, n_dp)
    old = complete(parts0, [], 0)
    take2 = next_step(take2)
    line.tick("dp", n_dp)
    parts1 = last_step(take1)
    line.take()
    input_parts = input_grads(scalars, pairs, w_gate, w_up, dgates, n_tp)[0]
    input_arrived = trade(input_parts, "tensor")
    line.tick("dp", n_dp)
    turned_near = turn(scalars, normed2_near, n_tp, n_dp)
    line.take()
    parts2 = last_step(take2)
    line.tick("dp", n_dp)
    hidden_near, pair_near, _ = run_experts(
        scalars, normed2_near, upstream_near, gates_near, w_gate, w_up, w_down, lead, shared, shift
    )
    line.take()

    def shared_sums(offset, count):
        keep, send = shared_grads(
            scalars, turned, turned_near, g_turned, g_turned_near, hiddens[3], hidden_near, pairs[3], pair_near,
            shift, 0, offset, count, n_dp,
        )
        return sum_step(keep, send, 1)

    def shared_next(take):
        keep, send = take()
        for mask in lower:
            if mask != near:
                keep, send = sum_step(keep, send, mask)()
        return sum_step(keep, send, far)

    some = (shared + 1) // 2
    take3 = shared_sums(0, some)
    dattn_rows, dgain2, drouter = stream_grad_rows(
        scalars, input_arrived, probs, kept, stream, normed2, factor2, upstream, gain2, w_router
    )
    dattn = lax.all_gather(dattn_rows, "tensor", axis=0, tiled=True)
    take3 = shared_next(take3)
    line.tick("dp", n_dp)
    old = complete(parts1, old, 1)
    line.take()
    take4 = shared_sums(some, shared - some)
    result_parts = results(scalars, hiddens, w_down, n_tp)[0]
    take4 = shared_next(take4)

    def spread(value, dimension):
        return lax.psum_scatter(value, "dp", scatter_dimension=dimension, tiled=True).astype(f32)

    take5 = sum_step(*output_weight_grads(scalars, *attended, dattn, n_tp, n_dp), 1)
    line.tick("dp", n_dp)
    dattended = attended_grad(scalars, dattn, w_output)
    result_arrived = trade(line.pin(result_parts), "tensor")
    line.take()
    take5 = sum_step(*take5(), lower[0])
    grads, dhead_gains = attend_back(
        scalars, q_rot, k_rot, value, dattended, totals, q_raw, k_raw, query_gain, key_gain, cosine, sine
    )
    line.tick("dp", n_dp)
    keep3, send3 = take3()
    given3 = swap(send3, "dp", n_dp, near)
    line.take()
    grad_qkv = spread(head_weight_grads(scalars, flipped, grads), 1)
    line.tick("dp", n_dp)
    old = complete(parts2, old, 2)
    line.take()
    slices, row_dot, dgain1 = normed_grad(scalars, grads, w_query, w_key, w_value, x, factor1, gain1, n_tp)
    slices_arrived = trade(slices, "tensor")

    mine = lambda array, dimension: lax.dynamic_slice_in_dim(
        array, dp * (array.shape[dimension] // n_dp), array.shape[dimension] // n_dp, dimension
    )
    flat_heads = dhead_gains.reshape(1, -1)
    flat_heads = jnp.pad(flat_heads, ((0, 0), (0, features - flat_heads.shape[1])))
    small = jnp.concatenate([drouter.T, dgain2, dgain1, flat_heads], axis=0)
    row_dot = row_dot.reshape(8, token_count // 8)

    def chain(value, axis, count):
        mask = 1
        while mask < count:
            arrived = swap(value, axis, count, mask)
            yield
            value = add_to(scalars, value, arrived)
            mask *= 2
        return value

    def small_chain():
        total = yield from chain(small, "dp", n_dp)
        own = yield from chain(mine(total[: experts + 2], 1), "tensor", n_tp)
        return total[experts + 2], own

    done = {}

    def advance(name, steps):
        if name not in done:
            try:
                next(steps)
            except StopIteration as end:
                done[name] = end.value

    rows_chain, small_chain = chain(row_dot, "tensor", n_tp), small_chain()
    advance("rows", rows_chain)
    advance("small", small_chain)
    output = output_of(scalars, stream, result_arrived)
    advance("rows", rows_chain)
    advance("small", small_chain)
    keep5, send5 = take5()
    for mask in lower[1:]:
        keep5, send5 = sum_step(keep5, send5, mask)()
    arrived5 = swap(send5, "dp", n_dp, far)
    keep4, send4 = take4()
    given4 = swap(send4, "dp", n_dp, near)
    old = finish(scalars, [keep3[0]], old, lead, shift, experts)
    advance("small", small_chain)
    old = finish(scalars, [given3[0]], old, lead, other_shift, experts)
    advance("small", small_chain)
    while "rows" not in done:
        advance("rows", rows_chain)
    row_dot = done["rows"].reshape(token_count, 1)
    input_grad = final_grad(scalars, dattn, x, factor1, row_dot, gain1, slices_arrived)
    advance("small", small_chain)
    old = finish(scalars, [keep4[0]], old, lead + some, shift, experts)
    while "small" not in done:
        advance("small", small_chain)
    grad_gate, grad_up, grad_down = finish(scalars, [given4[0]], old, lead + some, other_shift, experts)
    head_gains, small = done["small"]
    head_gains = mine(head_gains[: dhead_gains.size].reshape(dhead_gains.shape), 2)
    grad_output = keep5[0, 0].astype(f32) + line.pin(arrived5)[0, 0].astype(f32)
    return (
        output,
        input_grad,
        small[experts + 1],
        grad_qkv[0],
        grad_qkv[1],
        grad_qkv[2],
        head_gains[:, 0],
        head_gains[:, 1],
        grad_output,
        small[experts],
        small[:experts].T,
        grad_gate,
        grad_up,
        grad_down,
    )


def solution(mesh):
    placed = (
        P("dp", "tensor"),
        P("dp", "tensor"),
        P(),
        P(None, "tensor"),
        P(None, "tensor"),
        P(None, "tensor"),
        P("tensor", None),
        P("tensor", None),
        P("tensor", None),
        P(),
        P(),
        P(None, None, "tensor"),
        P(None, None, "tensor"),
        P(None, "tensor", None),
        P("dp", None),
    )
    n_dp, n_tp = mesh.shape["dp"], mesh.shape["tensor"]

    def layer(*args):
        cosine, sine = rope_constants(LEN, args[6].shape[1])
        return body(n_dp, n_tp, jnp.asarray(cosine), jnp.asarray(sine), *args)

    return jax.shard_map(
        layer,
        mesh=mesh,
        in_specs=placed,
        out_specs=(
            P("dp", "tensor"),
            P("dp", "tensor"),
            P("dp"),
            P("dp", "tensor"),
            P("dp", "tensor"),
            P("dp", "tensor"),
            P("tensor", "dp"),
            P("tensor", "dp"),
            P("tensor", "dp"),
            P("dp"),
            P("dp", None),
            P(None, "dp", "tensor"),
            P(None, "dp", "tensor"),
            P(None, "tensor", "dp"),
        ),
        check_vma=False,
    )
```

```python
import functools
import math

import jax
import jax.numpy as jnp
import numpy as np
from jax import lax
from jax.experimental import pallas as pl
from jax.experimental.pallas import tpu as pltpu
from jax.sharding import PartitionSpec as P

LEN = 1024
EPS = 1e-05
ROPE_BASE = 10000.0
VMEM_MIB = 60
TB = 256
MARKS = 4
PARTS = 1
HEAVY = 10**12
f32, bf16 = jnp.float32, jnp.bfloat16
NT = (((1,), (1,)), ((), ()))
TN = (((0,), (0,)), ((), ()))
NN = (((1,), (0,)), ((), ()))


def dot(left, right, dims=NN):
    return lax.dot_general(left, right, dims, preferred_element_type=f32)


def rope_constants(length, width):
    inv_freq = (ROPE_BASE ** (-(np.arange(width // 2, dtype=np.float32) * 2.0) / width)).astype(np.float32)
    angles = np.arange(length, dtype=np.float32)[:, None] * inv_freq[None, :]
    cosine, sine = np.cos(angles).astype(np.float32), np.sin(angles).astype(np.float32)
    return np.concatenate([cosine, cosine], axis=1), np.concatenate([-sine, sine], axis=1)


def bit_reverse(value, count):
    result, bit = 0, 1
    while bit < count:
        result = result * 2 + (value & 1)
        value >>= 1
        bit *= 2
    return result


def whole_spec():
    return pl.BlockSpec(memory_space=pltpu.VMEM)


class Line:
    def __init__(self):
        self.last = []

    def tick(self, axis, count):
        self.sent = swap(self.last[0], axis, count, 1)

    def take(self):
        self.last = [*self.last, self.sent]

    def pin(self, value):
        value, *self.last = lax.optimization_barrier((value, *self.last))
        return value


line = Line()


def call(body, grid, scalars, ins, in_specs, outs, out_specs, scratch=(), aliases=None, vmem=VMEM_MIB):
    deps, n_in, n_out = line.last, len(ins), len(outs)

    def without_deps(scalars, *refs):
        ins_outs = refs[len(deps) : n_in + n_out + len(deps)]
        body(scalars, *ins_outs, *refs[n_in + n_out + len(deps) + MARKS :])

    outs, out_specs = list(outs), list(out_specs)
    any_place = pl.BlockSpec(memory_space=pl.ANY)

    result = pl.pallas_call(
        without_deps,
        out_shape=outs + [struct((8, 128), f32)] * MARKS,
        grid_spec=pltpu.PrefetchScalarGridSpec(
            num_scalar_prefetch=1,
            grid=grid,
            in_specs=[any_place] * len(deps) + list(in_specs),
            out_specs=out_specs + [any_place] * MARKS,
            scratch_shapes=list(scratch),
        ),
        input_output_aliases={1 + len(deps) + k: v for k, v in (aliases or {}).items()},
        compiler_params=pltpu.CompilerParams(vmem_limit_bytes=vmem << 20),
        cost_estimate=pl.CostEstimate(flops=HEAVY, bytes_accessed=1, transcendentals=0),
    )(scalars, *deps, *ins)
    line.last = result[len(outs) :]
    return result[: len(outs)]


def struct(shape, dtype):
    return jax.ShapeDtypeStruct(shape, dtype)


def swap(value, axis, count, mask):
    return lax.ppermute(value, axis, [(i, i ^ mask) for i in range(count)])


def gather_pieces(value, axis, count, pin=lambda v: v):
    if count == 4 and isinstance(value, tuple):
        one, two = (tuple(swap(half, axis, count, mask) for half in value) for mask in (1, 2))
        one, two = pin((one, two))
        return [value, one, two, (swap(two[0], axis, count, 1), swap(one[1], axis, count, 2))]
    if isinstance(value, tuple):
        value = jnp.concatenate(value, axis=0)
    if count == 4:
        half = value.shape[0] // 2
        one, two = swap(value, axis, count, 1), swap(value, axis, count, 2)
        one, two = pin((one, two))
        return [value, one, two, (swap(two[:half], axis, count, 1), swap(one[half:], axis, count, 2))]
    pieces, mask = [value], 1
    while mask < count:
        pieces = pieces + [swap(piece, axis, count, mask) for piece in pieces]
        mask *= 2
    return pieces


def direct_pieces(value, axis, count):
    return [value] + [swap(value, axis, count, r) for r in range(1, count)]


def flat(pieces):
    return [part for piece in pieces for part in (piece if isinstance(piece, tuple) else (piece,))]


def piece_specs(pieces, block, width):
    specs = []
    for piece in pieces:
        if isinstance(piece, tuple):
            count = piece[0].shape[0] // block
            specs.append(pl.BlockSpec((block, width), lambda i, s, n=count: (jnp.minimum(i, n - 1), 0)))
            specs.append(pl.BlockSpec((block, width), lambda i, s, n=count: (jnp.maximum(i - n, 0), 0)))
        else:
            specs.append(pl.BlockSpec((block, width), lambda i, s: (i, 0)))
    return specs


def halved(pieces):
    return [isinstance(piece, tuple) for piece in pieces]


def read_pieces(refs, halves):
    refs, values = list(refs), []
    early = pl.program_id(0) < pl.num_programs(0) // 2
    for in_halves in halves:
        value = refs.pop(0)[...]
        values.append(jnp.where(early, value, refs.pop(0)[...]) if in_halves else value)
    return values


def trade(pieces, axis):
    return lax.all_to_all(pieces, axis, 0, 0, tiled=True)


def halves_kernel(scalars, keep, keep2, arrived, arrived2, keep_out, send_out):
    keep_out[...] = (keep[...].astype(f32) + arrived[...].astype(f32)).astype(bf16)
    send_out[...] = (keep2[...].astype(f32) + arrived2[...].astype(f32)).astype(bf16)


def add_halves(scalars, keep, arrived):
    keep, arrived = line.pin((keep, arrived))
    half = keep.shape[0] // 2
    low = lambda left, right: (left.astype(f32) + right.astype(f32)).astype(bf16)
    out = low(keep[:half], arrived[:half]), low(keep[half:], arrived[half:])
    line.last = [*line.last, out[1]]
    return out


def sum_kernel(scalars, left, right, out):
    out[...] = left[...] + right[...]


def add_to(scalars, left, right):
    whole = pl.BlockSpec(left.shape, lambda i, s: (0, 0))
    return call(sum_kernel, (1,), scalars, [left, right], [whole] * 2, [struct(left.shape, f32)], [whole])[0]


def two_terms(value, width):
    high = value.astype(bf16)
    low = (value - high.astype(f32)).astype(bf16)
    rest = jnp.zeros((value.shape[0], width - 2 * value.shape[1]), bf16)
    return jnp.concatenate([high, low, rest], axis=1)


def transpose_blocks(scalars, first, source, target, dp_count):
    width = source.shape[1] // dp_count
    for place in range(dp_count):
        cols = pl.ds(pl.multiple_of(scalars[first + place] * width, width), width)
        target[place * width : (place + 1) * width, :] = source[:, cols].T


def named_kernel(scalars, ids, *refs):
    *shares, out, shares_out = refs
    for r, share in enumerate(shares):
        shares_out[scalars[r]] = share[...]
    named = jnp.zeros(out.shape, jnp.bool_)
    lanes = lax.broadcasted_iota(jnp.int32, out.shape, 1)
    for choice in range(ids.shape[1]):
        named = named | (ids[:, choice : choice + 1] == lanes)
    out[...] = named.astype(f32)


def kept_kernel(capacity, scalars, named, out):
    tokens = named.shape[0]
    earlier = lax.broadcasted_iota(jnp.int32, (tokens, tokens), 0) > lax.broadcasted_iota(
        jnp.int32, (tokens, tokens), 1
    )
    rank = dot(jnp.where(earlier, 1.0, 0.0).astype(bf16), named[...].astype(bf16))
    out[...] = jnp.where(rank < capacity, named[...], 0.0)


def named_pairs(scalars, expert_ids, shares, experts):
    tokens, chosen = expert_ids.shape
    plain = lambda h, w: pl.BlockSpec((h, w), lambda i, s: (0, 0))
    rows, features = shares[0].shape
    whole = (len(shares), rows, features)
    return call(
        named_kernel,
        (1,),
        scalars,
        [expert_ids, *shares],
        [plain(tokens, chosen)] + [plain(rows, features)] * len(shares),
        [struct((tokens, experts), f32), struct(whole, shares[0].dtype)],
        [plain(tokens, experts), pl.BlockSpec(whole, lambda i, s: (0, 0, 0))],
    )


def kept_pairs(scalars, named, capacity):
    plain = pl.BlockSpec(named.shape, lambda i, s: (0, 0))
    out = [struct(named.shape, f32)]
    return call(functools.partial(kept_kernel, capacity), (1,), scalars, [named], [plain], out, [plain])[0]


def project_kernel(n_tp, halves, heads, scalars, *refs):
    n_in = len(halves) + sum(halves)
    pieces = read_pieces(refs[:n_in], halves)
    gain, wq, wk, wv, q_gain, k_gain, cosine, sine = refs[n_in : n_in + 8]
    x_out, normed_out, factor_out, q_raw, k_raw, q_rot, k_rot, v_out = refs[n_in + 8 :]
    width = pieces[0].shape[1]
    features = width * n_tp
    values = [piece.astype(f32) for piece in pieces]
    squares = sum(jnp.sum(value * value, axis=1, keepdims=True) for value in values)
    factor = lax.rsqrt(squares / features + EPS)
    factor_out[...] = factor
    for r in range(n_tp):
        cols = pl.ds(pl.multiple_of(scalars[r] * width, width), width)
        x_out[:, cols] = pieces[r]
        normed_out[:, cols] = (values[r] * factor * gain[:, cols]).astype(bf16)
    normed = normed_out[...]
    cos, sin = cosine[...], sine[...]
    hd = cos.shape[1]
    for weight, head_gain, raw, rotated in ((wq, q_gain, q_raw, q_rot), (wk, k_gain, k_raw, k_rot)):
        product = dot(normed, weight[...])
        raw[...] = product
        for h in range(heads):
            part = product[:, h * hd : (h + 1) * hd]
            scale = lax.rsqrt(jnp.mean(part * part, axis=1, keepdims=True) + EPS)
            part = part * scale * head_gain[h : h + 1, :]
            part = part * cos + pltpu.roll(part, hd // 2, 1) * sin
            rotated[:, h * hd : (h + 1) * hd] = part.astype(bf16)
    v_out[...] = dot(normed, wv[...]).astype(bf16)


def project(scalars, pieces, gain, wq, wk, wv, q_gain, k_gain, cosine, sine):
    n_tp = len(pieces)
    tokens, width = pieces[0].shape
    features = width * n_tp
    heads, hd = q_gain.shape
    local = heads * hd
    rows = lambda w: pl.BlockSpec((TB, w), lambda i, s: (i, 0))
    return call(
        functools.partial(project_kernel, n_tp, halved(pieces), heads),
        (tokens // TB,),
        scalars,
        [*flat(pieces), gain, wq, wk, wv, q_gain, k_gain, cosine, sine],
        piece_specs(pieces, TB, width) + [whole_spec()] * 6 + [rows(hd)] * 2,
        [
            struct((tokens, features), bf16),
            struct((tokens, features), bf16),
            struct((tokens, 1), f32),
            struct((tokens, local), f32),
            struct((tokens, local), f32),
            struct((tokens, local), bf16),
            struct((tokens, local), bf16),
            struct((tokens, local), bf16),
        ],
        [rows(features), rows(features), rows(1)] + [rows(local)] * 5,
    )


def attend_kernel(block, scalars, q_ref, k_ref, v_ref, top_ref, bottom_ref, total_ref):
    tokens, hd = q_ref.shape
    scale = 1.0 / math.sqrt(hd)
    for i in range(tokens // block):
        rows = slice(i * block, (i + 1) * block)
        reach = (i + 1) * block
        scores = dot(q_ref[rows, :], k_ref[:reach, :], NT) * scale
        at_row = i * block + lax.broadcasted_iota(jnp.int32, scores.shape, 0)
        at_col = lax.broadcasted_iota(jnp.int32, scores.shape, 1)
        scores = jnp.where(at_row >= at_col, scores, -1e30)
        top = jnp.max(scores, axis=1, keepdims=True)
        weights = jnp.exp(scores - top)
        total = jnp.sum(weights, axis=1, keepdims=True)
        probs = (weights * (1.0 / total)).astype(bf16)
        half = tokens // 2
        out_ref, first = (top_ref, 0) if reach <= half else (bottom_ref, half)
        out_ref[i * block - first : reach - first, :] = dot(probs, v_ref[:reach, :]).astype(bf16)
        total_ref[0, rows, :] = top + jnp.log(total)


def attend(scalars, q_rot, k_rot, value, heads):
    tokens, local = q_rot.shape
    hd = local // heads
    column = pl.BlockSpec((tokens, hd), lambda h, s: (0, h))
    return call(
        functools.partial(attend_kernel, min(256, tokens // 2)),
        (heads,),
        scalars,
        [q_rot, k_rot, value],
        [column] * 3,
        [struct((tokens // 2, local), bf16)] * 2 + [struct((heads, tokens, 1), f32)],
        [pl.BlockSpec((tokens // 2, hd), lambda h, s: (0, h))] * 2
        + [pl.BlockSpec((1, tokens, 1), lambda h, s: (h, 0, 0))],
    )


def attend_back_kernel(block, scalars, *refs):
    (q_ref, k_ref, v_ref, go_ref, total_ref, q_raw, k_raw, q_gain, k_gain, cosine, sine) = refs[:11]
    grads_out, dgain_out, dq_acc, dk_acc, dv_acc = refs[11:]
    tokens, hd = q_ref.shape
    scale = 1.0 / math.sqrt(hd)
    count = tokens // block
    for i in reversed(range(count)):
        rows = slice(i * block, (i + 1) * block)
        reach = (i + 1) * block
        query, grad = q_ref[rows, :], go_ref[rows, :]
        scores = dot(query, k_ref[:reach, :], NT) * scale
        at_row = i * block + lax.broadcasted_iota(jnp.int32, scores.shape, 0)
        at_col = lax.broadcasted_iota(jnp.int32, scores.shape, 1)
        scores = jnp.where(at_row >= at_col, scores, -1e30)
        probs = jnp.exp(scores - total_ref[0, rows, :])
        dprobs = dot(grad, v_ref[:reach, :], NT)
        delta = jnp.sum(dprobs * probs, axis=1, keepdims=True)
        dscores = (probs * (dprobs - delta)).astype(bf16)
        dq_acc[rows, :] = dot(dscores, k_ref[:reach, :]) * scale
        dk = dot(dscores, query, TN) * scale
        dv = dot(probs.astype(bf16), grad, TN)
        if i == count - 1:
            dk_acc[...] = dk
            dv_acc[...] = dv
        else:
            dk_acc[:reach, :] += dk
            dv_acc[:reach, :] += dv
    grads_out[2] = dv_acc[...].astype(bf16)
    cos, sin = cosine[...], sine[...]
    dgains = []
    for j, acc, raw_ref, gain_ref in ((0, dq_acc, q_raw, q_gain), (1, dk_acc, k_raw, k_gain)):
        grad = acc[...]
        grad = grad * cos - pltpu.roll(grad, hd // 2, 1) * sin
        raw = raw_ref[...]
        factor = lax.rsqrt(jnp.mean(raw * raw, axis=1, keepdims=True) + EPS)
        normal = raw * factor
        dgains.append(jnp.sum(grad * normal, axis=0, keepdims=True))
        scaled = grad * gain_ref[0]
        mean = jnp.mean(scaled * normal, axis=1, keepdims=True)
        grads_out[j] = (factor * (scaled - normal * mean)).astype(bf16)
    dgain_out[0] = jnp.concatenate(dgains, axis=0)


def attend_back(scalars, q_rot, k_rot, value, grad, totals, q_raw, k_raw, q_gain, k_gain, cosine, sine):
    tokens, local = q_rot.shape
    heads, hd = q_gain.shape
    column = pl.BlockSpec((tokens, hd), lambda h, s: (0, h))
    gain_spec = pl.BlockSpec((1, 1, hd), lambda h, s: (h, 0, 0))
    table = pl.BlockSpec((tokens, hd), lambda h, s: (0, 0))
    return call(
        functools.partial(attend_back_kernel, min(256, tokens)),
        (heads,),
        scalars,
        [q_rot, k_rot, value, grad, totals, q_raw, k_raw, q_gain[:, None, :], k_gain[:, None, :], cosine, sine],
        [column] * 4
        + [pl.BlockSpec((1, tokens, 1), lambda h, s: (h, 0, 0))]
        + [column] * 2
        + [gain_spec] * 2
        + [table] * 2,
        [struct((3, tokens, local), bf16), struct((heads, 2, hd), f32)],
        [
            pl.BlockSpec((3, tokens, hd), lambda h, s: (0, 0, h)),
            pl.BlockSpec((1, 2, hd), lambda h, s: (h, 0, 0)),
        ],
        [pltpu.VMEM((tokens, hd), f32)] * 3,
    )


def whole_first_kernel(n_in, each, base, scalars, *refs):
    pieces, (whole_out, turned_out) = refs[:n_in], refs[n_in:]
    width = pieces[0].shape[1]
    part = width // each
    for r in range(n_in):
        cols = pl.ds(pl.multiple_of(scalars[r] * width, width), width)
        whole_out[:, cols] = pieces[r][...]
        for q in range(each):
            rows = pl.ds(pl.multiple_of(scalars[base + r * each + q] * part, part), part)
            turned_out[rows, :] = pieces[r][:, q * part : (q + 1) * part].T


def whole_last_kernel(scalars, piece, old_whole, old_turned, whole_out, turned_out):
    whole_out[...] = piece[...]
    turned_out[...] = piece[...].T


def whole_first(scalars, pieces, n_tp, dp_count, base):
    tokens, width = pieces[0].shape
    features = width * n_tp
    return call(
        functools.partial(whole_first_kernel, len(pieces), dp_count // n_tp, base),
        (tokens // TB,),
        scalars,
        pieces,
        [pl.BlockSpec((TB, width), lambda i, s: (i, 0))] * len(pieces),
        [struct((tokens, features), bf16), struct((features, tokens), bf16)],
        [
            pl.BlockSpec((TB, features), lambda i, s: (i, 0)),
            pl.BlockSpec((features, TB), lambda i, s: (0, i)),
        ],
    )


def whole_last(scalars, piece, r, whole, turned, dp_count, n_tp, base):
    tokens, width = piece.shape
    each = dp_count // n_tp
    part = width // each
    place = lambda s, q: s[base + r * each + q]
    return call(
        whole_last_kernel,
        (tokens // TB, each),
        scalars,
        [piece, whole, turned],
        [pl.BlockSpec((TB, part), lambda i, q, s: (i, q))] + [pl.BlockSpec(memory_space=pl.ANY)] * 2,
        [struct(whole.shape, bf16), struct(turned.shape, bf16)],
        [
            pl.BlockSpec((TB, part), lambda i, q, s: (i, s[r] * each + q)),
            pl.BlockSpec((part, TB), lambda i, q, s: (place(s, q), i)),
        ],
        aliases={1: 0, 2: 1},
    )


def add_products(total, pieces, weights):
    for piece, weight in zip(pieces, weights):
        total += dot(piece, weight[...].reshape(piece.shape[1], weight.shape[-1]))
    return total


def stream_first_kernel(halves, scalars, x_ref, *refs):
    n_in = len(halves) + sum(halves)
    pieces, weights, out = read_pieces(refs[:n_in], halves), refs[n_in:-1], refs[-1]
    out[...] = add_products(x_ref[...].astype(f32), pieces, weights)


def weight_specs(w_all, places):
    n_dp, _, share, features = w_all.shape
    return [pl.BlockSpec((n_dp, 1, share, features), lambda i, s, r=r: (0, s[r], 0, 0)) for r in places]


def stream_first(scalars, pieces, x, w_all):
    tokens, features = x.shape
    rows = pl.BlockSpec((TB, features), lambda i, s: (i, 0))
    return call(
        functools.partial(stream_first_kernel, halved(pieces)),
        (tokens // TB,),
        scalars,
        [x, *flat(pieces)] + [w_all] * len(pieces),
        [rows] + piece_specs(pieces, TB, flat(pieces)[0].shape[1]) + weight_specs(w_all, range(len(pieces))),
        [struct((tokens, features), f32)],
        [rows],
    )[0]


def stream_kernel(n_tp, halves, dp_count, scalars, *refs):
    n_last, n_in = len(halves), len(halves) + sum(halves)
    pieces = read_pieces(refs[:n_in], halves)
    weights = refs[n_in : n_in + n_last]
    first, gain, router, kept = refs[n_in + n_last : n_in + n_last + 4]
    stream_out, normed_out, mine_out, turned_out, factor_out, probs_out, gates_out = refs[n_in + n_last + 4 :]
    total = add_products(first[...], pieces, weights)
    width = total.shape[1] // n_tp
    stream_out[...] = total
    factor = lax.rsqrt(jnp.mean(total * total, axis=1, keepdims=True) + EPS)
    factor_out[...] = factor
    normed = (total * factor * gain[...]).astype(bf16)
    normed_out[...] = normed
    mine_out[:, :width] = normed_out[:, pl.ds(pl.multiple_of(scalars[0] * width, width), width)]
    logits = dot(normed, router[...])
    power = jnp.exp(logits - jnp.max(logits, axis=1, keepdims=True))
    probs = power / jnp.sum(power, axis=1, keepdims=True)
    probs_out[...] = probs
    gates = probs * kept[...]
    gates_out[...] = gates
    mine_out[:, width:] = two_terms(gates, mine_out.shape[1] - width)
    transpose_blocks(scalars, n_tp, normed_out, turned_out, dp_count)


def stream_of(scalars, pieces, first, w_all, gain, router, kept, n_tp, dp_count):
    tokens, features = first.shape
    experts = router.shape[1]
    width = features // n_tp
    rows = lambda w: pl.BlockSpec((TB, w), lambda i, s: (i, 0))
    places = range(n_tp - len(pieces), n_tp)
    return call(
        functools.partial(stream_kernel, n_tp, halved(pieces), dp_count),
        (tokens // TB,),
        scalars,
        [*flat(pieces)] + [w_all] * len(pieces) + [first, gain, router, kept],
        piece_specs(pieces, TB, flat(pieces)[0].shape[1])
        + weight_specs(w_all, places)
        + [rows(features), whole_spec(), whole_spec(), rows(experts)],
        [
            struct((tokens, features), f32),
            struct((tokens, features), bf16),
            struct((tokens, width + 128), bf16),
            struct((features, tokens), bf16),
            struct((tokens, 1), f32),
            struct((tokens, experts), f32),
            struct((tokens, experts), f32),
        ],
        [
            rows(features),
            rows(features),
            rows(width + 128),
            pl.BlockSpec((features, TB), lambda i, s: (0, i)),
            rows(1),
            rows(experts),
            rows(experts),
        ],
    )


def expert_kernel(first, shift, scalars, n_ref, g_ref, gates_ref, wg, wu, wd, hidden_out, pair_out, dgate_out):
    step = pl.program_id(0)
    expert = first + step + (0 if shift is None else scalars[shift])
    width = wg.shape[-1]

    @pl.when(step == 0)
    def _():
        dgate_out[...] = jnp.zeros_like(dgate_out)

    gate_val, up_val = dot(n_ref[...], wg[0]), dot(n_ref[...], wu[0])
    back = dot(g_ref[...], wd[0], NT)
    gates = gates_ref[...]
    here = lax.broadcasted_iota(jnp.int32, gates.shape, 1) == expert
    gate = jnp.sum(jnp.where(here, gates, 0.0), axis=1, keepdims=True)
    sigmoid = 1.0 / (1.0 + jnp.exp(-gate_val))
    swish = gate_val * sigmoid
    hidden = (swish * up_val).astype(bf16).astype(f32)
    hidden_out[0] = (hidden * gate).astype(bf16)
    dgate = jnp.sum(back * hidden, axis=1, keepdims=True)
    dgate_out[...] = jnp.where(here, dgate, dgate_out[...])
    dhidden = back * gate
    pair_out[0, :, :width] = (dhidden * up_val * sigmoid * (1.0 + gate_val * (1.0 - sigmoid))).astype(bf16)
    pair_out[0, :, width:] = (dhidden * swish).astype(bf16)


def run_experts(scalars, normed, grad, gates, wg, wu, wd, first, count, shift=None):
    tokens, features = normed.shape
    experts, _, width = wg.shape
    place = lambda i, s: first + i + (0 if shift is None else s[shift])
    weight = lambda shape: pl.BlockSpec((1, *shape), lambda i, s: (place(i, s), 0, 0))
    given = lambda shape: pl.BlockSpec((1, *shape), lambda i, s: (i, 0, 0))
    return call(
        functools.partial(expert_kernel, first, shift),
        (count,),
        scalars,
        [normed, grad, gates, wg, wu, wd],
        [whole_spec()] * 3 + [weight((features, width))] * 2 + [weight((width, features))],
        [
            struct((count, tokens, width), bf16),
            struct((count, tokens, 2 * width), bf16),
            struct((tokens, experts), f32),
        ],
        [
            given((tokens, width)),
            given((tokens, 2 * width)),
            pl.BlockSpec((tokens, experts), lambda i, s: (0, 0)),
        ],
    )


def weight_grads_kernel(scalars, turned, g_turned, hidden, pair, keep_out, send_out):
    half, _, rows, _ = keep_out.shape
    width = hidden.shape[-1]
    first = dot(turned[...], pair[0]).astype(bf16).reshape(2 * half, rows, 2 * width)
    keep_out[:, 0, :, : 2 * width] = first[:half]
    send_out[:, 0, :, : 2 * width] = first[half:]
    second = dot(g_turned[...], hidden[0]).astype(bf16).reshape(2 * half, rows, width)
    keep_out[:, 0, :, 2 * width :] = second[:half]
    send_out[:, 0, :, 2 * width :] = second[half:]


def weight_grads(scalars, turned, g_turned, hidden, pair, offset, count, dp_count):
    features, tokens = turned.shape
    width = hidden.shape[-1]
    half, rows = dp_count // 2, features // dp_count
    out = struct((half, count, rows, 3 * width), bf16)
    out_spec = pl.BlockSpec((half, 1, rows, 3 * width), lambda i, s: (0, i, 0, 0))
    return call(
        weight_grads_kernel,
        (count,),
        scalars,
        [turned, g_turned, hidden, pair],
        [
            whole_spec(),
            whole_spec(),
            pl.BlockSpec((1, tokens, width), lambda i, s: (offset + i, 0, 0)),
            pl.BlockSpec((1, tokens, 2 * width), lambda i, s: (offset + i, 0, 0)),
        ],
        [out, out],
        [out_spec, out_spec],
    )


def inner_swap(index):
    return (index & ~3) | ((index & 1) << 1) | ((index >> 1) & 1)


def shared_grads_kernel(scalars, *refs):
    turned, turned2, g_turned, g_turned2, hidden, hidden2, pair, pair2, keep_out, send_out = refs
    half, _, rows, _ = keep_out.shape
    width = hidden.shape[-1]
    first = dot(turned[...], pair[0]) + dot(turned2[...], pair2[0])
    first = first.astype(bf16).reshape(2 * half, rows, 2 * width)
    second = dot(g_turned[...], hidden[0]) + dot(g_turned2[...], hidden2[0])
    second = second.astype(bf16).reshape(2 * half, rows, width)
    for out, base in ((keep_out, 0), (send_out, half)):
        for place in range(half):
            out[inner_swap(place), 0, :, : 2 * width] = first[base + place]
            out[inner_swap(place), 0, :, 2 * width :] = second[base + place]


def shared_grads(scalars, turned, turned2, g_turned, g_turned2, hidden, hidden2, pair, pair2, shift, base, offset, count,
                 dp_count):
    features, tokens = turned.shape
    width = hidden2.shape[-1]
    half, rows = dp_count // 2, features // dp_count
    out = struct((half, count, rows, 3 * width), bf16)
    out_spec = pl.BlockSpec((half, 1, rows, 3 * width), lambda i, s: (0, i, 0, 0))
    mine = lambda w: pl.BlockSpec((1, tokens, w), lambda i, s: (base + s[shift] + offset + i, 0, 0))
    other = lambda w: pl.BlockSpec((1, tokens, w), lambda i, s: (offset + i, 0, 0))
    return call(
        shared_grads_kernel,
        (count,),
        scalars,
        [turned, turned2, g_turned, g_turned2, hidden, hidden2, pair, pair2],
        [whole_spec()] * 4 + [mine(width), other(width), mine(2 * width), other(2 * width)],
        [out, out],
        [out_spec, out_spec],
    )


def finish_kernel(n_parts, n_old, scalars, *refs):
    parts = refs[:n_parts]
    gate_out, up_out, down_out = refs[n_parts + n_old :]
    width = gate_out.shape[-1]
    total = sum(part[0].astype(f32) for part in parts)
    gate_out[0] = total[:, :width]
    up_out[0] = total[:, width : 2 * width]
    down_out[0] = total[:, 2 * width :].T


def finish(scalars, parts, old, first, shift, experts):
    count, rows, wide = parts[0].shape
    width = wide // 3
    place = lambda i, s: (first + i + (0 if shift is None else s[shift]), 0, 0)
    spec = pl.BlockSpec((1, rows, width), place)
    down_spec = pl.BlockSpec((1, width, rows), place)
    return call(
        functools.partial(finish_kernel, len(parts), len(old)),
        (count,),
        scalars,
        [*parts, *old],
        [pl.BlockSpec((1, rows, wide), lambda i, s: (i, 0, 0))] * len(parts)
        + [pl.BlockSpec(memory_space=pl.ANY)] * len(old),
        [struct((experts, rows, width), f32)] * 2 + [struct((experts, width, rows), f32)],
        [spec, spec, down_spec],
        aliases={len(parts) + k: k for k in range(len(old))},
    )


def chunk_specs(chunks, shape):
    specs, first = [], 0
    for chunk in chunks:
        count = chunk.shape[0]
        specs.append(
            pl.BlockSpec(
                (1, *shape), lambda i, s, first=first, count=count: (jnp.clip(i - first, 0, count - 1), 0, 0)
            )
        )
        first += count
    return specs


def input_grad_kernel(sizes, n_tp, scalars, *refs):
    n = len(sizes)
    pairs, (wg, wu), dgates = refs[:n], refs[n : n + 2], refs[n + 2 : 2 * n + 2]
    out, acc = refs[-2:]
    step = pl.program_id(0)
    width = wg.shape[-1]
    first = 0
    for pair, size in zip(pairs, sizes):

        def product(pair=pair):
            return dot(pair[0, :, :width], wg[0], NT) + dot(pair[0, :, width:], wu[0], NT)

        if first == 0:

            @pl.when(step == 0)
            def _(product=product):
                acc[...] = product()

        @pl.when((step >= max(first, 1)) & (step < first + size))
        def _(product=product):
            acc[...] += product()

        first += size

    @pl.when(step == pl.num_programs(0) - 1)
    def _():
        rows, features = acc.shape[0] // n_tp, acc.shape[1]
        for k in range(n_tp):
            place = slice(k * rows, (k + 1) * rows)
            out[k, :, :features] = acc[place, :].astype(bf16)
            dgate = sum(ref[place, :] for ref in dgates)
            out[k, :, features:] = two_terms(dgate, out.shape[2] - features)


def input_grads(scalars, pairs, wg, wu, dgates, n_tp):
    experts, features, width = wg.shape
    tokens = pairs[0].shape[1]
    rows = tokens // n_tp
    weight = pl.BlockSpec((1, features, width), lambda i, s: (i, 0, 0))
    return call(
        functools.partial(input_grad_kernel, [pair.shape[0] for pair in pairs], n_tp),
        (experts,),
        scalars,
        [*pairs, wg, wu, *dgates],
        chunk_specs(pairs, (tokens, 2 * width)) + [weight] * 2 + [whole_spec()] * len(dgates),
        [struct((n_tp, rows, features + 128), bf16)],
        [pl.BlockSpec((n_tp, rows, features + 128), lambda i, s: (0, 0, 0))],
        [pltpu.VMEM((tokens, features), f32)],
    )


def result_kernel(sizes, n_tp, scalars, *refs):
    hiddens, wd = refs[: len(sizes)], refs[len(sizes)]
    out, acc = refs[-2:]
    step = pl.program_id(0)
    first = 0
    for hidden, size in zip(hiddens, sizes):

        if first == 0:

            @pl.when(step == 0)
            def _(hidden=hidden):
                acc[...] = dot(hidden[0], wd[0])

        @pl.when((step >= max(first, 1)) & (step < first + size))
        def _(hidden=hidden):
            acc[...] += dot(hidden[0], wd[0])

        first += size

    @pl.when(step == pl.num_programs(0) - 1)
    def _():
        cols = acc.shape[1] // n_tp
        for k in range(n_tp):
            out[k] = acc[:, k * cols : (k + 1) * cols].astype(bf16)


def results(scalars, hiddens, wd, n_tp):
    experts, width, features = wd.shape
    tokens = hiddens[0].shape[1]
    cols = features // n_tp
    return call(
        functools.partial(result_kernel, [hidden.shape[0] for hidden in hiddens], n_tp),
        (experts,),
        scalars,
        [*hiddens, wd],
        chunk_specs(hiddens, (tokens, width)) + [pl.BlockSpec((1, width, features), lambda i, s: (i, 0, 0))],
        [struct((n_tp, tokens, cols), bf16)],
        [pl.BlockSpec((n_tp, tokens, cols), lambda i, s: (0, 0, 0))],
        [pltpu.VMEM((tokens, features), f32)],
    )


def rows_kernel(n_tp, scalars, *refs):
    parts, probs, kept, stream, normed, factor, upstream, gain, router = refs[:9]
    grad_out, dgain_out, drouter_out = refs[9:]
    features, experts = router.shape
    total = sum(parts[k, :, :features].astype(f32) for k in range(n_tp))
    both = sum(parts[k, :, features:].astype(f32) for k in range(n_tp))
    dprobs = (both[:, :experts] + both[:, experts : 2 * experts]) * kept[...]
    soft = probs[...]
    dlogits = soft * (dprobs - jnp.sum(dprobs * soft, axis=1, keepdims=True))
    dlogits = dlogits.astype(bf16)
    drouter_out[...] = dot(normed[...], dlogits, TN)
    total += dot(dlogits, router[...], NT)
    scale = factor[...]
    normal = stream[...] * scale
    dgain_out[...] = jnp.sum(total * normal, axis=0, keepdims=True)
    scaled = total * gain[...]
    mean = jnp.mean(scaled * normal, axis=1, keepdims=True)
    grad_out[...] = (upstream[...].astype(f32) + scale * (scaled - normal * mean)).astype(bf16)


def stream_grad_rows(scalars, parts, probs, kept, stream, normed, factor, upstream, gain, router):
    n_tp, rows, _ = parts.shape
    features, experts = router.shape
    mine = lambda w: pl.BlockSpec((rows, w), lambda i, s: (s[0], 0))
    plain = lambda h, w: pl.BlockSpec((h, w), lambda i, s: (0, 0))
    return call(
        functools.partial(rows_kernel, n_tp),
        (1,),
        scalars,
        [parts, probs, kept, stream, normed, factor, upstream, gain, router],
        [pl.BlockSpec(parts.shape, lambda i, s: (0, 0, 0))]
        + [mine(experts), mine(experts), mine(features), mine(features), mine(1), mine(features)]
        + [plain(1, features), plain(features, experts)],
        [struct((rows, features), bf16), struct((1, features), f32), struct((features, experts), f32)],
        [plain(rows, features), plain(1, features), plain(features, experts)],
    )


def attended_grad_kernel(scalars, grad, w_ref, out):
    out[...] = dot(grad[...], w_ref[...], NT).astype(bf16)


def attended_grad(scalars, grad, w_output):
    tokens, features = grad.shape
    local = w_output.shape[0]
    rows = lambda w: pl.BlockSpec((tokens // 2, w), lambda i, s: (i, 0))
    return call(
        attended_grad_kernel,
        (2,),
        scalars,
        [grad, w_output],
        [rows(features), whole_spec()],
        [struct((tokens, local), bf16)],
        [rows(local)],
    )[0]


def normed_grad_kernel(scalars, grads, wq, wk, wv, x_ref, factor, gain, out, dot_out, dgain_out):
    total = sum(dot(grads[j], weight[...], NT) for j, weight in enumerate((wq, wk, wv)))
    out[0] = total.astype(bf16)
    normal = x_ref[...].astype(f32) * factor[...]
    product = total * normal
    dgain_out[...] = jnp.sum(product, axis=0, keepdims=True)
    part = jnp.sum(product * gain[...], axis=1, keepdims=True)

    @pl.when(pl.program_id(0) == 0)
    def _():
        dot_out[...] = part

    @pl.when(pl.program_id(0) > 0)
    def _():
        dot_out[...] += part


def normed_grad(scalars, grads, wq, wk, wv, x, factor, gain, n_tp):
    _, tokens, local = grads.shape
    features = wq.shape[0]
    width = features // n_tp
    weight = pl.BlockSpec((width, local), lambda i, s: (i, 0))
    column = lambda h: pl.BlockSpec((h, width), lambda i, s: (0, i))
    whole = pl.BlockSpec((tokens, 1), lambda i, s: (0, 0))
    return call(
        normed_grad_kernel,
        (n_tp,),
        scalars,
        [grads, wq, wk, wv, x, factor, gain],
        [pl.BlockSpec(grads.shape, lambda i, s: (0, 0, 0))] + [weight] * 3 + [column(tokens), whole, column(1)],
        [struct((n_tp, tokens, width), bf16), struct((tokens, 1), f32), struct((1, features), f32)],
        [pl.BlockSpec((1, tokens, width), lambda i, s: (i, 0, 0)), whole, column(1)],
    )


def head_weight_grads(scalars, turned, grads, dp_count):
    features, tokens = turned.shape
    count, _, local = grads.shape
    half, rows = dp_count // 2, features // dp_count

    def kernel(scalars, turned, grad, keep_out, send_out):
        product = dot(turned[...], grad[0]).astype(bf16).reshape(2 * half, rows, local)
        keep_out[:, 0] = product[:half]
        send_out[:, 0] = product[half:]

    block = pl.BlockSpec((half, 1, rows, local), lambda i, s: (0, i, 0, 0))
    return call(
        kernel,
        (count,),
        scalars,
        [turned, grads],
        [whole_spec(), pl.BlockSpec((1, tokens, local), lambda i, s: (i, 0, 0))],
        [struct((half, count, rows, local), bf16)] * 2,
        [block] * 2,
    )


def output_weight_grads(scalars, top, bottom, grad, first, dp_count):
    half, local = top.shape
    width = grad.shape[1] // dp_count

    def kernel(scalars, top, bottom, keep, send, keep_out, send_out):
        for grad, out in ((keep, keep_out), (send, send_out)):
            product = dot(top[...], grad[:half, :], TN) + dot(bottom[...], grad[half:, :], TN)
            out[0, 0] = product.astype(bf16)

    column = lambda base: pl.BlockSpec((2 * half, width), lambda i, s: (0, s[base + i]))
    block = pl.BlockSpec((1, 1, local, width), lambda i, s: (i, 0, 0, 0))
    return call(
        kernel,
        (dp_count // 2,),
        scalars,
        [top, bottom, grad, grad],
        [whole_spec(), whole_spec(), column(first), column(first + dp_count // 2)],
        [struct((dp_count // 2, 1, local, width), bf16)] * 2,
        [block] * 2,
    )


def turn_kernel(first, dp_count, scalars, source, target):
    transpose_blocks(scalars, first, source, target, dp_count)


def turn(scalars, value, n_tp, dp_count):
    tokens, features = value.shape
    return call(
        functools.partial(turn_kernel, n_tp, dp_count),
        (tokens // TB,),
        scalars,
        [value],
        [pl.BlockSpec((TB, features), lambda i, s: (i, 0))],
        [struct((features, tokens), bf16)],
        [pl.BlockSpec((features, TB), lambda i, s: (0, i))],
    )[0]


def output_kernel(scalars, stream, parts, out):
    out[...] = (stream[...] + sum(parts[k].astype(f32) for k in range(parts.shape[0]))).astype(bf16)


def output_of(scalars, stream, parts):
    n_tp, tokens, width = parts.shape
    return call(
        output_kernel,
        (tokens // TB,),
        scalars,
        [stream, parts],
        [
            pl.BlockSpec((TB, width), lambda i, s: (i, s[0])),
            pl.BlockSpec((n_tp, TB, width), lambda i, s: (0, i, 0)),
        ],
        [struct((tokens, width), bf16)],
        [pl.BlockSpec((TB, width), lambda i, s: (i, 0))],
    )[0]


def final_kernel(features, scalars, dattn, x_ref, factor, row_dot, gain, parts, out):
    total = sum(parts[k].astype(f32) for k in range(parts.shape[0]))
    scale = factor[...]
    normal = x_ref[...].astype(f32) * scale
    back = scale * (total * gain[...] - normal * (row_dot[...] / features))
    out[...] = (dattn[...].astype(f32) + back).astype(bf16)


def final_grad(scalars, dattn, x, factor, row_dot, gain, parts):
    n_tp, tokens, width = parts.shape
    plain = lambda w: pl.BlockSpec((TB, w), lambda i, s: (i, 0))
    mine = pl.BlockSpec((TB, width), lambda i, s: (i, s[0]))
    return call(
        functools.partial(final_kernel, dattn.shape[1]),
        (tokens // TB,),
        scalars,
        [dattn, x, factor, row_dot, gain, parts],
        [mine, mine, plain(1), plain(1), pl.BlockSpec((1, width), lambda i, s: (0, s[0]))]
        + [pl.BlockSpec((n_tp, TB, width), lambda i, s: (0, i, 0))],
        [struct((tokens, width), bf16)],
        [plain(width)],
    )[0]


def final_sum_kernel(scalars, left, right, out):
    out[...] = left[...].astype(f32) + right[...].astype(f32)


def final_sum(scalars, left, right):
    count, rows, width = left.shape
    block = pl.BlockSpec((1, rows, width), lambda i, s: (i, 0, 0))
    return call(
        final_sum_kernel, (count,), scalars, [left, right], [block] * 2, [struct(left.shape, f32)], [block]
    )[0]


def body(n_dp, n_tp, cosine, sine, tokens, cotangent, attn_gain, w_query, w_key, w_value, query_gain, key_gain,
         w_output, ffn_gain, w_router, w_gate, w_up, w_down, expert_ids):
    tp, dp = lax.axis_index("tensor"), lax.axis_index("dp")
    far, near = n_dp // 2, n_dp // 4
    side = (dp // near) % 2
    token_count, width = tokens.shape
    features = width * n_tp
    heads, hd = query_gain.shape
    local = heads * hd
    experts = w_router.shape[1]
    capacity = token_count * expert_ids.shape[1] // experts
    gain1, gain2 = attn_gain[None, :], ffn_gain[None, :]
    blocks = (2, 3, 3)
    lead = sum(blocks)
    shared = (experts - lead) // 2
    shift, other_shift = n_tp + n_dp, n_tp + n_dp + 1
    each = n_dp // n_tp
    scalars = jnp.stack(
        [tp ^ r for r in range(n_tp)]
        + [dp ^ bit_reverse(place, n_dp) for place in range(n_dp)]
        + [side * shared, (1 - side) * shared]
        + [bit_reverse(((tp ^ r) * each + q) ^ dp, n_dp) for r in range(n_tp) for q in range(each)]
    ).astype(jnp.int32)
    turned_base = n_tp + n_dp + 2

    line.last = []

    share = local // n_dp
    w_share = lax.dynamic_slice_in_dim(w_output, dp * share, share, 0)
    w_shares = direct_pieces(w_share, "tensor", n_tp)

    named, w_some = named_pairs(scalars, expert_ids, w_shares, experts)
    w_all = lax.all_gather(w_some, "dp")
    x_pieces = gather_pieces(tokens, "tensor", n_tp, pin=line.pin)
    kept = kept_pairs(scalars, named, capacity)
    x_pieces, g_mine = lax.optimization_barrier((x_pieces, cotangent))
    early = n_tp - 1 if n_tp == 4 else n_tp // 2
    g_pieces = [g_mine] + [swap(g_mine, "tensor", n_tp, r) for r in range(1, early)]
    x, normed1, factor1, q_raw, k_raw, q_rot, k_rot, value = project(
        scalars, x_pieces, gain1, w_query, w_key, w_value, query_gain, key_gain, cosine, sine
    )
    *attended, totals = attend(scalars, q_rot, k_rot, value, heads)
    attended, g_pieces = lax.optimization_barrier((tuple(attended), g_pieces))
    upstream, g_turned = whole_first(scalars, g_pieces, n_tp, n_dp, turned_base)
    turned1 = turn(scalars, normed1, n_tp, n_dp)
    attended_pieces = gather_pieces(attended, "tensor", n_tp, pin=line.pin)
    stream = stream_first(scalars, attended_pieces[:early], x, w_all)
    g_mine = line.pin(g_mine)
    g_last = [swap(g_mine, "tensor", n_tp, r) for r in range(early, n_tp)]
    g_near = swap(g_mine, "dp", n_dp, near)
    stream, normed2, normed2_mine, turned, factor2, probs, gates = stream_of(
        scalars, attended_pieces[early:], stream, w_all, gain2, w_router, kept, n_tp, n_dp
    )
    for r in range(early, n_tp):
        upstream, g_turned = whole_last(
            scalars, g_last[r - early], r, upstream, g_turned, n_dp, n_tp, turned_base
        )
    normed_near = swap(normed2_mine, "dp", n_dp, near)
    g_near, _ = lax.optimization_barrier((g_near, upstream))
    upstream_near = lax.all_gather(g_near, "tensor", axis=1, tiled=True)
    gates_near = normed_near[:, width : width + experts].astype(f32)
    gates_near += normed_near[:, width + experts : width + 2 * experts].astype(f32)
    normed2_near = lax.all_gather(normed_near[:, :width], "tensor", axis=1, tiled=True)

    hiddens, pairs, dgates = [], [], []

    def run(first, count):
        out = run_experts(scalars, normed2, upstream, gates, w_gate, w_up, w_down, first, count)
        for kind, array in zip((hiddens, pairs, dgates), out):
            kind.append(array)

    def sum_step(keep, send, mask):
        arrived = swap(send, "dp", n_dp, mask)
        return lambda: add_halves(scalars, keep, arrived)

    lower = [mask for mask in (2, 4, 8, 16) if mask < far]

    def own_sums(index):
        keep, send = weight_grads(scalars, turned, g_turned, hiddens[index], pairs[index], 0, blocks[index], n_dp)
        return sum_step(keep, send, 1)

    def next_step(take):
        return sum_step(*take(), lower[0])

    def last_step(take):
        keep, send = take()
        for mask in lower[1:]:
            keep, send = sum_step(keep, send, mask)()
        return [keep[0], swap(send, "dp", n_dp, far)[0]]

    def complete(parts, old, index):
        return finish(scalars, parts, old, sum(blocks[:index]), None, experts)

    run(0, blocks[0])
    take0 = own_sums(0)
    run(blocks[0], blocks[1])
    take0 = next_step(take0)
    take1 = own_sums(1)
    run(blocks[0] + blocks[1], blocks[2])
    parts0 = last_step(take0)
    take1 = next_step(take1)
    line.tick("dp", n_dp)
    run(sum(blocks[:3]), experts - sum(blocks[:3]))
    line.take()
    take2 = own_sums(2)
    g_turned_near = turn(scalars, upstream_near, n_tp, n_dp)
    old = complete(parts0, [], 0)
    take2 = next_step(take2)
    line.tick("dp", n_dp)
    parts1 = last_step(take1)
    line.take()
    input_parts = input_grads(scalars, pairs, w_gate, w_up, dgates, n_tp)[0]
    input_arrived = trade(input_parts, "tensor")
    line.tick("dp", n_dp)
    turned_near = turn(scalars, normed2_near, n_tp, n_dp)
    line.take()
    hidden_near, pair_near, _ = run_experts(
        scalars, normed2_near, upstream_near, gates_near, w_gate, w_up, w_down, lead, shared, shift
    )
    line.tick("dp", n_dp)
    parts2 = last_step(take2)
    line.take()

    def shared_sums(offset, count):
        keep, send = shared_grads(
            scalars, turned, turned_near, g_turned, g_turned_near, hiddens[3], hidden_near, pairs[3], pair_near,
            shift, 0, offset, count, n_dp,
        )
        return sum_step(keep, send, 1)

    def shared_next(take):
        keep, send = take()
        for mask in lower:
            if mask != near:
                keep, send = sum_step(keep, send, mask)()
        return sum_step(keep, send, far)

    some = (shared + 1) // 2
    take3 = shared_sums(0, some)
    dattn_rows, dgain2, drouter = stream_grad_rows(
        scalars, input_arrived, probs, kept, stream, normed2, factor2, upstream, gain2, w_router
    )
    dattn = lax.all_gather(dattn_rows, "tensor", axis=0, tiled=True)
    take3 = shared_next(take3)
    line.tick("dp", n_dp)
    old = complete(parts1, old, 1)
    line.take()
    take4 = shared_sums(some, shared - some)
    result_parts = results(scalars, hiddens, w_down, n_tp)[0]
    take4 = shared_next(take4)

    take5 = sum_step(*output_weight_grads(scalars, *attended, dattn, n_tp, n_dp), 1)
    line.tick("dp", n_dp)
    dattended = attended_grad(scalars, dattn, w_output)
    result_arrived = trade(line.pin(result_parts), "tensor")
    line.take()
    take5 = sum_step(*take5(), lower[0])
    grads, dhead_gains = attend_back(
        scalars, q_rot, k_rot, value, dattended, totals, q_raw, k_raw, query_gain, key_gain, cosine, sine
    )
    take6 = sum_step(*head_weight_grads(scalars, turned1, grads, n_dp), 1)
    line.tick("dp", n_dp)
    old = complete(parts2, old, 2)
    line.take()
    take6 = sum_step(*take6(), lower[0])
    slices, row_dot, dgain1 = normed_grad(scalars, grads, w_query, w_key, w_value, x, factor1, gain1, n_tp)
    slices_arrived = trade(slices, "tensor")

    own_heads = jnp.moveaxis(dhead_gains.reshape(heads, 2, n_dp, hd // n_dp), 2, 0).reshape(n_dp, -1)
    flat_heads = jnp.pad(own_heads, ((0, 0), (0, features // n_dp - own_heads.shape[1]))).reshape(1, -1)
    small = jnp.concatenate([drouter.T, dgain2, dgain1, flat_heads], axis=0)
    small = lax.psum_scatter(small, "dp", scatter_dimension=1, tiled=True)
    row_dot = row_dot.reshape(8, token_count // 8)

    def chain(value, axis, count):
        mask = 1
        while mask < count:
            arrived = swap(value, axis, count, mask)
            yield
            value = add_to(scalars, value, arrived)
            mask *= 2
        return value

    done = {}

    def advance(name, steps):
        if name not in done:
            try:
                next(steps)
            except StopIteration as end:
                done[name] = end.value

    def rest(take):
        keep, send = take()
        for mask in lower[1:]:
            keep, send = sum_step(keep, send, mask)()
        return keep, swap(send, "dp", n_dp, far)

    rows_chain = chain(row_dot, "tensor", n_tp)
    advance("rows", rows_chain)
    output = output_of(scalars, stream, result_arrived)
    advance("rows", rows_chain)
    keep3, send3 = take3()
    given3 = swap(send3, "dp", n_dp, near)
    keep4, send4 = take4()
    given4 = swap(send4, "dp", n_dp, near)
    old = finish(scalars, [keep3[0]], old, lead, shift, experts)
    keep5, arrived5 = rest(take5)
    keep6, arrived6 = rest(take6)
    line.tick("dp", n_dp)
    old = finish(scalars, [keep4[0]], old, lead + some, shift, experts)
    line.take()
    while "rows" not in done:
        advance("rows", rows_chain)
    row_dot = done["rows"].reshape(token_count, 1)
    head_gains = small[experts + 2, : own_heads.shape[1]].reshape(heads, 2, hd // n_dp)
    sums_chain = chain(small[: experts + 2], "tensor", n_tp)
    advance("sums", sums_chain)
    input_grad = final_grad(scalars, dattn, x, factor1, row_dot, gain1, slices_arrived)
    advance("sums", sums_chain)
    old = finish(scalars, [given3[0]], old, lead, other_shift, experts)
    while "sums" not in done:
        advance("sums", sums_chain)
    small = done["sums"]
    grad_output = final_sum(scalars, keep5[0], arrived5[0])[0]
    grad_gate, grad_up, grad_down = finish(scalars, [given4[0]], old, lead + some, other_shift, experts)
    grad_qkv = final_sum(scalars, keep6[0], arrived6[0])
    return (
        output,
        input_grad,
        small[experts + 1],
        grad_qkv[0],
        grad_qkv[1],
        grad_qkv[2],
        head_gains[:, 0],
        head_gains[:, 1],
        grad_output,
        small[experts],
        small[:experts].T,
        grad_gate,
        grad_up,
        grad_down,
    )


def solution(mesh):
    placed = (
        P("dp", "tensor"),
        P("dp", "tensor"),
        P(),
        P(None, "tensor"),
        P(None, "tensor"),
        P(None, "tensor"),
        P("tensor", None),
        P("tensor", None),
        P("tensor", None),
        P(),
        P(),
        P(None, None, "tensor"),
        P(None, None, "tensor"),
        P(None, "tensor", None),
        P("dp", None),
    )
    n_dp, n_tp = mesh.shape["dp"], mesh.shape["tensor"]

    def layer(*args):
        cosine, sine = rope_constants(LEN, args[6].shape[1])
        return body(n_dp, n_tp, jnp.asarray(cosine), jnp.asarray(sine), *args)

    return jax.shard_map(
        layer,
        mesh=mesh,
        in_specs=placed,
        out_specs=(
            P("dp", "tensor"),
            P("dp", "tensor"),
            P("dp"),
            P("dp", "tensor"),
            P("dp", "tensor"),
            P("dp", "tensor"),
            P("tensor", "dp"),
            P("tensor", "dp"),
            P("tensor", "dp"),
            P("dp"),
            P("dp", None),
            P(None, "dp", "tensor"),
            P(None, "dp", "tensor"),
            P(None, "tensor", "dp"),
        ),
        check_vma=False,
    )
```

```python
import functools
import math

import jax
import jax.numpy as jnp
import numpy as np
from jax import lax
from jax.experimental import pallas as pl
from jax.experimental.pallas import tpu as pltpu
from jax.sharding import PartitionSpec as P

LEN = 1024
EPS = 1e-05
ROPE_BASE = 10000.0
VMEM_MIB = 60
TB = 256
MARKS = 4
PARTS = 1
HEAVY = 10**12
f32, bf16 = jnp.float32, jnp.bfloat16
NT = (((1,), (1,)), ((), ()))
TN = (((0,), (0,)), ((), ()))
NN = (((1,), (0,)), ((), ()))


def dot(left, right, dims=NN):
    return lax.dot_general(left, right, dims, preferred_element_type=f32)


def rope_constants(length, width):
    inv_freq = (ROPE_BASE ** (-(np.arange(width // 2, dtype=np.float32) * 2.0) / width)).astype(np.float32)
    angles = np.arange(length, dtype=np.float32)[:, None] * inv_freq[None, :]
    cosine, sine = np.cos(angles).astype(np.float32), np.sin(angles).astype(np.float32)
    return np.concatenate([cosine, cosine], axis=1), np.concatenate([-sine, sine], axis=1)


def bit_reverse(value, count):
    result, bit = 0, 1
    while bit < count:
        result = result * 2 + (value & 1)
        value >>= 1
        bit *= 2
    return result


def whole_spec():
    return pl.BlockSpec(memory_space=pltpu.VMEM)


class Line:
    def __init__(self):
        self.last = []

    def tick(self, axis, count):
        self.sent = swap(self.last[0], axis, count, 1)

    def take(self):
        self.last = [*self.last, self.sent]

    def pin(self, value):
        value, *self.last = lax.optimization_barrier((value, *self.last))
        return value


line = Line()


def call(body, grid, scalars, ins, in_specs, outs, out_specs, scratch=(), aliases=None, vmem=VMEM_MIB):
    deps, n_in, n_out = line.last, len(ins), len(outs)

    def without_deps(scalars, *refs):
        ins_outs = refs[len(deps) : n_in + n_out + len(deps)]
        body(scalars, *ins_outs, *refs[n_in + n_out + len(deps) + MARKS :])

    outs, out_specs = list(outs), list(out_specs)
    any_place = pl.BlockSpec(memory_space=pl.ANY)

    result = pl.pallas_call(
        without_deps,
        out_shape=outs + [struct((8, 128), f32)] * MARKS,
        grid_spec=pltpu.PrefetchScalarGridSpec(
            num_scalar_prefetch=1,
            grid=grid,
            in_specs=[any_place] * len(deps) + list(in_specs),
            out_specs=out_specs + [any_place] * MARKS,
            scratch_shapes=list(scratch),
        ),
        input_output_aliases={1 + len(deps) + k: v for k, v in (aliases or {}).items()},
        compiler_params=pltpu.CompilerParams(vmem_limit_bytes=vmem << 20),
        cost_estimate=pl.CostEstimate(flops=HEAVY, bytes_accessed=1, transcendentals=0),
    )(scalars, *deps, *ins)
    line.last = result[len(outs) :]
    return result[: len(outs)]


def struct(shape, dtype):
    return jax.ShapeDtypeStruct(shape, dtype)


def swap(value, axis, count, mask):
    return lax.ppermute(value, axis, [(i, i ^ mask) for i in range(count)])


def gather_pieces(value, axis, count, pin=lambda v: v):
    if count == 4 and isinstance(value, tuple):
        one, two = (tuple(swap(half, axis, count, mask) for half in value) for mask in (1, 2))
        one, two = pin((one, two))
        return [value, one, two, (swap(two[0], axis, count, 1), swap(one[1], axis, count, 2))]
    if isinstance(value, tuple):
        value = jnp.concatenate(value, axis=0)
    if count == 4:
        half = value.shape[0] // 2
        one, two = swap(value, axis, count, 1), swap(value, axis, count, 2)
        one, two = pin((one, two))
        return [value, one, two, (swap(two[:half], axis, count, 1), swap(one[half:], axis, count, 2))]
    pieces, mask = [value], 1
    while mask < count:
        pieces = pieces + [swap(piece, axis, count, mask) for piece in pieces]
        mask *= 2
    return pieces


def direct_pieces(value, axis, count):
    return [value] + [swap(value, axis, count, r) for r in range(1, count)]


def flat(pieces):
    return [part for piece in pieces for part in (piece if isinstance(piece, tuple) else (piece,))]


def piece_specs(pieces, block, width):
    specs = []
    for piece in pieces:
        if isinstance(piece, tuple):
            count = piece[0].shape[0] // block
            specs.append(pl.BlockSpec((block, width), lambda i, s, n=count: (jnp.minimum(i, n - 1), 0)))
            specs.append(pl.BlockSpec((block, width), lambda i, s, n=count: (jnp.maximum(i - n, 0), 0)))
        else:
            specs.append(pl.BlockSpec((block, width), lambda i, s: (i, 0)))
    return specs


def halved(pieces):
    return [isinstance(piece, tuple) for piece in pieces]


def read_pieces(refs, halves):
    refs, values = list(refs), []
    early = pl.program_id(0) < pl.num_programs(0) // 2
    for in_halves in halves:
        value = refs.pop(0)[...]
        values.append(jnp.where(early, value, refs.pop(0)[...]) if in_halves else value)
    return values


def trade(pieces, axis):
    return lax.all_to_all(pieces, axis, 0, 0, tiled=True)


def halves_kernel(scalars, keep, keep2, arrived, arrived2, keep_out, send_out):
    keep_out[...] = (keep[...].astype(f32) + arrived[...].astype(f32)).astype(bf16)
    send_out[...] = (keep2[...].astype(f32) + arrived2[...].astype(f32)).astype(bf16)


def add_halves(scalars, keep, arrived):
    keep, arrived = line.pin((keep, arrived))
    half = keep.shape[0] // 2
    low = lambda left, right: (left.astype(f32) + right.astype(f32)).astype(bf16)
    out = low(keep[:half], arrived[:half]), low(keep[half:], arrived[half:])
    line.last = [*line.last, out[1]]
    return out


def sum_kernel(scalars, left, right, out):
    out[...] = left[...] + right[...]


def add_to(scalars, left, right):
    whole = pl.BlockSpec(left.shape, lambda i, s: (0, 0))
    return call(sum_kernel, (1,), scalars, [left, right], [whole] * 2, [struct(left.shape, f32)], [whole])[0]


def two_terms(value, width):
    high = value.astype(bf16)
    low = (value - high.astype(f32)).astype(bf16)
    rest = jnp.zeros((value.shape[0], width - 2 * value.shape[1]), bf16)
    return jnp.concatenate([high, low, rest], axis=1)


def transpose_blocks(scalars, first, source, target, dp_count):
    width = source.shape[1] // dp_count
    for place in range(dp_count):
        cols = pl.ds(pl.multiple_of(scalars[first + place] * width, width), width)
        target[place * width : (place + 1) * width, :] = source[:, cols].T


def named_kernel(scalars, ids, *refs):
    *shares, out, shares_out = refs
    for r, share in enumerate(shares):
        shares_out[scalars[r]] = share[...]
    named = jnp.zeros(out.shape, jnp.bool_)
    lanes = lax.broadcasted_iota(jnp.int32, out.shape, 1)
    for choice in range(ids.shape[1]):
        named = named | (ids[:, choice : choice + 1] == lanes)
    out[...] = named.astype(f32)


def kept_kernel(capacity, scalars, named, out):
    tokens = named.shape[0]
    earlier = lax.broadcasted_iota(jnp.int32, (tokens, tokens), 0) > lax.broadcasted_iota(
        jnp.int32, (tokens, tokens), 1
    )
    rank = dot(jnp.where(earlier, 1.0, 0.0).astype(bf16), named[...].astype(bf16))
    out[...] = jnp.where(rank < capacity, named[...], 0.0)


def named_pairs(scalars, expert_ids, shares, experts):
    tokens, chosen = expert_ids.shape
    plain = lambda h, w: pl.BlockSpec((h, w), lambda i, s: (0, 0))
    rows, features = shares[0].shape
    whole = (len(shares), rows, features)
    return call(
        named_kernel,
        (1,),
        scalars,
        [expert_ids, *shares],
        [plain(tokens, chosen)] + [plain(rows, features)] * len(shares),
        [struct((tokens, experts), f32), struct(whole, shares[0].dtype)],
        [plain(tokens, experts), pl.BlockSpec(whole, lambda i, s: (0, 0, 0))],
    )


def kept_pairs(scalars, named, capacity):
    plain = pl.BlockSpec(named.shape, lambda i, s: (0, 0))
    out = [struct(named.shape, f32)]
    return call(functools.partial(kept_kernel, capacity), (1,), scalars, [named], [plain], out, [plain])[0]


def project_kernel(n_tp, halves, heads, scalars, *refs):
    n_in = len(halves) + sum(halves)
    pieces = read_pieces(refs[:n_in], halves)
    gain, wq, wk, wv, q_gain, k_gain, cosine, sine = refs[n_in : n_in + 8]
    x_out, normed_out, factor_out, q_raw, k_raw, q_rot, k_rot, v_out = refs[n_in + 8 :]
    width = pieces[0].shape[1]
    features = width * n_tp
    values = [piece.astype(f32) for piece in pieces]
    squares = sum(jnp.sum(value * value, axis=1, keepdims=True) for value in values)
    factor = lax.rsqrt(squares / features + EPS)
    factor_out[...] = factor
    for r in range(n_tp):
        cols = pl.ds(pl.multiple_of(scalars[r] * width, width), width)
        x_out[:, cols] = pieces[r]
        normed_out[:, cols] = (values[r] * factor * gain[:, cols]).astype(bf16)
    normed = normed_out[...]
    cos, sin = cosine[...], sine[...]
    hd = cos.shape[1]
    for weight, head_gain, raw, rotated in ((wq, q_gain, q_raw, q_rot), (wk, k_gain, k_raw, k_rot)):
        product = dot(normed, weight[...])
        raw[...] = product
        for h in range(heads):
            part = product[:, h * hd : (h + 1) * hd]
            scale = lax.rsqrt(jnp.mean(part * part, axis=1, keepdims=True) + EPS)
            part = part * scale * head_gain[h : h + 1, :]
            part = part * cos + pltpu.roll(part, hd // 2, 1) * sin
            rotated[:, h * hd : (h + 1) * hd] = part.astype(bf16)
    v_out[...] = dot(normed, wv[...]).astype(bf16)


def project(scalars, pieces, gain, wq, wk, wv, q_gain, k_gain, cosine, sine):
    n_tp = len(pieces)
    tokens, width = pieces[0].shape
    features = width * n_tp
    heads, hd = q_gain.shape
    local = heads * hd
    rows = lambda w: pl.BlockSpec((TB, w), lambda i, s: (i, 0))
    return call(
        functools.partial(project_kernel, n_tp, halved(pieces), heads),
        (tokens // TB,),
        scalars,
        [*flat(pieces), gain, wq, wk, wv, q_gain, k_gain, cosine, sine],
        piece_specs(pieces, TB, width) + [whole_spec()] * 6 + [rows(hd)] * 2,
        [
            struct((tokens, features), bf16),
            struct((tokens, features), bf16),
            struct((tokens, 1), f32),
            struct((tokens, local), f32),
            struct((tokens, local), f32),
            struct((tokens, local), bf16),
            struct((tokens, local), bf16),
            struct((tokens, local), bf16),
        ],
        [rows(features), rows(features), rows(1)] + [rows(local)] * 5,
    )


def attend_kernel(block, scalars, q_ref, k_ref, v_ref, top_ref, bottom_ref, total_ref):
    tokens, hd = q_ref.shape
    scale = 1.0 / math.sqrt(hd)
    for i in range(tokens // block):
        rows = slice(i * block, (i + 1) * block)
        reach = (i + 1) * block
        scores = dot(q_ref[rows, :], k_ref[:reach, :], NT) * scale
        at_row = i * block + lax.broadcasted_iota(jnp.int32, scores.shape, 0)
        at_col = lax.broadcasted_iota(jnp.int32, scores.shape, 1)
        scores = jnp.where(at_row >= at_col, scores, -1e30)
        top = jnp.max(scores, axis=1, keepdims=True)
        weights = jnp.exp(scores - top)
        total = jnp.sum(weights, axis=1, keepdims=True)
        probs = (weights * (1.0 / total)).astype(bf16)
        half = tokens // 2
        out_ref, first = (top_ref, 0) if reach <= half else (bottom_ref, half)
        out_ref[i * block - first : reach - first, :] = dot(probs, v_ref[:reach, :]).astype(bf16)
        total_ref[0, rows, :] = top + jnp.log(total)


def attend(scalars, q_rot, k_rot, value, heads):
    tokens, local = q_rot.shape
    hd = local // heads
    column = pl.BlockSpec((tokens, hd), lambda h, s: (0, h))
    return call(
        functools.partial(attend_kernel, min(256, tokens // 2)),
        (heads,),
        scalars,
        [q_rot, k_rot, value],
        [column] * 3,
        [struct((tokens // 2, local), bf16)] * 2 + [struct((heads, tokens, 1), f32)],
        [pl.BlockSpec((tokens // 2, hd), lambda h, s: (0, h))] * 2
        + [pl.BlockSpec((1, tokens, 1), lambda h, s: (h, 0, 0))],
    )


def attend_back_kernel(block, scalars, *refs):
    (q_ref, k_ref, v_ref, go_ref, total_ref, q_raw, k_raw, q_gain, k_gain, cosine, sine) = refs[:11]
    grads_out, dgain_out, dq_acc, dk_acc, dv_acc = refs[11:]
    tokens, hd = q_ref.shape
    scale = 1.0 / math.sqrt(hd)
    count = tokens // block
    for i in reversed(range(count)):
        rows = slice(i * block, (i + 1) * block)
        reach = (i + 1) * block
        query, grad = q_ref[rows, :], go_ref[rows, :]
        scores = dot(query, k_ref[:reach, :], NT) * scale
        at_row = i * block + lax.broadcasted_iota(jnp.int32, scores.shape, 0)
        at_col = lax.broadcasted_iota(jnp.int32, scores.shape, 1)
        scores = jnp.where(at_row >= at_col, scores, -1e30)
        probs = jnp.exp(scores - total_ref[0, rows, :])
        dprobs = dot(grad, v_ref[:reach, :], NT)
        delta = jnp.sum(dprobs * probs, axis=1, keepdims=True)
        dscores = (probs * (dprobs - delta)).astype(bf16)
        dq_acc[rows, :] = dot(dscores, k_ref[:reach, :]) * scale
        dk = dot(dscores, query, TN) * scale
        dv = dot(probs.astype(bf16), grad, TN)
        if i == count - 1:
            dk_acc[...] = dk
            dv_acc[...] = dv
        else:
            dk_acc[:reach, :] += dk
            dv_acc[:reach, :] += dv
    grads_out[2] = dv_acc[...].astype(bf16)
    cos, sin = cosine[...], sine[...]
    dgains = []
    for j, acc, raw_ref, gain_ref in ((0, dq_acc, q_raw, q_gain), (1, dk_acc, k_raw, k_gain)):
        grad = acc[...]
        grad = grad * cos - pltpu.roll(grad, hd // 2, 1) * sin
        raw = raw_ref[...]
        factor = lax.rsqrt(jnp.mean(raw * raw, axis=1, keepdims=True) + EPS)
        normal = raw * factor
        dgains.append(jnp.sum(grad * normal, axis=0, keepdims=True))
        scaled = grad * gain_ref[0]
        mean = jnp.mean(scaled * normal, axis=1, keepdims=True)
        grads_out[j] = (factor * (scaled - normal * mean)).astype(bf16)
    dgain_out[0] = jnp.concatenate(dgains, axis=0)


def attend_back(scalars, q_rot, k_rot, value, grad, totals, q_raw, k_raw, q_gain, k_gain, cosine, sine):
    tokens, local = q_rot.shape
    heads, hd = q_gain.shape
    column = pl.BlockSpec((tokens, hd), lambda h, s: (0, h))
    gain_spec = pl.BlockSpec((1, 1, hd), lambda h, s: (h, 0, 0))
    table = pl.BlockSpec((tokens, hd), lambda h, s: (0, 0))
    return call(
        functools.partial(attend_back_kernel, min(256, tokens)),
        (heads,),
        scalars,
        [q_rot, k_rot, value, grad, totals, q_raw, k_raw, q_gain[:, None, :], k_gain[:, None, :], cosine, sine],
        [column] * 4
        + [pl.BlockSpec((1, tokens, 1), lambda h, s: (h, 0, 0))]
        + [column] * 2
        + [gain_spec] * 2
        + [table] * 2,
        [struct((3, tokens, local), bf16), struct((heads, 2, hd), f32)],
        [
            pl.BlockSpec((3, tokens, hd), lambda h, s: (0, 0, h)),
            pl.BlockSpec((1, 2, hd), lambda h, s: (h, 0, 0)),
        ],
        [pltpu.VMEM((tokens, hd), f32)] * 3,
    )


def whole_first_kernel(n_in, each, base, scalars, *refs):
    pieces, (whole_out, turned_out) = refs[:n_in], refs[n_in:]
    width = pieces[0].shape[1]
    part = width // each
    for r in range(n_in):
        cols = pl.ds(pl.multiple_of(scalars[r] * width, width), width)
        whole_out[:, cols] = pieces[r][...]
        for q in range(each):
            rows = pl.ds(pl.multiple_of(scalars[base + r * each + q] * part, part), part)
            turned_out[rows, :] = pieces[r][:, q * part : (q + 1) * part].T


def whole_last_kernel(scalars, piece, old_whole, old_turned, whole_out, turned_out):
    whole_out[...] = piece[...]
    turned_out[...] = piece[...].T


def whole_first(scalars, pieces, n_tp, dp_count, base):
    tokens, width = pieces[0].shape
    features = width * n_tp
    return call(
        functools.partial(whole_first_kernel, len(pieces), dp_count // n_tp, base),
        (tokens // TB,),
        scalars,
        pieces,
        [pl.BlockSpec((TB, width), lambda i, s: (i, 0))] * len(pieces),
        [struct((tokens, features), bf16), struct((features, tokens), bf16)],
        [
            pl.BlockSpec((TB, features), lambda i, s: (i, 0)),
            pl.BlockSpec((features, TB), lambda i, s: (0, i)),
        ],
    )


def whole_last(scalars, piece, r, whole, turned, dp_count, n_tp, base):
    tokens, width = piece.shape
    each = dp_count // n_tp
    part = width // each
    place = lambda s, q: s[base + r * each + q]
    return call(
        whole_last_kernel,
        (tokens // TB, each),
        scalars,
        [piece, whole, turned],
        [pl.BlockSpec((TB, part), lambda i, q, s: (i, q))] + [pl.BlockSpec(memory_space=pl.ANY)] * 2,
        [struct(whole.shape, bf16), struct(turned.shape, bf16)],
        [
            pl.BlockSpec((TB, part), lambda i, q, s: (i, s[r] * each + q)),
            pl.BlockSpec((part, TB), lambda i, q, s: (place(s, q), i)),
        ],
        aliases={1: 0, 2: 1},
    )


def add_products(total, pieces, weights):
    for piece, weight in zip(pieces, weights):
        total += dot(piece, weight[...].reshape(piece.shape[1], weight.shape[-1]))
    return total


def stream_first_kernel(halves, scalars, x_ref, *refs):
    n_in = len(halves) + sum(halves)
    pieces, weights, out = read_pieces(refs[:n_in], halves), refs[n_in:-1], refs[-1]
    out[...] = add_products(x_ref[...].astype(f32), pieces, weights)


def weight_specs(w_all, places):
    n_dp, _, share, features = w_all.shape
    return [pl.BlockSpec((n_dp, 1, share, features), lambda i, s, r=r: (0, s[r], 0, 0)) for r in places]


def stream_first(scalars, pieces, x, w_all):
    tokens, features = x.shape
    rows = pl.BlockSpec((TB, features), lambda i, s: (i, 0))
    return call(
        functools.partial(stream_first_kernel, halved(pieces)),
        (tokens // TB,),
        scalars,
        [x, *flat(pieces)] + [w_all] * len(pieces),
        [rows] + piece_specs(pieces, TB, flat(pieces)[0].shape[1]) + weight_specs(w_all, range(len(pieces))),
        [struct((tokens, features), f32)],
        [rows],
    )[0]


def stream_kernel(n_tp, halves, dp_count, scalars, *refs):
    n_last, n_in = len(halves), len(halves) + sum(halves)
    pieces = read_pieces(refs[:n_in], halves)
    weights = refs[n_in : n_in + n_last]
    first, gain, router, kept = refs[n_in + n_last : n_in + n_last + 4]
    stream_out, normed_out, mine_out, packed_out, turned_out, factor_out, probs_out, gates_out = refs[
        n_in + n_last + 4 :
    ]
    total = add_products(first[...], pieces, weights)
    width = total.shape[1] // n_tp
    stream_out[...] = total
    factor = lax.rsqrt(jnp.mean(total * total, axis=1, keepdims=True) + EPS)
    factor_out[...] = factor
    normed = (total * factor * gain[...]).astype(bf16)
    normed_out[...] = normed
    mine_out[...] = normed_out[:, pl.ds(pl.multiple_of(scalars[0] * width, width), width)]
    logits = dot(normed, router[...])
    power = jnp.exp(logits - jnp.max(logits, axis=1, keepdims=True))
    probs = power / jnp.sum(power, axis=1, keepdims=True)
    probs_out[...] = probs
    gates = probs * kept[...]
    gates_out[...] = gates
    packed_out[...] = two_terms(gates, packed_out.shape[1])
    transpose_blocks(scalars, n_tp, normed_out, turned_out, dp_count)


def stream_of(scalars, pieces, first, w_all, gain, router, kept, n_tp, dp_count):
    tokens, features = first.shape
    experts = router.shape[1]
    width = features // n_tp
    rows = lambda w: pl.BlockSpec((TB, w), lambda i, s: (i, 0))
    places = range(n_tp - len(pieces), n_tp)
    return call(
        functools.partial(stream_kernel, n_tp, halved(pieces), dp_count),
        (tokens // TB,),
        scalars,
        [*flat(pieces)] + [w_all] * len(pieces) + [first, gain, router, kept],
        piece_specs(pieces, TB, flat(pieces)[0].shape[1])
        + weight_specs(w_all, places)
        + [rows(features), whole_spec(), whole_spec(), rows(experts)],
        [
            struct((tokens, features), f32),
            struct((tokens, features), bf16),
            struct((tokens, width), bf16),
            struct((tokens, 128), bf16),
            struct((features, tokens), bf16),
            struct((tokens, 1), f32),
            struct((tokens, experts), f32),
            struct((tokens, experts), f32),
        ],
        [
            rows(features),
            rows(features),
            rows(width),
            rows(128),
            pl.BlockSpec((features, TB), lambda i, s: (0, i)),
            rows(1),
            rows(experts),
            rows(experts),
        ],
    )


def expert_kernel(first, shift, scalars, n_ref, g_ref, gates_ref, wg, wu, wd, hidden_out, pair_out, dgate_out):
    step = pl.program_id(0)
    expert = first + step + (0 if shift is None else scalars[shift])
    width = wg.shape[-1]

    @pl.when(step == 0)
    def _():
        dgate_out[...] = jnp.zeros_like(dgate_out)

    gate_val, up_val = dot(n_ref[...], wg[0]), dot(n_ref[...], wu[0])
    back = dot(g_ref[...], wd[0], NT)
    gates, experts = gates_ref[...], dgate_out.shape[1]
    if gates_ref.dtype == bf16:
        gates = gates[:, :experts].astype(f32) + gates[:, experts : 2 * experts].astype(f32)
    here = lax.broadcasted_iota(jnp.int32, gates.shape, 1) == expert
    gate = jnp.sum(jnp.where(here, gates, 0.0), axis=1, keepdims=True)
    sigmoid = 1.0 / (1.0 + jnp.exp(-gate_val))
    swish = gate_val * sigmoid
    hidden = (swish * up_val).astype(bf16).astype(f32)
    hidden_out[0] = (hidden * gate).astype(bf16)
    dgate = jnp.sum(back * hidden, axis=1, keepdims=True)
    dgate_out[...] = jnp.where(here, dgate, dgate_out[...])
    dhidden = back * gate
    pair_out[0, :, :width] = (dhidden * up_val * sigmoid * (1.0 + gate_val * (1.0 - sigmoid))).astype(bf16)
    pair_out[0, :, width:] = (dhidden * swish).astype(bf16)


def run_experts(scalars, normed, grad, gates, wg, wu, wd, first, count, shift=None):
    tokens, features = normed.shape
    experts, _, width = wg.shape
    place = lambda i, s: first + i + (0 if shift is None else s[shift])
    weight = lambda shape: pl.BlockSpec((1, *shape), lambda i, s: (place(i, s), 0, 0))
    given = lambda shape: pl.BlockSpec((1, *shape), lambda i, s: (i, 0, 0))
    return call(
        functools.partial(expert_kernel, first, shift),
        (count,),
        scalars,
        [normed, grad, gates, wg, wu, wd],
        [whole_spec()] * 3 + [weight((features, width))] * 2 + [weight((width, features))],
        [
            struct((count, tokens, width), bf16),
            struct((count, tokens, 2 * width), bf16),
            struct((tokens, experts), f32),
        ],
        [
            given((tokens, width)),
            given((tokens, 2 * width)),
            pl.BlockSpec((tokens, experts), lambda i, s: (0, 0)),
        ],
    )


def weight_grads_kernel(scalars, turned, g_turned, hidden, pair, keep_out, send_out):
    half, _, rows, _ = keep_out.shape
    width = hidden.shape[-1]
    first = dot(turned[...], pair[0]).astype(bf16).reshape(2 * half, rows, 2 * width)
    keep_out[:, 0, :, : 2 * width] = first[:half]
    send_out[:, 0, :, : 2 * width] = first[half:]
    second = dot(g_turned[...], hidden[0]).astype(bf16).reshape(2 * half, rows, width)
    keep_out[:, 0, :, 2 * width :] = second[:half]
    send_out[:, 0, :, 2 * width :] = second[half:]


def weight_grads(scalars, turned, g_turned, hidden, pair, offset, count, dp_count):
    features, tokens = turned.shape
    width = hidden.shape[-1]
    half, rows = dp_count // 2, features // dp_count
    out = struct((half, count, rows, 3 * width), bf16)
    out_spec = pl.BlockSpec((half, 1, rows, 3 * width), lambda i, s: (0, i, 0, 0))
    return call(
        weight_grads_kernel,
        (count,),
        scalars,
        [turned, g_turned, hidden, pair],
        [
            whole_spec(),
            whole_spec(),
            pl.BlockSpec((1, tokens, width), lambda i, s: (offset + i, 0, 0)),
            pl.BlockSpec((1, tokens, 2 * width), lambda i, s: (offset + i, 0, 0)),
        ],
        [out, out],
        [out_spec, out_spec],
    )


def inner_swap(index):
    return (index & ~3) | ((index & 1) << 1) | ((index >> 1) & 1)


def shared_grads_kernel(scalars, *refs):
    turned, turned2, g_turned, g_turned2, hidden, hidden2, pair, pair2, keep_out, send_out = refs
    half, _, rows, _ = keep_out.shape
    width = hidden.shape[-1]
    first = dot(turned[...], pair[0]) + dot(turned2[...], pair2[0])
    first = first.astype(bf16).reshape(2 * half, rows, 2 * width)
    second = dot(g_turned[...], hidden[0]) + dot(g_turned2[...], hidden2[0])
    second = second.astype(bf16).reshape(2 * half, rows, width)
    for out, base in ((keep_out, 0), (send_out, half)):
        for place in range(half):
            out[inner_swap(place), 0, :, : 2 * width] = first[base + place]
            out[inner_swap(place), 0, :, 2 * width :] = second[base + place]


def shared_grads(scalars, turned, turned2, g_turned, g_turned2, hidden, hidden2, pair, pair2, shift, base, offset, count,
                 dp_count):
    features, tokens = turned.shape
    width = hidden2.shape[-1]
    half, rows = dp_count // 2, features // dp_count
    out = struct((half, count, rows, 3 * width), bf16)
    out_spec = pl.BlockSpec((half, 1, rows, 3 * width), lambda i, s: (0, i, 0, 0))
    mine = lambda w: pl.BlockSpec((1, tokens, w), lambda i, s: (base + s[shift] + offset + i, 0, 0))
    other = lambda w: pl.BlockSpec((1, tokens, w), lambda i, s: (offset + i, 0, 0))
    return call(
        shared_grads_kernel,
        (count,),
        scalars,
        [turned, turned2, g_turned, g_turned2, hidden, hidden2, pair, pair2],
        [whole_spec()] * 4 + [mine(width), other(width), mine(2 * width), other(2 * width)],
        [out, out],
        [out_spec, out_spec],
    )


def finish_kernel(n_parts, n_old, scalars, *refs):
    parts = refs[:n_parts]
    gate_out, up_out, down_out = refs[n_parts + n_old :]
    width = gate_out.shape[-1]
    total = sum(part[0].astype(f32) for part in parts)
    gate_out[0] = total[:, :width]
    up_out[0] = total[:, width : 2 * width]
    down_out[0] = total[:, 2 * width :].T


def finish(scalars, parts, old, first, shift, experts):
    count, rows, wide = parts[0].shape
    width = wide // 3
    place = lambda i, s: (first + i + (0 if shift is None else s[shift]), 0, 0)
    spec = pl.BlockSpec((1, rows, width), place)
    down_spec = pl.BlockSpec((1, width, rows), place)
    return call(
        functools.partial(finish_kernel, len(parts), len(old)),
        (count,),
        scalars,
        [*parts, *old],
        [pl.BlockSpec((1, rows, wide), lambda i, s: (i, 0, 0))] * len(parts)
        + [pl.BlockSpec(memory_space=pl.ANY)] * len(old),
        [struct((experts, rows, width), f32)] * 2 + [struct((experts, width, rows), f32)],
        [spec, spec, down_spec],
        aliases={len(parts) + k: k for k in range(len(old))},
    )


def chunk_specs(chunks, shape):
    specs, first = [], 0
    for chunk in chunks:
        count = chunk.shape[0]
        specs.append(
            pl.BlockSpec(
                (1, *shape), lambda i, s, first=first, count=count: (jnp.clip(i - first, 0, count - 1), 0, 0)
            )
        )
        first += count
    return specs


def input_grad_kernel(sizes, n_tp, scalars, *refs):
    n = len(sizes)
    pairs, (wg, wu), dgates = refs[:n], refs[n : n + 2], refs[n + 2 : 2 * n + 2]
    out, acc = refs[-2:]
    step = pl.program_id(0)
    width = wg.shape[-1]
    first = 0
    for pair, size in zip(pairs, sizes):

        def product(pair=pair):
            return dot(pair[0, :, :width], wg[0], NT) + dot(pair[0, :, width:], wu[0], NT)

        if first == 0:

            @pl.when(step == 0)
            def _(product=product):
                acc[...] = product()

        @pl.when((step >= max(first, 1)) & (step < first + size))
        def _(product=product):
            acc[...] += product()

        first += size

    @pl.when(step == pl.num_programs(0) - 1)
    def _():
        rows, features = acc.shape[0] // n_tp, acc.shape[1]
        for k in range(n_tp):
            place = slice(k * rows, (k + 1) * rows)
            out[k, :, :features] = acc[place, :].astype(bf16)
            dgate = sum(ref[place, :] for ref in dgates)
            out[k, :, features:] = two_terms(dgate, out.shape[2] - features)


def input_grads(scalars, pairs, wg, wu, dgates, n_tp):
    experts, features, width = wg.shape
    tokens = pairs[0].shape[1]
    rows = tokens // n_tp
    weight = pl.BlockSpec((1, features, width), lambda i, s: (i, 0, 0))
    return call(
        functools.partial(input_grad_kernel, [pair.shape[0] for pair in pairs], n_tp),
        (experts,),
        scalars,
        [*pairs, wg, wu, *dgates],
        chunk_specs(pairs, (tokens, 2 * width)) + [weight] * 2 + [whole_spec()] * len(dgates),
        [struct((n_tp, rows, features + 128), bf16)],
        [pl.BlockSpec((n_tp, rows, features + 128), lambda i, s: (0, 0, 0))],
        [pltpu.VMEM((tokens, features), f32)],
    )


def result_kernel(sizes, n_tp, scalars, *refs):
    hiddens, wd = refs[: len(sizes)], refs[len(sizes)]
    out, acc = refs[-2:]
    step = pl.program_id(0)
    first = 0
    for hidden, size in zip(hiddens, sizes):

        if first == 0:

            @pl.when(step == 0)
            def _(hidden=hidden):
                acc[...] = dot(hidden[0], wd[0])

        @pl.when((step >= max(first, 1)) & (step < first + size))
        def _(hidden=hidden):
            acc[...] += dot(hidden[0], wd[0])

        first += size

    @pl.when(step == pl.num_programs(0) - 1)
    def _():
        cols = acc.shape[1] // n_tp
        for k in range(n_tp):
            out[k] = acc[:, k * cols : (k + 1) * cols].astype(bf16)


def results(scalars, hiddens, wd, n_tp):
    experts, width, features = wd.shape
    tokens = hiddens[0].shape[1]
    cols = features // n_tp
    return call(
        functools.partial(result_kernel, [hidden.shape[0] for hidden in hiddens], n_tp),
        (experts,),
        scalars,
        [*hiddens, wd],
        chunk_specs(hiddens, (tokens, width)) + [pl.BlockSpec((1, width, features), lambda i, s: (i, 0, 0))],
        [struct((n_tp, tokens, cols), bf16)],
        [pl.BlockSpec((n_tp, tokens, cols), lambda i, s: (0, 0, 0))],
        [pltpu.VMEM((tokens, features), f32)],
    )


def rows_kernel(n_tp, scalars, *refs):
    parts, probs, kept, stream, normed, factor, upstream, gain, router = refs[:9]
    grad_out, dgain_out, drouter_out = refs[9:]
    features, experts = router.shape
    total = sum(parts[k, :, :features].astype(f32) for k in range(n_tp))
    both = sum(parts[k, :, features:].astype(f32) for k in range(n_tp))
    dprobs = (both[:, :experts] + both[:, experts : 2 * experts]) * kept[...]
    soft = probs[...]
    dlogits = soft * (dprobs - jnp.sum(dprobs * soft, axis=1, keepdims=True))
    dlogits = dlogits.astype(bf16)
    drouter_out[...] = dot(dlogits, normed[...], TN)
    total += dot(dlogits, router[...], NT)
    scale = factor[...]
    normal = stream[...] * scale
    dgain_out[...] = jnp.sum(total * normal, axis=0, keepdims=True)
    scaled = total * gain[...]
    mean = jnp.mean(scaled * normal, axis=1, keepdims=True)
    grad_out[...] = (upstream[...].astype(f32) + scale * (scaled - normal * mean)).astype(bf16)


def stream_grad_rows(scalars, parts, probs, kept, stream, normed, factor, upstream, gain, router):
    n_tp, rows, _ = parts.shape
    features, experts = router.shape
    mine = lambda w: pl.BlockSpec((rows, w), lambda i, s: (s[0], 0))
    plain = lambda h, w: pl.BlockSpec((h, w), lambda i, s: (0, 0))
    return call(
        functools.partial(rows_kernel, n_tp),
        (1,),
        scalars,
        [parts, probs, kept, stream, normed, factor, upstream, gain, router],
        [pl.BlockSpec(parts.shape, lambda i, s: (0, 0, 0))]
        + [mine(experts), mine(experts), mine(features), mine(features), mine(1), mine(features)]
        + [plain(1, features), plain(features, experts)],
        [struct((rows, features), bf16), struct((1, features), f32), struct((experts, features), f32)],
        [plain(rows, features), plain(1, features), plain(experts, features)],
    )


def attended_grad_kernel(scalars, grad, w_ref, out):
    out[...] = dot(grad[...], w_ref[...], NT).astype(bf16)


def attended_grad(scalars, grad, w_output):
    tokens, features = grad.shape
    local = w_output.shape[0]
    rows = lambda w: pl.BlockSpec((tokens // 2, w), lambda i, s: (i, 0))
    return call(
        attended_grad_kernel,
        (2,),
        scalars,
        [grad, w_output],
        [rows(features), whole_spec()],
        [struct((tokens, local), bf16)],
        [rows(local)],
    )[0]


def normed_grad_kernel(scalars, grads, wq, wk, wv, x_ref, factor, gain, out, dot_out, dgain_out):
    total = sum(dot(grads[j], weight[...], NT) for j, weight in enumerate((wq, wk, wv)))
    out[0] = total.astype(bf16)
    normal = x_ref[...].astype(f32) * factor[...]
    product = total * normal
    dgain_out[...] = jnp.sum(product, axis=0, keepdims=True)
    part = jnp.sum(product * gain[...], axis=1, keepdims=True)

    @pl.when(pl.program_id(0) == 0)
    def _():
        dot_out[...] = part

    @pl.when(pl.program_id(0) > 0)
    def _():
        dot_out[...] += part


def normed_grad(scalars, grads, wq, wk, wv, x, factor, gain, n_tp):
    _, tokens, local = grads.shape
    features = wq.shape[0]
    width = features // n_tp
    weight = pl.BlockSpec((width, local), lambda i, s: (i, 0))
    column = lambda h: pl.BlockSpec((h, width), lambda i, s: (0, i))
    whole = pl.BlockSpec((tokens, 1), lambda i, s: (0, 0))
    return call(
        normed_grad_kernel,
        (n_tp,),
        scalars,
        [grads, wq, wk, wv, x, factor, gain],
        [pl.BlockSpec(grads.shape, lambda i, s: (0, 0, 0))] + [weight] * 3 + [column(tokens), whole, column(1)],
        [struct((n_tp, tokens, width), bf16), struct((tokens, 1), f32), struct((1, features), f32)],
        [pl.BlockSpec((1, tokens, width), lambda i, s: (i, 0, 0)), whole, column(1)],
    )


def head_weight_grads(scalars, turned, grads, dp_count):
    features, tokens = turned.shape
    count, _, local = grads.shape
    half, rows = dp_count // 2, features // dp_count

    def kernel(scalars, turned, grad, keep_out, send_out):
        product = dot(turned[...], grad[0]).astype(bf16).reshape(2 * half, rows, local)
        keep_out[:, 0] = product[:half]
        send_out[:, 0] = product[half:]

    block = pl.BlockSpec((half, 1, rows, local), lambda i, s: (0, i, 0, 0))
    return call(
        kernel,
        (count,),
        scalars,
        [turned, grads],
        [whole_spec(), pl.BlockSpec((1, tokens, local), lambda i, s: (i, 0, 0))],
        [struct((half, count, rows, local), bf16)] * 2,
        [block] * 2,
    )


def output_weight_grads(scalars, top, bottom, grad, first, dp_count):
    half, local = top.shape
    width = grad.shape[1] // dp_count

    def kernel(scalars, top, bottom, keep, send, keep_out, send_out):
        for grad, out in ((keep, keep_out), (send, send_out)):
            product = dot(top[...], grad[:half, :], TN) + dot(bottom[...], grad[half:, :], TN)
            out[0, 0] = product.astype(bf16)

    column = lambda base: pl.BlockSpec((2 * half, width), lambda i, s: (0, s[base + i]))
    block = pl.BlockSpec((1, 1, local, width), lambda i, s: (i, 0, 0, 0))
    return call(
        kernel,
        (dp_count // 2,),
        scalars,
        [top, bottom, grad, grad],
        [whole_spec(), whole_spec(), column(first), column(first + dp_count // 2)],
        [struct((dp_count // 2, 1, local, width), bf16)] * 2,
        [block] * 2,
    )


def turn_kernel(first, dp_count, scalars, source, target):
    transpose_blocks(scalars, first, source, target, dp_count)


def turn(scalars, value, n_tp, dp_count):
    tokens, features = value.shape
    return call(
        functools.partial(turn_kernel, n_tp, dp_count),
        (tokens // TB,),
        scalars,
        [value],
        [pl.BlockSpec((TB, features), lambda i, s: (i, 0))],
        [struct((features, tokens), bf16)],
        [pl.BlockSpec((features, TB), lambda i, s: (0, i))],
    )[0]


def output_kernel(scalars, stream, parts, out):
    out[...] = (stream[...] + sum(parts[k].astype(f32) for k in range(parts.shape[0]))).astype(bf16)


def output_of(scalars, stream, parts):
    n_tp, tokens, width = parts.shape
    return call(
        output_kernel,
        (tokens // TB,),
        scalars,
        [stream, parts],
        [
            pl.BlockSpec((TB, width), lambda i, s: (i, s[0])),
            pl.BlockSpec((n_tp, TB, width), lambda i, s: (0, i, 0)),
        ],
        [struct((tokens, width), bf16)],
        [pl.BlockSpec((TB, width), lambda i, s: (i, 0))],
    )[0]


def final_kernel(features, scalars, dattn, x_ref, factor, row_dot, gain, parts, out):
    total = sum(parts[k].astype(f32) for k in range(parts.shape[0]))
    scale = factor[...]
    normal = x_ref[...].astype(f32) * scale
    back = scale * (total * gain[...] - normal * (row_dot[...] / features))
    out[...] = (dattn[...].astype(f32) + back).astype(bf16)


def final_grad(scalars, dattn, x, factor, row_dot, gain, parts):
    n_tp, tokens, width = parts.shape
    plain = lambda w: pl.BlockSpec((TB, w), lambda i, s: (i, 0))
    mine = pl.BlockSpec((TB, width), lambda i, s: (i, s[0]))
    return call(
        functools.partial(final_kernel, dattn.shape[1]),
        (tokens // TB,),
        scalars,
        [dattn, x, factor, row_dot, gain, parts],
        [mine, mine, plain(1), plain(1), pl.BlockSpec((1, width), lambda i, s: (0, s[0]))]
        + [pl.BlockSpec((n_tp, TB, width), lambda i, s: (0, i, 0))],
        [struct((tokens, width), bf16)],
        [plain(width)],
    )[0]


def final_sum_kernel(scalars, left, right, out):
    out[...] = left[...].astype(f32) + right[...].astype(f32)


def final_sum(scalars, left, right):
    count, rows, width = left.shape
    block = pl.BlockSpec((1, rows, width), lambda i, s: (i, 0, 0))
    return call(
        final_sum_kernel, (count,), scalars, [left, right], [block] * 2, [struct(left.shape, f32)], [block]
    )[0]


def body(n_dp, n_tp, cosine, sine, tokens, cotangent, attn_gain, w_query, w_key, w_value, query_gain, key_gain,
         w_output, ffn_gain, w_router, w_gate, w_up, w_down, expert_ids):
    tp, dp = lax.axis_index("tensor"), lax.axis_index("dp")
    far, near = n_dp // 2, n_dp // 4
    side = (dp // near) % 2
    token_count, width = tokens.shape
    features = width * n_tp
    heads, hd = query_gain.shape
    local = heads * hd
    experts = w_router.shape[1]
    capacity = token_count * expert_ids.shape[1] // experts
    gain1, gain2 = attn_gain[None, :], ffn_gain[None, :]
    blocks = (2, 3, 3)
    lead = sum(blocks)
    shared = (experts - lead) // 2
    shift, other_shift = n_tp + n_dp, n_tp + n_dp + 1
    each = n_dp // n_tp
    scalars = jnp.stack(
        [tp ^ r for r in range(n_tp)]
        + [dp ^ bit_reverse(place, n_dp) for place in range(n_dp)]
        + [side * shared, (1 - side) * shared]
        + [bit_reverse(((tp ^ r) * each + q) ^ dp, n_dp) for r in range(n_tp) for q in range(each)]
    ).astype(jnp.int32)
    turned_base = n_tp + n_dp + 2

    line.last = []

    share = local // n_dp
    w_share = lax.dynamic_slice_in_dim(w_output, dp * share, share, 0)
    w_shares = direct_pieces(w_share, "tensor", n_tp)

    named, w_some = named_pairs(scalars, expert_ids, w_shares, experts)
    w_all = lax.all_gather(w_some, "dp")
    x_pieces = gather_pieces(tokens, "tensor", n_tp, pin=line.pin)
    kept = kept_pairs(scalars, named, capacity)
    x_pieces, g_mine = lax.optimization_barrier((x_pieces, cotangent))
    early = n_tp - 1 if n_tp == 4 else n_tp // 2
    g_pieces = [g_mine] + [swap(g_mine, "tensor", n_tp, r) for r in range(1, early)]
    x, normed1, factor1, q_raw, k_raw, q_rot, k_rot, value = project(
        scalars, x_pieces, gain1, w_query, w_key, w_value, query_gain, key_gain, cosine, sine
    )
    *attended, totals = attend(scalars, q_rot, k_rot, value, heads)
    attended, g_pieces = lax.optimization_barrier((tuple(attended), g_pieces))
    upstream, g_turned = whole_first(scalars, g_pieces, n_tp, n_dp, turned_base)
    turned1 = turn(scalars, normed1, n_tp, n_dp)
    attended_pieces = gather_pieces(attended, "tensor", n_tp, pin=line.pin)
    stream = stream_first(scalars, attended_pieces[:early], x, w_all)
    g_mine = line.pin(g_mine)
    g_last = [swap(g_mine, "tensor", n_tp, r) for r in range(early, n_tp)]
    g_near = swap(g_mine, "dp", n_dp, near)
    stream, normed2, normed2_mine, packed, turned, factor2, probs, gates = stream_of(
        scalars, attended_pieces[early:], stream, w_all, gain2, w_router, kept, n_tp, n_dp
    )
    for r in range(early, n_tp):
        upstream, g_turned = whole_last(
            scalars, g_last[r - early], r, upstream, g_turned, n_dp, n_tp, turned_base
        )
    normed_near = swap(normed2_mine, "dp", n_dp, near)
    g_near, _ = lax.optimization_barrier((g_near, upstream))
    upstream_near = lax.all_gather(g_near, "tensor", axis=1, tiled=True)
    gates_near = swap(packed, "dp", n_dp, near)
    normed2_near = lax.all_gather(normed_near, "tensor", axis=1, tiled=True)

    hiddens, pairs, dgates = [], [], []

    def run(first, count):
        out = run_experts(scalars, normed2, upstream, gates, w_gate, w_up, w_down, first, count)
        for kind, array in zip((hiddens, pairs, dgates), out):
            kind.append(array)

    def sum_step(keep, send, mask):
        arrived = swap(send, "dp", n_dp, mask)
        return lambda: add_halves(scalars, keep, arrived)

    lower = [mask for mask in (2, 4, 8, 16) if mask < far]

    def own_sums(index):
        keep, send = weight_grads(scalars, turned, g_turned, hiddens[index], pairs[index], 0, blocks[index], n_dp)
        return sum_step(keep, send, 1)

    def next_step(take):
        return sum_step(*take(), lower[0])

    def last_step(take):
        keep, send = take()
        for mask in lower[1:]:
            keep, send = sum_step(keep, send, mask)()
        return [keep[0], swap(send, "dp", n_dp, far)[0]]

    def complete(parts, old, index):
        return finish(scalars, parts, old, sum(blocks[:index]), None, experts)

    run(0, blocks[0])
    take0 = own_sums(0)
    run(blocks[0], blocks[1])
    take0 = next_step(take0)
    take1 = own_sums(1)
    run(blocks[0] + blocks[1], blocks[2])
    parts0 = last_step(take0)
    take1 = next_step(take1)
    line.tick("dp", n_dp)
    run(sum(blocks[:3]), experts - sum(blocks[:3]))
    line.take()
    take2 = own_sums(2)
    g_turned_near = turn(scalars, upstream_near, n_tp, n_dp)
    old = complete(parts0, [], 0)
    take2 = next_step(take2)
    line.tick("dp", n_dp)
    parts1 = last_step(take1)
    line.take()
    input_parts = input_grads(scalars, pairs, w_gate, w_up, dgates, n_tp)[0]
    input_arrived = trade(input_parts, "tensor")
    line.tick("dp", n_dp)
    turned_near = turn(scalars, normed2_near, n_tp, n_dp)
    line.take()
    hidden_near, pair_near, _ = run_experts(
        scalars, normed2_near, upstream_near, gates_near, w_gate, w_up, w_down, lead, shared, shift
    )
    line.tick("dp", n_dp)
    parts2 = last_step(take2)
    line.take()

    def shared_sums(offset, count):
        keep, send = shared_grads(
            scalars, turned, turned_near, g_turned, g_turned_near, hiddens[3], hidden_near, pairs[3], pair_near,
            shift, 0, offset, count, n_dp,
        )
        return sum_step(keep, send, 1)

    def shared_next(take):
        keep, send = take()
        for mask in lower:
            if mask != near:
                keep, send = sum_step(keep, send, mask)()
        return sum_step(keep, send, far)

    some = (shared + 1) // 2
    take3 = shared_sums(0, some)
    dattn_rows, dgain2, drouter = stream_grad_rows(
        scalars, input_arrived, probs, kept, stream, normed2, factor2, upstream, gain2, w_router
    )
    dattn = lax.all_gather(dattn_rows, "tensor", axis=0, tiled=True)
    take3 = shared_next(take3)
    line.tick("dp", n_dp)
    old = complete(parts1, old, 1)
    line.take()
    take4 = shared_sums(some, shared - some)
    result_parts = results(scalars, hiddens, w_down, n_tp)[0]
    take4 = shared_next(take4)

    take5 = sum_step(*output_weight_grads(scalars, *attended, dattn, n_tp, n_dp), 1)
    line.tick("dp", n_dp)
    dattended = attended_grad(scalars, dattn, w_output)
    result_arrived = trade(line.pin(result_parts), "tensor")
    line.take()
    take5 = sum_step(*take5(), lower[0])
    grads, dhead_gains = attend_back(
        scalars, q_rot, k_rot, value, dattended, totals, q_raw, k_raw, query_gain, key_gain, cosine, sine
    )
    take6 = sum_step(*head_weight_grads(scalars, turned1, grads, n_dp), 1)
    line.tick("dp", n_dp)
    old = complete(parts2, old, 2)
    line.take()
    take6 = sum_step(*take6(), lower[0])
    slices, row_dot, dgain1 = normed_grad(scalars, grads, w_query, w_key, w_value, x, factor1, gain1, n_tp)
    slices_arrived = trade(slices, "tensor")

    own_heads = jnp.moveaxis(dhead_gains.reshape(heads, 2, n_dp, hd // n_dp), 2, 0).reshape(n_dp, -1)
    flat_heads = jnp.pad(own_heads, ((0, 0), (0, features // n_dp - own_heads.shape[1]))).reshape(1, -1)
    small = jnp.concatenate([drouter, dgain2, dgain1, flat_heads], axis=0)
    small = lax.psum_scatter(small, "dp", scatter_dimension=1, tiled=True)
    row_dot = row_dot.reshape(8, token_count // 8)

    def chain(value, axis, count):
        mask = 1
        while mask < count:
            arrived = swap(value, axis, count, mask)
            yield
            value = add_to(scalars, value, arrived)
            mask *= 2
        return value

    done = {}

    def advance(name, steps):
        if name not in done:
            try:
                next(steps)
            except StopIteration as end:
                done[name] = end.value

    def rest(take):
        keep, send = take()
        for mask in lower[1:]:
            keep, send = sum_step(keep, send, mask)()
        return keep, swap(send, "dp", n_dp, far)

    rows_chain = chain(row_dot, "tensor", n_tp)
    advance("rows", rows_chain)
    output = output_of(scalars, stream, result_arrived)
    advance("rows", rows_chain)
    keep3, send3 = take3()
    given3 = swap(send3, "dp", n_dp, near)
    keep4, send4 = take4()
    given4 = swap(send4, "dp", n_dp, near)
    old = finish(scalars, [keep3[0]], old, lead, shift, experts)
    keep5, arrived5 = rest(take5)
    keep6, arrived6 = rest(take6)
    line.tick("dp", n_dp)
    old = finish(scalars, [keep4[0]], old, lead + some, shift, experts)
    line.take()
    while "rows" not in done:
        advance("rows", rows_chain)
    row_dot = done["rows"].reshape(token_count, 1)
    head_gains = small[experts + 2, : own_heads.shape[1]].reshape(heads, 2, hd // n_dp)
    sums_chain = chain(small[: experts + 2], "tensor", n_tp)
    advance("sums", sums_chain)
    input_grad = final_grad(scalars, dattn, x, factor1, row_dot, gain1, slices_arrived)
    advance("sums", sums_chain)
    old = finish(scalars, [given3[0]], old, lead, other_shift, experts)
    while "sums" not in done:
        advance("sums", sums_chain)
    small = done["sums"]
    grad_output = final_sum(scalars, keep5[0], arrived5[0])[0]
    grad_gate, grad_up, grad_down = finish(scalars, [given4[0]], old, lead + some, other_shift, experts)
    grad_qkv = final_sum(scalars, keep6[0], arrived6[0])
    return (
        output,
        input_grad,
        small[experts + 1],
        grad_qkv[0],
        grad_qkv[1],
        grad_qkv[2],
        head_gains[:, 0],
        head_gains[:, 1],
        grad_output,
        small[experts],
        small[:experts].T,
        grad_gate,
        grad_up,
        grad_down,
    )


def solution(mesh):
    placed = (
        P("dp", "tensor"),
        P("dp", "tensor"),
        P(),
        P(None, "tensor"),
        P(None, "tensor"),
        P(None, "tensor"),
        P("tensor", None),
        P("tensor", None),
        P("tensor", None),
        P(),
        P(),
        P(None, None, "tensor"),
        P(None, None, "tensor"),
        P(None, "tensor", None),
        P("dp", None),
    )
    n_dp, n_tp = mesh.shape["dp"], mesh.shape["tensor"]

    def layer(*args):
        cosine, sine = rope_constants(LEN, args[6].shape[1])
        return body(n_dp, n_tp, jnp.asarray(cosine), jnp.asarray(sine), *args)

    return jax.shard_map(
        layer,
        mesh=mesh,
        in_specs=placed,
        out_specs=(
            P("dp", "tensor"),
            P("dp", "tensor"),
            P("dp"),
            P("dp", "tensor"),
            P("dp", "tensor"),
            P("dp", "tensor"),
            P("tensor", "dp"),
            P("tensor", "dp"),
            P("tensor", "dp"),
            P("dp"),
            P("dp", None),
            P(None, "dp", "tensor"),
            P(None, "dp", "tensor"),
            P(None, "tensor", "dp"),
        ),
        check_vma=False,
    )
```
